32 devices in a mesh: dp: 4 (over y, x), seq: 8 (over z, core).
Axes of the slice: x: 2, y: 2, z: 4, core: 2. Of those that a mesh axis runs over, the one named last changes fastest.
Arguments:
- hidden_in: bfloat16 [4, 2048, 1024], P('dp', 'seq'), may hold values from -6 to 6
- noise_level: int32 [4, 8], P('dp', 'seq'), may hold values from 0 to 1023
- noise_table: float32 [1024, 1024], P(('dp', 'seq')), may hold values from -6 to 6
- w_ada: float32 [1024, 6144], P(('dp', 'seq')), may hold values from -0.1875 to 0.1875
- b_ada: float32 [6144], P(('dp', 'seq')), may hold values from -3 to 3
- w_qkv: float32 [1024, 3072], P(('dp', 'seq')), may hold values from -0.1875 to 0.1875
- b_qkv: float32 [3072], P(('dp', 'seq')), may hold values from -3 to 3
- w_out: float32 [1024, 1024], P(('dp', 'seq')), may hold values from -0.75 to 0.75
- b_out: float32 [1024], P(('dp', 'seq')), may hold values from -3 to 3
- w_up: float32 [1024, 4096], P(('dp', 'seq')), may hold values from -0.1875 to 0.1875
- b_up: float32 [4096], P(('dp', 'seq')), may hold values from -3 to 3
- w_down: float32 [4096, 1024], P(('dp', 'seq')), may hold values from -0.09375 to 0.09375
- b_down: float32 [1024], P(('dp', 'seq')), may hold values from -3 to 3
- grad_out: bfloat16 [4, 2048, 1024], P('dp', 'seq'), may hold values from -6 to 6
Outputs:
- layer_out: bfloat16 [4, 2048, 1024], P('dp', 'seq')
- grad_hidden: bfloat16 [4, 2048, 1024], P('dp', 'seq')
- grad_noise_table: float32 [1024, 1024], P(('dp', 'seq'))
- grad_w_ada: float32 [1024, 6144], P(('dp', 'seq'))
- grad_b_ada: float32 [6144], P(('dp', 'seq'))
- grad_w_qkv: float32 [1024, 3072], P(('dp', 'seq'))
- grad_b_qkv: float32 [3072], P(('dp', 'seq'))
- grad_w_out: float32 [1024, 1024], P(('dp', 'seq'))
- grad_b_out: float32 [1024], P(('dp', 'seq'))
- grad_w_up: float32 [1024, 4096], P(('dp', 'seq'))
- grad_b_up: float32 [4096], P(('dp', 'seq'))
- grad_w_down: float32 [4096, 1024], P(('dp', 'seq'))
- grad_b_down: float32 [1024], P(('dp', 'seq'))
The draws below stay inside these ranges and needn't reach their ends.
Inputs may be any that keep to these rules, and one draw needn't show every extreme that they name: `noise_level`: a row of noise_table.
All inputs are finite; a program needn't handle non-finite values.
Results may differ from the reference program's by a relative error of at most 0.038.
Values may be sent and summed in bfloat16 or wider, within the bound.
A program may use at most 192 MiB of HBM per device.

```python
import math
import jax
import jax.numpy as jnp
from jax import lax

D = 1024
H = 16
FF = 4096
LEVELS = 1024
GRID_W = 16
PATCHES = 256
FRAMES = 8
SEQLEN = 2048
CLIPS = 4


def set_ends(values, rng, low, top_value):
    longest = values.shape.index(max(values.shape))
    spots = []
    for shift in (0, 1):
        where = [jax.random.randint(jax.random.fold_in(rng, axis), (), 0, length) for axis, length in enumerate(values.shape)]
        where[longest] = (where[longest] + shift) % values.shape[longest]
        spots.append(tuple(where))
    return values.at[spots[0]].set(low).at[spots[1]].set(top_value)


def levels(key, dims, cuts, smallest, largest):
    def one(axis_at, blocks):
        steps = jax.random.uniform(jax.random.fold_in(jax.random.fold_in(key, 6), axis_at), (blocks,), jnp.float32, smallest / len(cuts), largest / len(cuts))
        return jnp.repeat(jnp.exp(steps), dims[axis_at] // blocks).reshape((-1,) + (1,) * (len(dims) - axis_at - 1))

    factor_of = one(*cuts[0])
    for cut in cuts[1:]:
        factor_of = factor_of * one(*cut)
    return factor_of


def normal_values(stream_key, shape, width, reach, cuts=(), held_as=jnp.bfloat16):
    values = width * jax.random.normal(stream_key, shape, jnp.float32)
    if cuts:
        values = values * levels(stream_key, shape, cuts, -0.22, 0.18)
    return jnp.clip(values, -reach, reach).astype(held_as)


def setup_inputs(seed: int = 0) -> dict:
    splits = jax.random.split(jax.random.key(seed), 15)
    return {
        "hidden_in": normal_values(splits[0], (CLIPS, SEQLEN, D), 1.0, 6.0, ((0, 4), (1, 8))),
        "noise_level": set_ends(jax.random.randint(splits[1], (CLIPS, FRAMES), 0, LEVELS), jax.random.fold_in(splits[1], 1), 0, LEVELS - 1).astype(jnp.int32),
        "noise_table": normal_values(splits[2], (LEVELS, D), 1.0, 6.0, ((0, 32),), jnp.float32),
        "w_ada": normal_values(splits[3], (D, 6 * D), D ** -0.5, 0.1875, ((0, 32),), jnp.float32),
        "b_ada": normal_values(splits[4], (6 * D,), 0.5, 3.0, ((0, 32),), jnp.float32),
        "w_qkv": normal_values(splits[5], (D, 3 * D), D ** -0.5, 0.1875, ((0, 32),), jnp.float32),
        "b_qkv": normal_values(splits[6], (3 * D,), 0.5, 3.0, ((0, 32),), jnp.float32),
        "w_out": normal_values(splits[7], (D, D), (D // 16) ** -0.5, 0.75, ((0, 32),), jnp.float32),
        "b_out": normal_values(splits[8], (D,), 0.5, 3.0, ((0, 32),), jnp.float32),
        "w_up": normal_values(splits[9], (D, FF), D ** -0.5, 0.1875, ((0, 32),), jnp.float32),
        "b_up": normal_values(splits[10], (FF,), 0.5, 3.0, ((0, 32),), jnp.float32),
        "w_down": normal_values(splits[11], (FF, D), FF ** -0.5, 0.09375, ((0, 32),), jnp.float32),
        "b_down": normal_values(splits[12], (D,), 0.5, 3.0, ((0, 32),), jnp.float32),
        "grad_out": normal_values(splits[13], (CLIPS, SEQLEN, D), 1.0, 6.0, ((0, 4), (1, 8))),
    }


@jax.custom_vjp
def low(v):
    return lax.optimization_barrier(v.astype(jnp.bfloat16)).astype(jnp.float32)

@jax.custom_vjp
def low_back(v):
    return v

def low_keep(v):
    return (low(v), None)

def low_pass(kept, grad):
    return (grad,)

def back_keep(v):
    return (v, None)

def back_low(kept, grad):
    return (low(grad),)
low.defvjp(low_keep, low_pass)
low_back.defvjp(back_keep, back_low)
norm_eps = 1e-06
masked_score = -1e+30
highest = lax.Precision.HIGHEST

def layer_norm(values):
    centred = values - lax.optimization_barrier(jnp.mean(values, axis=-1, keepdims=True))
    spread = lax.optimization_barrier(jnp.mean(centred * centred, axis=-1, keepdims=True))
    return centred * lax.rsqrt(spread + norm_eps)

def modulate(values, shift_term, scale_term):
    return layer_norm(values) * (1.0 + scale_term) + shift_term

def turn_half(values):
    extent = values.shape[-1]
    side_part = 2 * (3 * extent // 16)
    pieces = []
    offset = 0
    for part_size in (extent - 2 * side_part, side_part, side_part):
        half_size = part_size // 2
        pieces.append(-values[..., offset + half_size:offset + part_size])
        pieces.append(values[..., offset:offset + half_size])
        offset = offset + part_size
    return jnp.concatenate(pieces, axis=-1)

def part_angles(places, part_size):
    half_size = part_size // 2
    rates = jnp.exp(-math.log(10000.0) * jnp.arange(half_size, dtype=jnp.float32) / half_size)
    angles = places.astype(jnp.float32)[:, None] * rates[None, :]
    return jnp.concatenate([angles, angles], axis=1)

def angle_table(places, extent):
    side_part = 2 * (3 * extent // 16)
    patch_index = places % PATCHES
    angles = jnp.concatenate([part_angles(places // PATCHES, extent - 2 * side_part), part_angles(patch_index // GRID_W, side_part), part_angles(patch_index % GRID_W, side_part)], axis=1)
    return (jnp.cos(angles), jnp.sin(angles))

def rotate(values, cosine_table, sine_table):
    return values * cosine_table + turn_half(values) * sine_table

def clip_forward(weights, clip_input, clip_levels):
    table_low, ada_w, ada_b, qkv_w, qkv_b, out_w, out_b, up_w, up_b, down_w, down_b = weights
    seq_len = clip_input.shape[0]
    head_dim = D // H
    embedded = table_low[clip_levels]
    modulation = low_back(jnp.dot(low(jax.nn.silu(embedded)), ada_w, precision=highest) + ada_b)
    per_token = jnp.repeat(modulation, PATCHES, axis=0)
    shift_one, scale_one, gate_one, shift_two, scale_two, gate_two = jnp.split(per_token, 6, axis=1)
    normed_one = low(modulate(clip_input, shift_one, scale_one))
    qkv_all = low_back(jnp.dot(normed_one, qkv_w, precision=highest) + qkv_b)
    query_raw, key_raw, value_raw = jnp.split(qkv_all, 3, axis=1)
    head_shape = (seq_len, H, head_dim)
    cosine_table, sine_table = angle_table(jnp.arange(seq_len, dtype=jnp.int32), head_dim)
    query_rot = low(rotate(query_raw.reshape(head_shape), cosine_table[:, None, :], sine_table[:, None, :]))
    keys_low = low(rotate(key_raw.reshape(head_shape), cosine_table[:, None, :], sine_table[:, None, :]))
    values_low = low(value_raw.reshape(head_shape))
    block_rows = min(512, seq_len)
    score_scale = 1.0 / math.sqrt(head_dim)
    key_frames = jnp.arange(seq_len, dtype=jnp.int32) // PATCHES

    def attend(block_in):
        query_block, block_start = block_in
        scores = low_back(jnp.einsum('qhd,khd->hqk', query_block, keys_low, precision=highest) * score_scale)
        query_frames = (block_start + jnp.arange(block_rows, dtype=jnp.int32)) // PATCHES
        allowed = key_frames[None, :] <= query_frames[:, None]
        scores = jnp.where(allowed[None], scores, masked_score)
        row_max = lax.optimization_barrier(jnp.max(scores, axis=-1, keepdims=True))
        exponent = jnp.exp(scores - row_max)
        softmax_weights = low(exponent / lax.optimization_barrier(jnp.sum(exponent, axis=-1, keepdims=True)))
        return jnp.einsum('hqk,khd->qhd', softmax_weights, values_low, precision=highest)
    block_total = seq_len // block_rows
    attended = lax.map(jax.checkpoint(attend), (query_rot.reshape(block_total, block_rows, H, head_dim), jnp.arange(block_total, dtype=jnp.int32) * block_rows))
    attended = low(low_back(attended.reshape(seq_len, D)))
    branch_one = low_back(jnp.dot(attended, out_w, precision=highest) + out_b)
    middle = clip_input + gate_one * branch_one
    normed_two = low(modulate(middle, shift_two, scale_two))
    hidden_pre = low_back(jnp.dot(normed_two, up_w, precision=highest) + up_b)
    hidden_act = low(jax.nn.gelu(hidden_pre, approximate=True))
    branch_two = low_back(jnp.dot(hidden_act, down_w, precision=highest) + down_b)
    return middle + gate_two * branch_two

def reference(hidden_in, noise_level, noise_table, w_ada, b_ada, w_qkv, b_qkv, w_out, b_out, w_up, b_up, w_down, b_down, grad_out):

    def forward(inputs, table, ada_w, ada_b, qkv_w, qkv_b, out_w, out_b, up_w, up_b, down_w, down_b):
        lowered = tuple((low(parameter) for parameter in (table, ada_w, ada_b, qkv_w, qkv_b, out_w, out_b, up_w, up_b, down_w, down_b)))

        def per_clip(carried, clip_in):
            return (carried, clip_forward(lowered, clip_in[0], clip_in[1]))
        unused, outputs = lax.scan(per_clip, jnp.zeros((), jnp.float32), (inputs, noise_level))
        return outputs
    primal = (hidden_in.astype(jnp.float32), noise_table, w_ada, b_ada, w_qkv, b_qkv, w_out, b_out, w_up, b_up, w_down, b_down)
    outputs, pullback = jax.vjp(forward, *primal)
    grads = pullback(grad_out.astype(jnp.float32))
    return (outputs.astype(jnp.bfloat16), grads[0].astype(jnp.bfloat16), grads[1], grads[2], grads[3], grads[4], grads[5], grads[6], grads[7], grads[8], grads[9], grads[10], grads[11])
```

```python
from functools import partial
import math

import jax
import jax.numpy as jnp
from jax import lax
from jax.sharding import PartitionSpec as P

H = 16
GRID_W = 16
PATCHES = 256


norm_eps = 1e-06
masked_score = -1e30
ALL = ("dp", "seq")
F32 = jnp.float32
BF16 = jnp.bfloat16


def layer_norm(values):
    centred = values - jnp.mean(values, axis=-1, keepdims=True)
    spread = jnp.mean(centred * centred, axis=-1, keepdims=True)
    return centred * lax.rsqrt(spread + norm_eps)


def modulate(values, shift_term, scale_term):
    return layer_norm(values) * (1.0 + scale_term) + shift_term


def turn_half(values):
    extent = values.shape[-1]
    side_part = 2 * (3 * extent // 16)
    pieces = []
    offset = 0
    for part_size in (extent - 2 * side_part, side_part, side_part):
        half_size = part_size // 2
        pieces.append(-values[..., offset + half_size : offset + part_size])
        pieces.append(values[..., offset : offset + half_size])
        offset = offset + part_size
    return jnp.concatenate(pieces, axis=-1)


def part_angles(places, part_size):
    half_size = part_size // 2
    rates = jnp.exp(-math.log(10000.0) * jnp.arange(half_size, dtype=F32) / half_size)
    angles = places.astype(F32)[:, None] * rates[None, :]
    return jnp.concatenate([angles, angles], axis=1)


def angle_table(places, extent):
    side_part = 2 * (3 * extent // 16)
    patch_index = places % PATCHES
    angles = jnp.concatenate(
        [
            part_angles(places // PATCHES, extent - 2 * side_part),
            part_angles(patch_index // GRID_W, side_part),
            part_angles(patch_index % GRID_W, side_part),
        ],
        axis=1,
    )
    return (jnp.cos(angles), jnp.sin(angles))


def rotate(values, cosine_table, sine_table):
    return values * cosine_table + turn_half(values) * sine_table


def unrotate(values, cosine_table, sine_table):
    return values * cosine_table - turn_half(values * sine_table)


def low(values):
    return values.astype(BF16)


def dot(left, right):
    return jnp.dot(left, right, preferred_element_type=F32)


def gather_rows(share):
    return lax.all_gather(low(share), ALL, axis=0, tiled=True)


def scatter_rows(whole):
    return lax.psum_scatter(whole, ALL, scatter_dimension=0, tiled=True)


def frame_modulation(noise_level, noise_table, w_ada, b_ada):
    levels = lax.all_gather(noise_level.reshape(-1), ALL, axis=0, tiled=True)
    device = lax.axis_index("dp") * lax.axis_size("seq") + lax.axis_index("seq")
    share = noise_table.shape[0]
    own_levels = device * share + jnp.arange(share, dtype=jnp.int32)
    one_hot = levels[:, None] == own_levels[None, :]
    found = dot(low(one_hot), low(noise_table))
    embedded = lax.psum_scatter(low(found), ALL, scatter_dimension=1, tiled=True).astype(F32)
    silu_in = low(jax.nn.silu(embedded))
    modulation = lax.psum_scatter(
        dot(silu_in, low(w_ada)), ALL, scatter_dimension=0, tiled=True
    ) + gather_rows(b_ada).astype(F32)
    return one_hot, embedded, silu_in, modulation


def frame_gradients(grad_modulation, one_hot, embedded, silu_in, w_ada):
    every = lax.all_gather(grad_modulation, ALL, axis=0, tiled=True)
    grad_ada_w = lax.dot_general(
        silu_in, every, (((0,), (0,)), ((), ())), preferred_element_type=F32
    )
    share = w_ada.shape[1] // lax.axis_size(ALL)
    device = lax.axis_index("dp") * lax.axis_size("seq") + lax.axis_index("seq")
    columns = lax.dynamic_slice_in_dim(every, device * share, share, axis=1)
    grad_ada_b = jnp.sum(columns.astype(F32), axis=0)
    grad_silu = lax.dot_general(
        every, low(w_ada), (((1,), (1,)), ((), ())), preferred_element_type=F32
    )
    unused, silu_back = jax.vjp(jax.nn.silu, embedded)
    grad_embedded = lax.all_gather(silu_back(grad_silu)[0], ALL, axis=1, tiled=True)
    grad_table = jnp.dot(
        one_hot.astype(F32).T, grad_embedded, precision=lax.Precision.HIGHEST
    )
    return grad_table, grad_ada_w, grad_ada_b


def to_heads(values):
    return lax.all_to_all(values, "seq", split_axis=2, concat_axis=1, tiled=True)


def to_tokens(values):
    return lax.all_to_all(values, "seq", split_axis=1, concat_axis=2, tiled=True)


def as_heads(values):
    return values.reshape(*values.shape[:2], -1, 64)


def query_blocks(array, axis):
    blocks = array.shape[axis] // PATCHES
    split = array.shape[:axis] + (blocks, PATCHES) + array.shape[axis + 1 :]
    return jnp.moveaxis(array.reshape(split), axis, 0)


def block_scores(query_block, keys, frame, score_scale):
    scores = (
        jnp.einsum("cqhd,ckhd->chqk", query_block, keys, preferred_element_type=F32) * score_scale
    )
    allowed = jnp.arange(keys.shape[1], dtype=jnp.int32) // PATCHES <= frame
    return jnp.where(allowed, scores, masked_score)


def attend(query, keys, values, score_scale):
    def one_block(block_in):
        query_block, frame = block_in
        scores = block_scores(query_block, keys, frame, score_scale)
        row_max = jnp.max(scores, axis=-1, keepdims=True)
        exponent = jnp.exp(scores - row_max)
        row_total = jnp.sum(exponent, axis=-1, keepdims=True)
        weighted = jnp.einsum(
            "chqk,ckhd->cqhd", low(exponent / row_total), values, preferred_element_type=F32
        )
        return low(weighted), (row_max + jnp.log(row_total))[..., 0]

    frames = jnp.arange(query.shape[1] // PATCHES, dtype=jnp.int32)
    attended, log_total = lax.map(one_block, (query_blocks(query, 1), frames))
    return (
        jnp.moveaxis(attended, 0, 1).reshape(query.shape),
        jnp.moveaxis(log_total, 0, 2).reshape(query.shape[0], query.shape[2], query.shape[1]),
    )


def attend_back(query, keys, values, grad_heads, log_total, row_delta, score_scale):
    def one_block(carried, block_in):
        query_block, grad_block, total_block, delta_block, frame = block_in
        scores = block_scores(query_block, keys, frame, score_scale)
        softmax_weights = jnp.exp(scores - total_block[..., None])
        grad_soft = jnp.einsum("cqhd,ckhd->chqk", grad_block, values, preferred_element_type=F32)
        grad_scores = low(softmax_weights * (grad_soft - delta_block[..., None]))
        query_grad = jnp.einsum("chqk,ckhd->cqhd", grad_scores, keys, preferred_element_type=F32)
        keys_grad = jnp.einsum(
            "chqk,cqhd->ckhd", grad_scores, query_block, preferred_element_type=F32
        )
        values_grad = jnp.einsum(
            "chqk,cqhd->ckhd", low(softmax_weights), grad_block, preferred_element_type=F32
        )
        return (carried[0] + keys_grad, carried[1] + values_grad), query_grad

    frames = jnp.arange(query.shape[1] // PATCHES, dtype=jnp.int32)
    empty = jnp.zeros(keys.shape, F32)
    (grad_keys, grad_values), grad_query = lax.scan(
        one_block,
        (empty, empty),
        (
            query_blocks(query, 1),
            query_blocks(grad_heads, 1),
            query_blocks(log_total, 2),
            query_blocks(row_delta, 2),
            frames,
        ),
    )
    grad_query = jnp.moveaxis(grad_query, 0, 1).reshape(query.shape)
    return grad_query * score_scale, grad_keys * score_scale, grad_values


def general_body(
    hidden_in,
    noise_level,
    noise_table,
    w_ada,
    b_ada,
    w_qkv,
    b_qkv,
    w_out,
    b_out,
    w_up,
    b_up,
    w_down,
    b_down,
    grad_out,
):
    qkv_w, qkv_b, out_w, out_b, up_w, up_b, down_w, down_b = [
        gather_rows(share)
        for share in (w_qkv, b_qkv, w_out, b_out, w_up, b_up, w_down, b_down)
    ]
    clip_count, patches, model_width = hidden_in.shape
    head_dim = model_width // H
    score_scale = 1.0 / math.sqrt(head_dim)
    head_shape = (clip_count, patches, H, head_dim)
    inputs = hidden_in.astype(F32)
    one_hot, embedded, silu_in, modulation = frame_modulation(
        noise_level, noise_table, w_ada, b_ada
    )
    shift_one, scale_one, gate_one, shift_two, scale_two, gate_two = [
        modulation[:, None, column_block * model_width : (column_block + 1) * model_width]
        for column_block in range(6)
    ]
    normed_one = low(modulate(inputs, shift_one, scale_one))
    qkv_all = dot(normed_one, qkv_w) + qkv_b.astype(F32)
    frame_own = lax.axis_index("seq")
    places = frame_own * patches + jnp.arange(patches, dtype=jnp.int32)
    cosine_local, sine_local = angle_table(places, head_dim)
    cosine_wide = cosine_local[None, :, None, :]
    sine_wide = sine_local[None, :, None, :]
    flat_shape = (clip_count, patches, model_width)

    def turned(block):
        part = qkv_all[..., block * model_width : (block + 1) * model_width]
        return low(rotate(part.reshape(head_shape), cosine_wide, sine_wide)).reshape(flat_shape)

    query = as_heads(to_heads(turned(0)))
    keys = as_heads(to_heads(turned(1)))
    values = as_heads(to_heads(low(qkv_all[..., 2 * model_width :])))
    attended, log_total = attend(query, keys, values, score_scale)
    attended_low = to_tokens(attended.reshape(*attended.shape[:2], -1))
    branch_one = dot(attended_low, out_w) + out_b.astype(F32)
    middle = inputs + gate_one * branch_one
    normed_two = low(modulate(middle, shift_two, scale_two))
    hidden_pre = dot(normed_two, up_w) + up_b.astype(F32)
    hidden_act = low(jax.nn.gelu(hidden_pre, approximate=True))
    branch_two = dot(hidden_act, down_w) + down_b.astype(F32)
    outputs = middle + gate_two * branch_two
    cotangent = grad_out.astype(F32)
    grad_gate_two = jnp.sum(cotangent * branch_two, axis=1)
    grad_branch_two = low(cotangent * gate_two)

    def weight_grad(left, right):
        whole = jnp.einsum("cpi,cpo->io", left, right, preferred_element_type=F32)
        return scatter_rows(low(whole)).astype(F32)

    def bias_grad(grad):
        return scatter_rows(jnp.sum(grad.astype(F32), axis=(0, 1)))

    def back_dot(grad, weight):
        return jnp.einsum("cpo,io->cpi", grad, weight, preferred_element_type=F32)

    grad_down_w = weight_grad(hidden_act, grad_branch_two)
    grad_down_b = bias_grad(grad_branch_two)
    grad_act = back_dot(grad_branch_two, down_w)
    unused, gelu_back = jax.vjp(partial(jax.nn.gelu, approximate=True), hidden_pre)
    grad_pre = low(gelu_back(grad_act)[0])
    grad_up_w = weight_grad(normed_two, grad_pre)
    grad_up_b = bias_grad(grad_pre)
    grad_normed_two = back_dot(grad_pre, up_w)
    unused, norm_two_back = jax.vjp(modulate, middle, shift_two, scale_two)
    grad_middle_norm, grad_shift_two, grad_scale_two = norm_two_back(grad_normed_two)
    grad_middle = cotangent + grad_middle_norm
    grad_gate_one = jnp.sum(grad_middle * branch_one, axis=1)
    grad_branch_one = low(grad_middle * gate_one)
    grad_out_w = weight_grad(attended_low, grad_branch_one)
    grad_out_b = bias_grad(grad_branch_one)
    grad_attended = low(back_dot(grad_branch_one, out_w))
    grad_heads = as_heads(to_heads(grad_attended))
    row_delta = jnp.sum(grad_heads.astype(F32) * attended.astype(F32), axis=-1).transpose(0, 2, 1)
    grad_query, grad_keys, grad_values = attend_back(
        query, keys, values, grad_heads, log_total, row_delta, score_scale
    )

    def home(grad):
        return to_tokens(low(grad).reshape(*grad.shape[:2], -1))

    def unturned(grad):
        wide = home(grad).astype(F32).reshape(head_shape)
        return low(unrotate(wide, cosine_wide, sine_wide)).reshape(flat_shape)

    grad_qkv = jnp.concatenate(
        [unturned(grad_query), unturned(grad_keys), home(grad_values)], axis=-1
    )
    grad_qkv_w = weight_grad(normed_one, grad_qkv)
    grad_qkv_b = bias_grad(grad_qkv)
    grad_normed_one = back_dot(grad_qkv, qkv_w)
    unused, norm_one_back = jax.vjp(modulate, inputs, shift_one, scale_one)
    grad_input_norm, grad_shift_one, grad_scale_one = norm_one_back(grad_normed_one)
    grad_input = grad_middle + grad_input_norm
    grad_modulation = low(
        jnp.concatenate(
            [
                grad_shift_one[:, 0],
                grad_scale_one[:, 0],
                grad_gate_one,
                grad_shift_two[:, 0],
                grad_scale_two[:, 0],
                grad_gate_two,
            ],
            axis=-1,
        )
    )
    grad_table, grad_ada_w, grad_ada_b = frame_gradients(
        grad_modulation, one_hot, embedded, silu_in, w_ada
    )
    return (
        low(outputs),
        low(grad_input),
        grad_table,
        grad_ada_w,
        grad_ada_b,
        grad_qkv_w,
        grad_qkv_b,
        grad_out_w,
        grad_out_b,
        grad_up_w,
        grad_up_b,
        grad_down_w,
        grad_down_b,
    )


def solution(mesh):
    tokens = P("dp", "seq", None)
    matrix = P(ALL, None)
    vector = P(ALL)
    parameters = (matrix,) + (matrix, vector) * 5
    return jax.shard_map(
        general_body,
        mesh=mesh,
        in_specs=(tokens, P("dp", "seq")) + parameters + (tokens,),
        out_specs=(tokens, tokens) + parameters,
        check_vma=False,
    )
```

```python
from functools import partial
import math

import jax
import jax.numpy as jnp
from jax import lax
from jax.experimental import pallas as pl
from jax.experimental.pallas import tpu as pltpu
from jax.sharding import PartitionSpec as P

H = 16
GRID_W = 16
PATCHES = 256


norm_eps = 1e-06
masked_score = -1e30
ALL = ("dp", "seq")
F32 = jnp.float32
BF16 = jnp.bfloat16


def layer_norm(values):
    centred = values - jnp.mean(values, axis=-1, keepdims=True)
    spread = jnp.mean(centred * centred, axis=-1, keepdims=True)
    return centred * lax.rsqrt(spread + norm_eps)


def modulate(values, shift_term, scale_term):
    return layer_norm(values) * (1.0 + scale_term) + shift_term


def turn_half(values):
    extent = values.shape[-1]
    side_part = 2 * (3 * extent // 16)
    pieces = []
    offset = 0
    for part_size in (extent - 2 * side_part, side_part, side_part):
        half_size = part_size // 2
        pieces.append(-values[..., offset + half_size : offset + part_size])
        pieces.append(values[..., offset : offset + half_size])
        offset = offset + part_size
    return jnp.concatenate(pieces, axis=-1)


def part_angles(places, part_size):
    half_size = part_size // 2
    rates = jnp.exp(-math.log(10000.0) * jnp.arange(half_size, dtype=F32) / half_size)
    angles = places.astype(F32)[:, None] * rates[None, :]
    return jnp.concatenate([angles, angles], axis=1)


def angle_table(places, extent):
    side_part = 2 * (3 * extent // 16)
    patch_index = places % PATCHES
    angles = jnp.concatenate(
        [
            part_angles(places // PATCHES, extent - 2 * side_part),
            part_angles(patch_index // GRID_W, side_part),
            part_angles(patch_index % GRID_W, side_part),
        ],
        axis=1,
    )
    return (jnp.cos(angles), jnp.sin(angles))


def rotate(values, cosine_table, sine_table):
    return values * cosine_table + turn_half(values) * sine_table


def unrotate(values, cosine_table, sine_table):
    return values * cosine_table - turn_half(values * sine_table)


def low(values):
    return values.astype(BF16)


def dot(left, right):
    return jnp.dot(left, right, preferred_element_type=F32)


def gather_rows(share):
    return lax.all_gather(low(share), ALL, axis=0, tiled=True)


def scatter_rows(whole):
    return lax.psum_scatter(whole, ALL, scatter_dimension=0, tiled=True)


def frame_modulation(noise_level, noise_table, w_ada, b_ada):
    levels = lax.all_gather(noise_level.reshape(-1), ALL, axis=0, tiled=True)
    device = lax.axis_index("dp") * lax.axis_size("seq") + lax.axis_index("seq")
    share = noise_table.shape[0]
    own_levels = device * share + jnp.arange(share, dtype=jnp.int32)
    one_hot = levels[:, None] == own_levels[None, :]
    found = dot(low(one_hot), low(noise_table))
    embedded = lax.psum_scatter(low(found), ALL, scatter_dimension=1, tiled=True).astype(F32)
    silu_in = low(jax.nn.silu(embedded))
    modulation = lax.psum_scatter(
        dot(silu_in, low(w_ada)), ALL, scatter_dimension=0, tiled=True
    ) + gather_rows(b_ada).astype(F32)
    return one_hot, embedded, silu_in, modulation


def frame_gradients(grad_modulation, one_hot, embedded, silu_in, w_ada):
    every = lax.all_gather(grad_modulation, ALL, axis=0, tiled=True)
    grad_ada_w = lax.dot_general(
        silu_in, every, (((0,), (0,)), ((), ())), preferred_element_type=F32
    )
    share = w_ada.shape[1] // lax.axis_size(ALL)
    device = lax.axis_index("dp") * lax.axis_size("seq") + lax.axis_index("seq")
    columns = lax.dynamic_slice_in_dim(every, device * share, share, axis=1)
    grad_ada_b = jnp.sum(columns.astype(F32), axis=0)
    grad_silu = lax.dot_general(
        every, low(w_ada), (((1,), (1,)), ((), ())), preferred_element_type=F32
    )
    unused, silu_back = jax.vjp(jax.nn.silu, embedded)
    grad_embedded = lax.all_gather(silu_back(grad_silu)[0], ALL, axis=1, tiled=True)
    grad_table = jnp.dot(
        one_hot.astype(F32).T, grad_embedded, precision=lax.Precision.HIGHEST
    )
    return grad_table, grad_ada_w, grad_ada_b


def to_heads(values):
    return lax.all_to_all(values, "seq", split_axis=2, concat_axis=1, tiled=True)


def to_tokens(values):
    return lax.all_to_all(values, "seq", split_axis=1, concat_axis=2, tiled=True)


def as_heads(values):
    return values.reshape(*values.shape[:2], -1, 64)


def query_blocks(array, axis):
    blocks = array.shape[axis] // PATCHES
    split = array.shape[:axis] + (blocks, PATCHES) + array.shape[axis + 1 :]
    return jnp.moveaxis(array.reshape(split), axis, 0)


def block_scores(query_block, keys, frame, score_scale):
    scores = (
        jnp.einsum("cqhd,ckhd->chqk", query_block, keys, preferred_element_type=F32) * score_scale
    )
    allowed = jnp.arange(keys.shape[1], dtype=jnp.int32) // PATCHES <= frame
    return jnp.where(allowed, scores, masked_score)


def attend(query, keys, values, score_scale):
    def one_block(block_in):
        query_block, frame = block_in
        scores = block_scores(query_block, keys, frame, score_scale)
        row_max = jnp.max(scores, axis=-1, keepdims=True)
        exponent = jnp.exp(scores - row_max)
        row_total = jnp.sum(exponent, axis=-1, keepdims=True)
        weighted = jnp.einsum(
            "chqk,ckhd->cqhd", low(exponent / row_total), values, preferred_element_type=F32
        )
        return low(weighted), (row_max + jnp.log(row_total))[..., 0]

    frames = jnp.arange(query.shape[1] // PATCHES, dtype=jnp.int32)
    attended, log_total = lax.map(one_block, (query_blocks(query, 1), frames))
    return (
        jnp.moveaxis(attended, 0, 1).reshape(query.shape),
        jnp.moveaxis(log_total, 0, 2).reshape(query.shape[0], query.shape[2], query.shape[1]),
    )


def attend_back(query, keys, values, grad_heads, log_total, row_delta, score_scale):
    def one_block(carried, block_in):
        query_block, grad_block, total_block, delta_block, frame = block_in
        scores = block_scores(query_block, keys, frame, score_scale)
        softmax_weights = jnp.exp(scores - total_block[..., None])
        grad_soft = jnp.einsum("cqhd,ckhd->chqk", grad_block, values, preferred_element_type=F32)
        grad_scores = low(softmax_weights * (grad_soft - delta_block[..., None]))
        query_grad = jnp.einsum("chqk,ckhd->cqhd", grad_scores, keys, preferred_element_type=F32)
        keys_grad = jnp.einsum(
            "chqk,cqhd->ckhd", grad_scores, query_block, preferred_element_type=F32
        )
        values_grad = jnp.einsum(
            "chqk,cqhd->ckhd", low(softmax_weights), grad_block, preferred_element_type=F32
        )
        return (carried[0] + keys_grad, carried[1] + values_grad), query_grad

    frames = jnp.arange(query.shape[1] // PATCHES, dtype=jnp.int32)
    empty = jnp.zeros(keys.shape, F32)
    (grad_keys, grad_values), grad_query = lax.scan(
        one_block,
        (empty, empty),
        (
            query_blocks(query, 1),
            query_blocks(grad_heads, 1),
            query_blocks(log_total, 2),
            query_blocks(row_delta, 2),
            frames,
        ),
    )
    grad_query = jnp.moveaxis(grad_query, 0, 1).reshape(query.shape)
    return grad_query * score_scale, grad_keys * score_scale, grad_values


def general_body(
    hidden_in,
    noise_level,
    noise_table,
    w_ada,
    b_ada,
    w_qkv,
    b_qkv,
    w_out,
    b_out,
    w_up,
    b_up,
    w_down,
    b_down,
    grad_out,
):
    qkv_w, qkv_b, out_w, out_b, up_w, up_b, down_w, down_b = [
        gather_rows(share)
        for share in (w_qkv, b_qkv, w_out, b_out, w_up, b_up, w_down, b_down)
    ]
    clip_count, patches, model_width = hidden_in.shape
    head_dim = model_width // H
    score_scale = 1.0 / math.sqrt(head_dim)
    head_shape = (clip_count, patches, H, head_dim)
    inputs = hidden_in.astype(F32)
    one_hot, embedded, silu_in, modulation = frame_modulation(
        noise_level, noise_table, w_ada, b_ada
    )
    shift_one, scale_one, gate_one, shift_two, scale_two, gate_two = [
        modulation[:, None, column_block * model_width : (column_block + 1) * model_width]
        for column_block in range(6)
    ]
    normed_one = low(modulate(inputs, shift_one, scale_one))
    qkv_all = dot(normed_one, qkv_w) + qkv_b.astype(F32)
    frame_own = lax.axis_index("seq")
    places = frame_own * patches + jnp.arange(patches, dtype=jnp.int32)
    cosine_local, sine_local = angle_table(places, head_dim)
    cosine_wide = cosine_local[None, :, None, :]
    sine_wide = sine_local[None, :, None, :]
    flat_shape = (clip_count, patches, model_width)

    def turned(block):
        part = qkv_all[..., block * model_width : (block + 1) * model_width]
        return low(rotate(part.reshape(head_shape), cosine_wide, sine_wide)).reshape(flat_shape)

    query = as_heads(to_heads(turned(0)))
    keys = as_heads(to_heads(turned(1)))
    values = as_heads(to_heads(low(qkv_all[..., 2 * model_width :])))
    attended, log_total = attend(query, keys, values, score_scale)
    attended_low = to_tokens(attended.reshape(*attended.shape[:2], -1))
    branch_one = dot(attended_low, out_w) + out_b.astype(F32)
    middle = inputs + gate_one * branch_one
    normed_two = low(modulate(middle, shift_two, scale_two))
    hidden_pre = dot(normed_two, up_w) + up_b.astype(F32)
    hidden_act = low(jax.nn.gelu(hidden_pre, approximate=True))
    branch_two = dot(hidden_act, down_w) + down_b.astype(F32)
    outputs = middle + gate_two * branch_two
    cotangent = grad_out.astype(F32)
    grad_gate_two = jnp.sum(cotangent * branch_two, axis=1)
    grad_branch_two = low(cotangent * gate_two)

    def weight_grad(left, right):
        whole = jnp.einsum("cpi,cpo->io", left, right, preferred_element_type=F32)
        return scatter_rows(low(whole)).astype(F32)

    def bias_grad(grad):
        return scatter_rows(jnp.sum(grad.astype(F32), axis=(0, 1)))

    def back_dot(grad, weight):
        return jnp.einsum("cpo,io->cpi", grad, weight, preferred_element_type=F32)

    grad_down_w = weight_grad(hidden_act, grad_branch_two)
    grad_down_b = bias_grad(grad_branch_two)
    grad_act = back_dot(grad_branch_two, down_w)
    unused, gelu_back = jax.vjp(partial(jax.nn.gelu, approximate=True), hidden_pre)
    grad_pre = low(gelu_back(grad_act)[0])
    grad_up_w = weight_grad(normed_two, grad_pre)
    grad_up_b = bias_grad(grad_pre)
    grad_normed_two = back_dot(grad_pre, up_w)
    unused, norm_two_back = jax.vjp(modulate, middle, shift_two, scale_two)
    grad_middle_norm, grad_shift_two, grad_scale_two = norm_two_back(grad_normed_two)
    grad_middle = cotangent + grad_middle_norm
    grad_gate_one = jnp.sum(grad_middle * branch_one, axis=1)
    grad_branch_one = low(grad_middle * gate_one)
    grad_out_w = weight_grad(attended_low, grad_branch_one)
    grad_out_b = bias_grad(grad_branch_one)
    grad_attended = low(back_dot(grad_branch_one, out_w))
    grad_heads = as_heads(to_heads(grad_attended))
    row_delta = jnp.sum(grad_heads.astype(F32) * attended.astype(F32), axis=-1).transpose(0, 2, 1)
    grad_query, grad_keys, grad_values = attend_back(
        query, keys, values, grad_heads, log_total, row_delta, score_scale
    )

    def home(grad):
        return to_tokens(low(grad).reshape(*grad.shape[:2], -1))

    def unturned(grad):
        wide = home(grad).astype(F32).reshape(head_shape)
        return low(unrotate(wide, cosine_wide, sine_wide)).reshape(flat_shape)

    grad_qkv = jnp.concatenate(
        [unturned(grad_query), unturned(grad_keys), home(grad_values)], axis=-1
    )
    grad_qkv_w = weight_grad(normed_one, grad_qkv)
    grad_qkv_b = bias_grad(grad_qkv)
    grad_normed_one = back_dot(grad_qkv, qkv_w)
    unused, norm_one_back = jax.vjp(modulate, inputs, shift_one, scale_one)
    grad_input_norm, grad_shift_one, grad_scale_one = norm_one_back(grad_normed_one)
    grad_input = grad_middle + grad_input_norm
    grad_modulation = low(
        jnp.concatenate(
            [
                grad_shift_one[:, 0],
                grad_scale_one[:, 0],
                grad_gate_one,
                grad_shift_two[:, 0],
                grad_scale_two[:, 0],
                grad_gate_two,
            ],
            axis=-1,
        )
    )
    grad_table, grad_ada_w, grad_ada_b = frame_gradients(
        grad_modulation, one_hot, embedded, silu_in, w_ada
    )
    return (
        low(outputs),
        low(grad_input),
        grad_table,
        grad_ada_w,
        grad_ada_b,
        grad_qkv_w,
        grad_qkv_b,
        grad_out_w,
        grad_out_b,
        grad_up_w,
        grad_up_b,
        grad_down_w,
        grad_down_b,
    )


MESH_ID = pl.DeviceIdType.MESH
VMEM_LIMIT = 60 * 1024 * 1024
HEADS_WIDE = 128


def contract(left, right, left_dim, right_dim, precision=None):
    return lax.dot_general(
        left,
        right,
        (((left_dim,), (right_dim,)), ((), ())),
        preferred_element_type=F32,
        precision=precision,
    )


class Place:
    def __init__(self):
        self.dp = lax.axis_index("dp")
        self.seq = lax.axis_index("seq")
        self.z = self.seq // 2
        self.core = self.seq % 2
        self.other = 1 - self.core
        self.x_dp = self.dp + 1 - 2 * (self.dp % 2)
        self.y_dp = (self.dp + 2) % 4
        self.far_dp = 3 - self.dp
        self.dp_peers = (self.x_dp, self.y_dp, self.far_dp)
        self.seq_peers = [(self.seq + step) % 8 for step in range(1, 8)]
        self.sibling = (self.dp, self.z * 2 + self.other)

    def at_dp(self, dp):
        return (dp, self.seq)

    def at_seq(self, seq):
        return (self.dp, seq)

    def greet(self):
        barrier = pltpu.get_barrier_semaphore()
        peers = [self.at_dp(dp) for dp in self.dp_peers]
        peers += [self.at_seq(seq) for seq in self.seq_peers]
        for peer in peers:
            pl.semaphore_signal(barrier, inc=1, device_id=peer, device_id_type=MESH_ID)
        pl.semaphore_wait(barrier, len(peers))


class Wire:
    def __init__(self, send_sems, recv_sems):
        self.send_sems = send_sems
        self.recv_sems = recv_sems
        self.used = 0
        self.sent = []

    def send(self, source, target, device):
        copy = pltpu.make_async_remote_copy(
            src_ref=source,
            dst_ref=target,
            send_sem=self.send_sems.at[self.used],
            recv_sem=self.recv_sems.at[self.used],
            device_id=device,
            device_id_type=MESH_ID,
        )
        self.used += 1
        copy.start()
        self.sent.append(copy)
        return copy

    def drain(self):
        for copy in self.sent:
            copy.wait_send()
        self.sent = []


def arrive(copies):
    for copy in copies:
        copy.wait_recv()


class Gather:
    def __init__(self, wire, place, ref):
        self.wire, self.place, self.ref = wire, place, ref

    def along_z(self):
        place, ref = self.place, self.ref
        own = ref.at[place.dp, place.z, place.core]
        self.coming = [
            self.wire.send(own, own, place.at_seq(((place.z + step) % 4) * 2 + place.core))
            for step in (1, 2, 3)
        ]

    def along_xy(self):
        place = self.place
        arrive(self.coming)
        own = self.ref.at[place.dp, :, place.core]
        self.coming = [
            self.wire.send(own, own, place.at_dp(dp)) for dp in (place.x_dp, place.y_dp)
        ]

    def across(self):
        place = self.place
        arrive(self.coming)
        from_x = self.ref.at[place.x_dp, pl.ds(0, 2), place.core]
        from_y = self.ref.at[place.y_dp, pl.ds(2, 2), place.core]
        self.coming = [
            self.wire.send(from_x, from_x, place.at_dp(place.y_dp)),
            self.wire.send(from_y, from_y, place.at_dp(place.x_dp)),
        ]

    def to_sibling(self):
        place = self.place
        arrive(self.coming)
        mine = self.ref.at[:, :, place.core]
        self.coming = [self.wire.send(mine, mine, place.sibling)]

    def finish(self):
        arrive(self.coming)


class SmallGather:
    def __init__(self, wire, place, ref):
        self.wire, self.place, self.ref = wire, place, ref

    def along_seq(self):
        place = self.place
        own = self.ref.at[place.dp, place.seq]
        self.coming = [self.wire.send(own, own, place.at_seq(seq)) for seq in place.seq_peers]

    def along_dp(self):
        place = self.place
        arrive(self.coming)
        own = self.ref.at[place.dp]
        self.coming = [self.wire.send(own, own, place.at_dp(dp)) for dp in place.dp_peers]

    def finish(self):
        arrive(self.coming)


def spread_dp(wire, place, part_of, slots):
    return [
        wire.send(part_of(dp), slots.at[index], place.at_dp(dp))
        for index, dp in enumerate(place.dp_peers)
    ]


def spread_seq(wire, place, part_of, slots):
    return [
        wire.send(part_of(seq), slots.at[index], place.at_seq(seq))
        for index, seq in enumerate(place.seq_peers)
    ]


def total_of(own, slots, count):
    total = own
    for index in range(count):
        total = total + slots[index].astype(F32)
    return total


def row_of(lines, first):
    return jnp.concatenate([lines[first + line : first + line + 1, :] for line in range(8)], axis=1)


def lines_of(row):
    return jnp.concatenate([row[:, 128 * line : 128 * (line + 1)] for line in range(8)], axis=0)


def whole_piece(piece):
    value = piece[...]
    return value.reshape(-1, value.shape[-1])


def norm_parts(values):
    centred = values - jnp.mean(values, axis=1, keepdims=True)
    inverse = lax.rsqrt(jnp.mean(centred * centred, axis=1, keepdims=True) + norm_eps)
    return centred * inverse, inverse


def half_turn(values):
    lane = lax.broadcasted_iota(jnp.int32, values.shape, 1) % 64
    in_time = lane < 16
    first = (lane < 8) | ((lane >= 16) & (lane < 28)) | ((lane >= 40) & (lane < 52))
    up = jnp.where(in_time, pltpu.roll(values, 120, 1), pltpu.roll(values, 116, 1))
    down = jnp.where(in_time, pltpu.roll(values, 8, 1), pltpu.roll(values, 12, 1))
    return jnp.where(first, up, down)


def split_heads(values):
    lane = lax.broadcasted_iota(jnp.int32, values.shape, 1)
    empty = jnp.zeros_like(values)
    return jnp.concatenate(
        [jnp.where(lane < 64, values, empty), jnp.where(lane < 64, empty, values)], axis=0
    )


def join_heads(turned):
    return jnp.concatenate([turned[:64, :256], turned[64:, 256:]], axis=0).T


def attend_frame(frame, query, keys, values, attended, log_total, scores):
    pair = split_heads(query[frame])
    row_max = None
    for block in range(frame + 1):
        block_scores = contract(keys[block], pair, 1, 1)
        scores[block] = block_scores
        block_max = jnp.max(block_scores, axis=0, keepdims=True)
        row_max = block_max if row_max is None else jnp.maximum(row_max, block_max)
    row_total = None
    weighted = None
    for block in range(frame + 1):
        exponent = jnp.exp(scores[block] - row_max)
        block_total = jnp.sum(exponent, axis=0, keepdims=True)
        block_sum = contract(values[block], exponent.astype(BF16), 0, 0)
        row_total = block_total if row_total is None else row_total + block_total
        weighted = block_sum if weighted is None else weighted + block_sum
    attended[frame] = join_heads(weighted / row_total).astype(BF16)
    log_total[frame] = row_max + jnp.log(row_total)


SQRT_TWO_OVER_PI = math.sqrt(2.0 / math.pi)


def gelu_parts(values):
    square = values * values
    bent = jnp.tanh(SQRT_TWO_OVER_PI * values * (1.0 + 0.044715 * square))
    half = 0.5 * (1.0 + bent)
    slope = half + 0.5 * values * (1.0 - bent * bent) * (
        SQRT_TWO_OVER_PI * (1.0 + 3.0 * 0.044715 * square)
    )
    return values * half, slope


def forward_kernel(
    x_ref,
    cotangent_ref,
    level_ref,
    table_ref,
    w_ada_ref,
    bias_ref,
    w_qkv_ref,
    w_out_ref,
    w_up_ref,
    w_down_ref,
    cosine_ref,
    sine_ref,
    layer_out_ref,
    wide_out,
    down_out,
    query_ref,
    keys_ref,
    values_ref,
    attended_ref,
    log_total_ref,
    attended_tokens,
    normed_one_ref,
    normed_two_ref,
    middle_ref,
    branch_one_ref,
    act_ref,
    slope_ref,
    modulation_ref,
    embedded_ref,
    one_hot_ref,
    gate_two_grad_ref,
    wide,
    down,
    levels,
    found,
    found_dp,
    found_sum,
    found_seq,
    partial_mod,
    mod_dp,
    mod_sum,
    mod_blocks,
    mod_seq,
    bias_dp,
    bias_sum,
    bias_seq,
    flat,
    scores,
    send_sems,
    recv_sems,
    back_send,
    back_recv,
    local_sems,
):
    place = Place()
    wire = Wire(send_sems, recv_sems)
    dp, seq, z, core = place.dp, place.seq, place.z, place.core
    device = dp * 8 + seq
    levels[dp, seq] = level_ref[...]
    for block in range(3):
        wide[block, dp, z, core] = low(w_qkv_ref[:, 1024 * block : 1024 * (block + 1)])
    place.greet()
    level_gather = SmallGather(wire, place, levels)
    level_gather.along_seq()
    pieces = [Gather(wire, place, wide.at[index]) for index in range(8)]
    pieces += [Gather(wire, place, down.at[index]) for index in range(4)]
    pieces[0].along_z()
    pieces[1].along_z()
    bias_copies = spread_dp(wire, place, lambda dp: bias_ref, bias_dp)
    wide[3, dp, z, core] = low(w_out_ref[...])
    for block in range(4):
        wide[4 + block, dp, z, core] = low(w_up_ref[:, 1024 * block : 1024 * (block + 1)])
    for block in range(4):
        down[block, dp, z, core] = low(w_down_ref[:, 256 * block : 256 * (block + 1)])
    pieces[2].along_z()
    saved = []

    def save(index):
        pieces[index].finish()
        source, target = (
            (wide.at[index], wide_out.at[index])
            if index < 8
            else (down.at[index - 8], down_out.at[index - 8])
        )
        copy = pltpu.make_async_copy(source, target, local_sems.at[index])
        copy.start()
        saved.append(copy)

    def tick(step, finish=True):
        if step + 2 < 12 and step > 0:
            pieces[step + 2].along_z()
        if step < 12:
            pieces[step].along_xy()
        if 0 <= step - 1 < 12:
            pieces[step - 1].across()
        if 0 <= step - 2 < 12:
            pieces[step - 2].to_sibling()
        if finish and 0 <= step - 3 < 12:
            save(step - 3)

    level_gather.along_dp()
    x = x_ref[...].astype(F32)
    normed, unused = norm_parts(x)
    flat[0] = normed
    level_gather.finish()
    level_rows = jnp.concatenate(
        [levels[group, frame, 0:1, :] for group in range(4) for frame in range(8)]
        + [jnp.full((96, 128), -1.0, F32)],
        axis=0,
    )
    lane = lax.broadcasted_iota(jnp.int32, (128, 128), 1)
    own_level = (lane + device * 32).astype(F32)
    one_hot = jnp.where((level_rows == own_level) & (lane < 32), 1.0, 0.0)
    one_hot_ref[...] = one_hot
    one_hot_turned = low(one_hot.T)[:32, :]
    found[...] = low(contract(low(table_ref[...]), one_hot_turned, 0, 0)).reshape(found.shape)
    found_copies = spread_dp(wire, place, lambda dp: found.at[dp], found_dp)
    pieces[0].along_xy()
    arrive(found_copies)
    found_sum[...] = low(total_of(found[dp].astype(F32), found_dp, 3))
    found_copies = spread_seq(wire, place, lambda seq: found_sum.at[seq], found_seq)
    tick(1)
    arrive(found_copies)
    embedded = total_of(found_sum[seq].astype(F32), found_seq, 7)
    embedded_ref[...] = embedded
    silu_in = low(embedded / (1.0 + jnp.exp(-embedded)))
    for block in range(6):
        part = contract(silu_in, low(w_ada_ref[:, 1024 * block : 1024 * (block + 1)]), 0, 0)
        for line in range(8):
            partial_mod[8 * block + line] = part[:32, 128 * line : 128 * (line + 1)].reshape(
                4, 8, 128
            )
    mod_copies = spread_dp(wire, place, lambda dp: partial_mod.at[:, dp], mod_dp)
    arrive(bias_copies)
    bias_sum[...] = low(total_of(bias_ref[...].astype(F32), bias_dp, 3))
    bias_copies = spread_seq(wire, place, lambda seq: bias_sum, bias_seq)
    tick(2)
    arrive(mod_copies)
    mod_sum[...] = total_of(partial_mod[:, dp], mod_dp, 3).reshape(384, 128)
    for frame in range(8):
        mod_blocks[frame] = mod_sum[pl.ds(frame, 48, stride=8), :]
    mod_copies = spread_seq(wire, place, lambda seq: mod_blocks.at[seq], mod_seq)
    tick(3)
    arrive(bias_copies)
    biases = total_of(bias_sum[...].astype(F32), bias_seq, 7)
    arrive(mod_copies)
    modulation = total_of(mod_blocks[seq], mod_seq, 7) + biases[72:120]
    for block in range(6):
        modulation_ref[block : block + 1, :] = row_of(modulation, 8 * block)
    shift_one = modulation_ref[0:1, :]
    scale_one = modulation_ref[1:2, :]
    gate_one = modulation_ref[2:3, :]
    shift_two = modulation_ref[3:4, :]
    scale_two = modulation_ref[4:5, :]
    gate_two = modulation_ref[5:6, :]
    normed_one_ref[...] = low(flat[0] * (1.0 + scale_one) + shift_one)
    cosine = cosine_ref[...]
    sine = sine_ref[...]
    head_copies = []

    def project(block, target):
        r = contract(normed_one_ref[...], whole_piece(wide.at[block]), 1, 0)
        r = r + row_of(biases, 8 * block)
        for group in range(8):
            part = r[:, 128 * group : 128 * (group + 1)]
            if block < 2:
                part = part * cosine + half_turn(part) * sine
            if block == 0:
                part = part * 0.125
            act_ref[:, 1024 * block + 128 * group : 1024 * block + 128 * (group + 1)] = low(part)
        for other in place.seq_peers:
            columns = pl.ds(pl.multiple_of(1024 * block + other * 128, 128), 128)
            head_copies.append(
                wire.send(act_ref.at[:, columns], target.at[seq], place.at_seq(other))
            )
        columns = pl.ds(pl.multiple_of(1024 * block + seq * 128, 128), 128)
        target[seq] = act_ref[:, columns]

    project(0, query_ref)
    tick(4)
    project(1, keys_ref)
    tick(5)
    project(2, values_ref)
    tick(6)
    arrive(head_copies)
    back_copies = []

    def send_back(frame):
        columns = pl.ds(pl.multiple_of(seq * 128, 128), 128)

        @pl.when(seq != frame)
        def _():
            pltpu.make_async_remote_copy(
                src_ref=attended_ref.at[frame],
                dst_ref=attended_tokens.at[:, columns],
                send_sem=back_send.at[frame],
                recv_sem=back_recv.at[seq],
                device_id=place.at_seq(frame),
                device_id_type=MESH_ID,
            ).start()

        @pl.when(seq == frame)
        def _():
            attended_tokens[:, columns] = attended_ref[frame]

    def back_copy(other):
        columns = pl.ds(pl.multiple_of(other * 128, 128), 128)
        return pltpu.make_async_remote_copy(
            src_ref=attended_ref.at[other],
            dst_ref=attended_tokens.at[:, columns],
            send_sem=back_send.at[other],
            recv_sem=back_recv.at[other],
            device_id=place.at_seq(other),
            device_id_type=MESH_ID,
        )

    for frame in range(8):
        attend_frame(
            frame, query_ref, keys_ref, values_ref, attended_ref, log_total_ref, scores
        )
        send_back(frame)
        if frame in (2, 5):
            tick(7 if frame == 2 else 8)
    tick(9)
    for other in place.seq_peers:
        back_copy(other).wait_recv()
    for other in place.seq_peers:
        back_copy(other).wait_send()
    for copy in head_copies:
        copy.wait_send()
    wire.sent = [copy for copy in wire.sent if not any(copy is done for done in head_copies)]
    branch_one = contract(attended_tokens[...], whole_piece(wide.at[3]), 1, 0)
    branch_one = branch_one + row_of(biases, 24)
    branch_one_ref[...] = branch_one
    middle = x_ref[...].astype(F32) + gate_one * branch_one
    middle_ref[...] = middle
    normed, unused = norm_parts(middle)
    normed_two_ref[...] = low(normed * (1.0 + scale_two) + shift_two)
    for block in range(4):
        if block == 3:
            tick(10)
        pre = contract(normed_two_ref[...], whole_piece(wide.at[4 + block]), 1, 0)
        act, slope = gelu_parts(pre + row_of(biases, 32 + 8 * block))
        act_ref[:, 1024 * block : 1024 * (block + 1)] = low(act)
        slope_ref[:, 1024 * block : 1024 * (block + 1)] = low(slope)
    for block in range(4):
        tick(11 + block)
        flat[0, :, 256 * block : 256 * (block + 1)] = contract(
            act_ref[...], whole_piece(down.at[block]), 1, 0
        )
    branch_two = flat[0] + row_of(biases, 64)
    layer_out_ref[...] = low(middle_ref[...] + gate_two * branch_two)
    gate_two_grad_ref[...] = jnp.sum(
        cotangent_ref[...].astype(F32) * branch_two, axis=0, keepdims=True
    )
    wire.drain()
    for copy in saved:
        copy.wait()


def vmem(shape, dtype=F32):
    return pltpu.VMEM(shape, dtype)


def run_forward(x, cotangent, level, table, w_ada, biases, w_qkv, w_out, w_up, w_down, cosine, sine):
    shape = jax.ShapeDtypeStruct
    heads = shape((8, 256, 128), BF16)
    outs = [
        ((256, 1024), BF16),
        ((8, 4, 4, 2, 32, 1024), BF16),
        ((4, 4, 4, 2, 128, 256), BF16),
        ((8, 256, 128), BF16),
        ((8, 256, 128), BF16),
        ((8, 256, 128), BF16),
        ((8, 256, 128), BF16),
        ((8, 1, 512), F32),
        ((256, 1024), BF16),
        ((256, 1024), BF16),
        ((256, 1024), BF16),
        ((256, 1024), F32),
        ((256, 1024), F32),
        ((256, 4096), BF16),
        ((256, 4096), BF16),
        ((8, 1024), F32),
        ((32, 128), F32),
        ((128, 128), F32),
        ((1, 1024), F32),
    ]
    in_vmem = pl.BlockSpec(memory_space=pltpu.VMEM)
    anywhere = pl.BlockSpec(memory_space=pl.ANY)
    scratch = [
        vmem((8, 4, 4, 2, 32, 1024), BF16),
        vmem((4, 4, 4, 2, 128, 256), BF16),
        vmem((4, 8, 8, 128)),
        vmem((4, 8, 32, 128), BF16),
        vmem((3, 8, 32, 128), BF16),
        vmem((8, 32, 128), BF16),
        vmem((7, 32, 128), BF16),
        vmem((48, 4, 8, 128)),
        vmem((3, 48, 8, 128)),
        vmem((384, 128)),
        vmem((8, 48, 128)),
        vmem((7, 48, 128)),
        vmem((3, 128, 128), BF16),
        vmem((128, 128), BF16),
        vmem((7, 128, 128), BF16),
        vmem((1, 256, 1024)),
        vmem((8, 256, 512)),
        pltpu.SemaphoreType.DMA((170,)),
        pltpu.SemaphoreType.DMA((170,)),
        pltpu.SemaphoreType.DMA((8,)),
        pltpu.SemaphoreType.DMA((8,)),
        pltpu.SemaphoreType.DMA((12,)),
    ]
    return pl.pallas_call(
        forward_kernel,
        out_shape=[shape(*out) for out in outs],
        in_specs=[in_vmem] * 12,
        out_specs=[in_vmem, anywhere, anywhere] + [in_vmem] * 16,
        scratch_shapes=scratch,
        compiler_params=pltpu.CompilerParams(
            collective_id=0, has_side_effects=True, vmem_limit_bytes=VMEM_LIMIT
        ),
        name="block_forward",
    )(x, cotangent, level, table, w_ada, biases, w_qkv, w_out, w_up, w_down, cosine, sine)


def rope_tables(head_dim):
    places = lax.axis_index("seq") * PATCHES + jnp.arange(PATCHES, dtype=jnp.int32)
    cosine, sine = angle_table(places, head_dim)
    lane = jnp.arange(head_dim)
    first = jnp.where(lane < 16, lane < 8, (lane - 16) % 24 < 12)
    sine = jnp.where(first, -sine, sine)
    return jnp.tile(cosine, (1, 2)), jnp.tile(sine, (1, 2))


def own_biases(shares):
    device = lax.axis_index("dp") * 8 + lax.axis_index("seq")
    parts = []
    for share in shares:
        whole = jnp.zeros((32,) + share.shape, BF16)
        parts.append(lax.dynamic_update_slice(whole, low(share)[None], (device, 0)).reshape(-1))
    lines = jnp.concatenate(parts).reshape(-1, 128)
    return jnp.pad(lines, ((0, 128 - lines.shape[0]), (0, 0)))


def fast_body(
    hidden_in,
    noise_level,
    noise_table,
    w_ada,
    b_ada,
    w_qkv,
    b_qkv,
    w_out,
    b_out,
    w_up,
    b_up,
    w_down,
    b_down,
    grad_out,
):
    cosine, sine = rope_tables(64)
    level = jnp.broadcast_to(noise_level.astype(F32), (8, 128))
    biases = own_biases((b_qkv, b_out, b_up, b_down, b_ada))
    (
        layer_out,
        wide,
        down,
        query,
        keys,
        values,
        attended,
        log_total,
        attended_tokens,
        normed_one,
        normed_two,
        middle,
        branch_one,
        act,
        slope,
        modulation,
        embedded,
        one_hot,
        grad_gate_two,
    ) = run_forward(
        hidden_in[0],
        grad_out[0],
        level,
        noise_table,
        w_ada,
        biases,
        w_qkv,
        w_out,
        w_up,
        w_down,
        cosine,
        sine,
    )
    wide = wide.reshape(8, 1024, 1024)
    down = down.reshape(4, 4096, 256)
    shift_one, scale_one, gate_one, shift_two, scale_two, gate_two = [
        modulation[block : block + 1] for block in range(6)
    ]
    cotangent = grad_out[0].astype(F32)
    grad_branch_two = low(cotangent * gate_two)

    def weight_grad(left, right):
        return scatter_rows(low(contract(left, right, 0, 0))).astype(F32)

    def bias_grad(grad):
        return scatter_rows(jnp.sum(grad.astype(F32), axis=0))

    down_flat = down.transpose(1, 0, 2).reshape(4096, 1024)
    up_flat = wide[4:].transpose(1, 0, 2).reshape(1024, 4096)
    qkv_flat = wide[:3].transpose(1, 0, 2).reshape(1024, 3072)
    grad_down_w = weight_grad(act, grad_branch_two)
    grad_pre = low(contract(grad_branch_two, down_flat, 1, 1) * slope.astype(F32))
    grad_up_w = weight_grad(normed_two, grad_pre)
    grad_normed_two = contract(grad_pre, up_flat, 1, 1)
    unused, norm_two_back = jax.vjp(modulate, middle, shift_two, scale_two)
    grad_middle_norm, grad_shift_two, grad_scale_two = norm_two_back(grad_normed_two)
    grad_middle = cotangent + grad_middle_norm
    grad_gate_one = jnp.sum(grad_middle * branch_one, axis=0, keepdims=True)
    grad_branch_one = low(grad_middle * gate_one)
    grad_out_w = weight_grad(attended_tokens, grad_branch_one)
    grad_attended = low(contract(grad_branch_one, wide[3], 1, 1))
    grad_heads = to_heads(grad_attended[None])

    def headed(piece):
        return piece.reshape(1, 2048, 2, 64)

    row_delta = jnp.sum(
        headed(grad_heads).astype(F32) * headed(attended).astype(F32), axis=-1
    ).transpose(0, 2, 1)
    totals = log_total.reshape(8, 2, 256).transpose(1, 0, 2).reshape(1, 2, 2048)
    gradients = attend_back(
        headed(query), headed(keys), headed(values), headed(grad_heads), totals, row_delta, 1.0
    )
    grad_query, grad_keys, grad_values = [
        to_tokens(low(grad).reshape(1, 2048, 128))[0].astype(F32) for grad in gradients
    ]
    wide_cosine, wide_sine = jnp.tile(cosine, (1, 8)), jnp.tile(sine, (1, 8))

    def unturned(grad):
        lane = jnp.arange(1024) % 64
        first = (lane < 8) | ((lane >= 16) & (lane < 28)) | ((lane >= 40) & (lane < 52))
        up = jnp.where(lane < 16, jnp.roll(grad, -8, 1), jnp.roll(grad, -12, 1))
        back = jnp.where(lane < 16, jnp.roll(grad, 8, 1), jnp.roll(grad, 12, 1))
        return low(grad * wide_cosine - jnp.where(first, up, back) * wide_sine)

    grad_qkv = jnp.concatenate(
        [unturned(grad_query * 0.125), unturned(grad_keys), low(grad_values)], axis=1
    )
    grad_qkv_w = weight_grad(normed_one, grad_qkv)
    grad_normed_one = contract(grad_qkv, qkv_flat, 1, 1)
    unused, norm_one_back = jax.vjp(modulate, hidden_in[0].astype(F32), shift_one, scale_one)
    grad_input_norm, grad_shift_one, grad_scale_one = norm_one_back(grad_normed_one)
    grad_modulation = low(
        jnp.concatenate(
            [
                grad_shift_one,
                grad_scale_one,
                grad_gate_one,
                grad_shift_two,
                grad_scale_two,
                grad_gate_two,
            ],
            axis=1,
        )
    )
    columns = embedded[:, :32].T
    grad_table, grad_ada_w, grad_ada_b = frame_gradients(
        grad_modulation, one_hot[:32, :32], columns, low(jax.nn.silu(columns)), w_ada
    )
    return (
        layer_out[None],
        low(grad_middle + grad_input_norm)[None],
        grad_table,
        grad_ada_w,
        grad_ada_b,
        grad_qkv_w,
        bias_grad(grad_qkv),
        grad_out_w,
        bias_grad(grad_branch_one),
        grad_up_w,
        bias_grad(grad_pre),
        grad_down_w,
        bias_grad(grad_branch_two),
    )


def solution(mesh):
    tokens = P("dp", "seq", None)
    matrix = P(ALL, None)
    vector = P(ALL)
    parameters = (matrix,) + (matrix, vector) * 5
    chips = dict(mesh.shape) == {"dp": 4, "seq": 8}
    return jax.shard_map(
        fast_body if chips else general_body,
        mesh=mesh,
        in_specs=(tokens, P("dp", "seq")) + parameters + (tokens,),
        out_specs=(tokens, tokens) + parameters,
        check_vma=False,
    )
```

```python
from functools import partial
import math

import jax
import jax.numpy as jnp
from jax import lax
from jax.experimental import pallas as pl
from jax.experimental.pallas import tpu as pltpu
from jax.sharding import PartitionSpec as P

H = 16
GRID_W = 16
PATCHES = 256


norm_eps = 1e-06
masked_score = -1e30
ALL = ("dp", "seq")
F32 = jnp.float32
BF16 = jnp.bfloat16


def layer_norm(values):
    centred = values - jnp.mean(values, axis=-1, keepdims=True)
    spread = jnp.mean(centred * centred, axis=-1, keepdims=True)
    return centred * lax.rsqrt(spread + norm_eps)


def modulate(values, shift_term, scale_term):
    return layer_norm(values) * (1.0 + scale_term) + shift_term


def turn_half(values):
    extent = values.shape[-1]
    side_part = 2 * (3 * extent // 16)
    pieces = []
    offset = 0
    for part_size in (extent - 2 * side_part, side_part, side_part):
        half_size = part_size // 2
        pieces.append(-values[..., offset + half_size : offset + part_size])
        pieces.append(values[..., offset : offset + half_size])
        offset = offset + part_size
    return jnp.concatenate(pieces, axis=-1)


def part_angles(places, part_size):
    half_size = part_size // 2
    rates = jnp.exp(-math.log(10000.0) * jnp.arange(half_size, dtype=F32) / half_size)
    angles = places.astype(F32)[:, None] * rates[None, :]
    return jnp.concatenate([angles, angles], axis=1)


def angle_table(places, extent):
    side_part = 2 * (3 * extent // 16)
    patch_index = places % PATCHES
    angles = jnp.concatenate(
        [
            part_angles(places // PATCHES, extent - 2 * side_part),
            part_angles(patch_index // GRID_W, side_part),
            part_angles(patch_index % GRID_W, side_part),
        ],
        axis=1,
    )
    return (jnp.cos(angles), jnp.sin(angles))


def rotate(values, cosine_table, sine_table):
    return values * cosine_table + turn_half(values) * sine_table


def unrotate(values, cosine_table, sine_table):
    return values * cosine_table - turn_half(values * sine_table)


def low(values):
    return values.astype(BF16)


def dot(left, right):
    return jnp.dot(left, right, preferred_element_type=F32)


def gather_rows(share):
    return lax.all_gather(low(share), ALL, axis=0, tiled=True)


def scatter_rows(whole):
    return lax.psum_scatter(whole, ALL, scatter_dimension=0, tiled=True)


def frame_modulation(noise_level, noise_table, w_ada, b_ada):
    levels = lax.all_gather(noise_level.reshape(-1), ALL, axis=0, tiled=True)
    device = lax.axis_index("dp") * lax.axis_size("seq") + lax.axis_index("seq")
    share = noise_table.shape[0]
    own_levels = device * share + jnp.arange(share, dtype=jnp.int32)
    one_hot = levels[:, None] == own_levels[None, :]
    found = dot(low(one_hot), low(noise_table))
    embedded = lax.psum_scatter(low(found), ALL, scatter_dimension=1, tiled=True).astype(F32)
    silu_in = low(jax.nn.silu(embedded))
    modulation = lax.psum_scatter(
        dot(silu_in, low(w_ada)), ALL, scatter_dimension=0, tiled=True
    ) + gather_rows(b_ada).astype(F32)
    return one_hot, embedded, silu_in, modulation


def frame_gradients(grad_modulation, one_hot, embedded, silu_in, w_ada):
    every = lax.all_gather(grad_modulation, ALL, axis=0, tiled=True)
    grad_ada_w = lax.dot_general(
        silu_in, every, (((0,), (0,)), ((), ())), preferred_element_type=F32
    )
    share = w_ada.shape[1] // lax.axis_size(ALL)
    device = lax.axis_index("dp") * lax.axis_size("seq") + lax.axis_index("seq")
    columns = lax.dynamic_slice_in_dim(every, device * share, share, axis=1)
    grad_ada_b = jnp.sum(columns.astype(F32), axis=0)
    grad_silu = lax.dot_general(
        every, low(w_ada), (((1,), (1,)), ((), ())), preferred_element_type=F32
    )
    unused, silu_back = jax.vjp(jax.nn.silu, embedded)
    grad_embedded = lax.all_gather(silu_back(grad_silu)[0], ALL, axis=1, tiled=True)
    grad_table = jnp.dot(
        one_hot.astype(F32).T, grad_embedded, precision=lax.Precision.HIGHEST
    )
    return grad_table, grad_ada_w, grad_ada_b


def to_heads(values):
    return lax.all_to_all(values, "seq", split_axis=2, concat_axis=1, tiled=True)


def to_tokens(values):
    return lax.all_to_all(values, "seq", split_axis=1, concat_axis=2, tiled=True)


def as_heads(values):
    return values.reshape(*values.shape[:2], -1, 64)


def query_blocks(array, axis):
    blocks = array.shape[axis] // PATCHES
    split = array.shape[:axis] + (blocks, PATCHES) + array.shape[axis + 1 :]
    return jnp.moveaxis(array.reshape(split), axis, 0)


def block_scores(query_block, keys, frame, score_scale):
    scores = (
        jnp.einsum("cqhd,ckhd->chqk", query_block, keys, preferred_element_type=F32) * score_scale
    )
    allowed = jnp.arange(keys.shape[1], dtype=jnp.int32) // PATCHES <= frame
    return jnp.where(allowed, scores, masked_score)


def attend(query, keys, values, score_scale):
    def one_block(block_in):
        query_block, frame = block_in
        scores = block_scores(query_block, keys, frame, score_scale)
        row_max = jnp.max(scores, axis=-1, keepdims=True)
        exponent = jnp.exp(scores - row_max)
        row_total = jnp.sum(exponent, axis=-1, keepdims=True)
        weighted = jnp.einsum(
            "chqk,ckhd->cqhd", low(exponent / row_total), values, preferred_element_type=F32
        )
        return low(weighted), (row_max + jnp.log(row_total))[..., 0]

    frames = jnp.arange(query.shape[1] // PATCHES, dtype=jnp.int32)
    attended, log_total = lax.map(one_block, (query_blocks(query, 1), frames))
    return (
        jnp.moveaxis(attended, 0, 1).reshape(query.shape),
        jnp.moveaxis(log_total, 0, 2).reshape(query.shape[0], query.shape[2], query.shape[1]),
    )


def attend_back(query, keys, values, grad_heads, log_total, row_delta, score_scale):
    def one_block(carried, block_in):
        query_block, grad_block, total_block, delta_block, frame = block_in
        scores = block_scores(query_block, keys, frame, score_scale)
        softmax_weights = jnp.exp(scores - total_block[..., None])
        grad_soft = jnp.einsum("cqhd,ckhd->chqk", grad_block, values, preferred_element_type=F32)
        grad_scores = low(softmax_weights * (grad_soft - delta_block[..., None]))
        query_grad = jnp.einsum("chqk,ckhd->cqhd", grad_scores, keys, preferred_element_type=F32)
        keys_grad = jnp.einsum(
            "chqk,cqhd->ckhd", grad_scores, query_block, preferred_element_type=F32
        )
        values_grad = jnp.einsum(
            "chqk,cqhd->ckhd", low(softmax_weights), grad_block, preferred_element_type=F32
        )
        return (carried[0] + keys_grad, carried[1] + values_grad), query_grad

    frames = jnp.arange(query.shape[1] // PATCHES, dtype=jnp.int32)
    empty = jnp.zeros(keys.shape, F32)
    (grad_keys, grad_values), grad_query = lax.scan(
        one_block,
        (empty, empty),
        (
            query_blocks(query, 1),
            query_blocks(grad_heads, 1),
            query_blocks(log_total, 2),
            query_blocks(row_delta, 2),
            frames,
        ),
    )
    grad_query = jnp.moveaxis(grad_query, 0, 1).reshape(query.shape)
    return grad_query * score_scale, grad_keys * score_scale, grad_values


def general_body(
    hidden_in,
    noise_level,
    noise_table,
    w_ada,
    b_ada,
    w_qkv,
    b_qkv,
    w_out,
    b_out,
    w_up,
    b_up,
    w_down,
    b_down,
    grad_out,
):
    qkv_w, qkv_b, out_w, out_b, up_w, up_b, down_w, down_b = [
        gather_rows(share)
        for share in (w_qkv, b_qkv, w_out, b_out, w_up, b_up, w_down, b_down)
    ]
    clip_count, patches, model_width = hidden_in.shape
    head_dim = model_width // H
    score_scale = 1.0 / math.sqrt(head_dim)
    head_shape = (clip_count, patches, H, head_dim)
    inputs = hidden_in.astype(F32)
    one_hot, embedded, silu_in, modulation = frame_modulation(
        noise_level, noise_table, w_ada, b_ada
    )
    shift_one, scale_one, gate_one, shift_two, scale_two, gate_two = [
        modulation[:, None, column_block * model_width : (column_block + 1) * model_width]
        for column_block in range(6)
    ]
    normed_one = low(modulate(inputs, shift_one, scale_one))
    qkv_all = dot(normed_one, qkv_w) + qkv_b.astype(F32)
    frame_own = lax.axis_index("seq")
    places = frame_own * patches + jnp.arange(patches, dtype=jnp.int32)
    cosine_local, sine_local = angle_table(places, head_dim)
    cosine_wide = cosine_local[None, :, None, :]
    sine_wide = sine_local[None, :, None, :]
    flat_shape = (clip_count, patches, model_width)

    def turned(block):
        part = qkv_all[..., block * model_width : (block + 1) * model_width]
        return low(rotate(part.reshape(head_shape), cosine_wide, sine_wide)).reshape(flat_shape)

    query = as_heads(to_heads(turned(0)))
    keys = as_heads(to_heads(turned(1)))
    values = as_heads(to_heads(low(qkv_all[..., 2 * model_width :])))
    attended, log_total = attend(query, keys, values, score_scale)
    attended_low = to_tokens(attended.reshape(*attended.shape[:2], -1))
    branch_one = dot(attended_low, out_w) + out_b.astype(F32)
    middle = inputs + gate_one * branch_one
    normed_two = low(modulate(middle, shift_two, scale_two))
    hidden_pre = dot(normed_two, up_w) + up_b.astype(F32)
    hidden_act = low(jax.nn.gelu(hidden_pre, approximate=True))
    branch_two = dot(hidden_act, down_w) + down_b.astype(F32)
    outputs = middle + gate_two * branch_two
    cotangent = grad_out.astype(F32)
    grad_gate_two = jnp.sum(cotangent * branch_two, axis=1)
    grad_branch_two = low(cotangent * gate_two)

    def weight_grad(left, right):
        whole = jnp.einsum("cpi,cpo->io", left, right, preferred_element_type=F32)
        return scatter_rows(low(whole)).astype(F32)

    def bias_grad(grad):
        return scatter_rows(jnp.sum(grad.astype(F32), axis=(0, 1)))

    def back_dot(grad, weight):
        return jnp.einsum("cpo,io->cpi", grad, weight, preferred_element_type=F32)

    grad_down_w = weight_grad(hidden_act, grad_branch_two)
    grad_down_b = bias_grad(grad_branch_two)
    grad_act = back_dot(grad_branch_two, down_w)
    unused, gelu_back = jax.vjp(partial(jax.nn.gelu, approximate=True), hidden_pre)
    grad_pre = low(gelu_back(grad_act)[0])
    grad_up_w = weight_grad(normed_two, grad_pre)
    grad_up_b = bias_grad(grad_pre)
    grad_normed_two = back_dot(grad_pre, up_w)
    unused, norm_two_back = jax.vjp(modulate, middle, shift_two, scale_two)
    grad_middle_norm, grad_shift_two, grad_scale_two = norm_two_back(grad_normed_two)
    grad_middle = cotangent + grad_middle_norm
    grad_gate_one = jnp.sum(grad_middle * branch_one, axis=1)
    grad_branch_one = low(grad_middle * gate_one)
    grad_out_w = weight_grad(attended_low, grad_branch_one)
    grad_out_b = bias_grad(grad_branch_one)
    grad_attended = low(back_dot(grad_branch_one, out_w))
    grad_heads = as_heads(to_heads(grad_attended))
    row_delta = jnp.sum(grad_heads.astype(F32) * attended.astype(F32), axis=-1).transpose(0, 2, 1)
    grad_query, grad_keys, grad_values = attend_back(
        query, keys, values, grad_heads, log_total, row_delta, score_scale
    )

    def home(grad):
        return to_tokens(low(grad).reshape(*grad.shape[:2], -1))

    def unturned(grad):
        wide = home(grad).astype(F32).reshape(head_shape)
        return low(unrotate(wide, cosine_wide, sine_wide)).reshape(flat_shape)

    grad_qkv = jnp.concatenate(
        [unturned(grad_query), unturned(grad_keys), home(grad_values)], axis=-1
    )
    grad_qkv_w = weight_grad(normed_one, grad_qkv)
    grad_qkv_b = bias_grad(grad_qkv)
    grad_normed_one = back_dot(grad_qkv, qkv_w)
    unused, norm_one_back = jax.vjp(modulate, inputs, shift_one, scale_one)
    grad_input_norm, grad_shift_one, grad_scale_one = norm_one_back(grad_normed_one)
    grad_input = grad_middle + grad_input_norm
    grad_modulation = low(
        jnp.concatenate(
            [
                grad_shift_one[:, 0],
                grad_scale_one[:, 0],
                grad_gate_one,
                grad_shift_two[:, 0],
                grad_scale_two[:, 0],
                grad_gate_two,
            ],
            axis=-1,
        )
    )
    grad_table, grad_ada_w, grad_ada_b = frame_gradients(
        grad_modulation, one_hot, embedded, silu_in, w_ada
    )
    return (
        low(outputs),
        low(grad_input),
        grad_table,
        grad_ada_w,
        grad_ada_b,
        grad_qkv_w,
        grad_qkv_b,
        grad_out_w,
        grad_out_b,
        grad_up_w,
        grad_up_b,
        grad_down_w,
        grad_down_b,
    )


MESH_ID = pl.DeviceIdType.MESH
VMEM_LIMIT = 63 * 1024 * 1024
HEADS_WIDE = 128


def contract(left, right, left_dim, right_dim, precision=None):
    return lax.dot_general(
        left,
        right,
        (((left_dim,), (right_dim,)), ((), ())),
        preferred_element_type=F32,
        precision=precision,
    )


class Place:
    def __init__(self):
        self.dp = lax.axis_index("dp")
        self.seq = lax.axis_index("seq")
        self.z = self.seq // 2
        self.core = self.seq % 2
        self.other = 1 - self.core
        self.x_dp = self.dp + 1 - 2 * (self.dp % 2)
        self.y_dp = (self.dp + 2) % 4
        self.far_dp = 3 - self.dp
        self.dp_peers = (self.x_dp, self.y_dp, self.far_dp)
        self.seq_peers = [(self.seq + step) % 8 for step in range(1, 8)]
        self.sibling = (self.dp, self.z * 2 + self.other)

    def at_dp(self, dp):
        return (dp, self.seq)

    def at_seq(self, seq):
        return (self.dp, seq)

    def greet(self):
        barrier = pltpu.get_barrier_semaphore()
        peers = [self.at_dp(dp) for dp in self.dp_peers]
        peers += [self.at_seq(seq) for seq in self.seq_peers]
        for peer in peers:
            pl.semaphore_signal(barrier, inc=1, device_id=peer, device_id_type=MESH_ID)
        pl.semaphore_wait(barrier, len(peers))


class Wire:
    def __init__(self, send_sems, recv_sems):
        self.send_sems = send_sems
        self.recv_sems = recv_sems
        self.used = 0
        self.sent = []

    def send(self, source, target, device):
        copy = pltpu.make_async_remote_copy(
            src_ref=source,
            dst_ref=target,
            send_sem=self.send_sems.at[self.used],
            recv_sem=self.recv_sems.at[self.used],
            device_id=device,
            device_id_type=MESH_ID,
        )
        self.used += 1
        copy.start()
        self.sent.append(copy)
        return copy

    def drain(self):
        for copy in self.sent:
            copy.wait_send()
        self.sent = []


def arrive(copies):
    for copy in copies:
        copy.wait_recv()


class Gather:
    def __init__(self, wire, place, ref):
        self.wire, self.place, self.ref = wire, place, ref

    def along_z(self):
        place, ref = self.place, self.ref
        own = ref.at[place.dp, place.z, place.core]
        self.coming = [
            self.wire.send(own, own, place.at_seq(((place.z + step) % 4) * 2 + place.core))
            for step in (1, 2, 3)
        ]

    def along_xy(self):
        place = self.place
        arrive(self.coming)
        own = self.ref.at[place.dp, :, place.core]
        self.coming = [
            self.wire.send(own, own, place.at_dp(dp)) for dp in (place.x_dp, place.y_dp)
        ]

    def across(self):
        place = self.place
        arrive(self.coming)
        from_x = self.ref.at[place.x_dp, pl.ds(0, 2), place.core]
        from_y = self.ref.at[place.y_dp, pl.ds(2, 2), place.core]
        self.coming = [
            self.wire.send(from_x, from_x, place.at_dp(place.y_dp)),
            self.wire.send(from_y, from_y, place.at_dp(place.x_dp)),
        ]

    def to_sibling(self):
        place = self.place
        arrive(self.coming)
        mine = self.ref.at[:, :, place.core]
        self.coming = [self.wire.send(mine, mine, place.sibling)]

    def finish(self):
        arrive(self.coming)


class SmallGather:
    def __init__(self, wire, place, ref):
        self.wire, self.place, self.ref = wire, place, ref

    def along_seq(self):
        place = self.place
        own = self.ref.at[place.dp, place.seq]
        self.coming = [self.wire.send(own, own, place.at_seq(seq)) for seq in place.seq_peers]

    def along_dp(self):
        place = self.place
        arrive(self.coming)
        own = self.ref.at[place.dp]
        self.coming = [self.wire.send(own, own, place.at_dp(dp)) for dp in place.dp_peers]

    def finish(self):
        arrive(self.coming)


def spread_dp(wire, place, part_of, slots):
    return [
        wire.send(part_of(dp), slots.at[index], place.at_dp(dp))
        for index, dp in enumerate(place.dp_peers)
    ]


def spread_seq(wire, place, part_of, slots):
    return [
        wire.send(part_of(seq), slots.at[index], place.at_seq(seq))
        for index, seq in enumerate(place.seq_peers)
    ]


def total_of(own, slots, count):
    total = own
    for index in range(count):
        total = total + slots[index].astype(F32)
    return total


def row_of(lines, first):
    return jnp.concatenate([lines[first + line : first + line + 1, :] for line in range(8)], axis=1)


def lines_of(row):
    return jnp.concatenate([row[:, 128 * line : 128 * (line + 1)] for line in range(8)], axis=0)


def whole_piece(piece):
    value = piece[...]
    return value.reshape(-1, value.shape[-1])


def norm_parts(values):
    centred = values - jnp.mean(values, axis=1, keepdims=True)
    inverse = lax.rsqrt(jnp.mean(centred * centred, axis=1, keepdims=True) + norm_eps)
    return centred * inverse, inverse


def half_turn(values):
    lane = lax.broadcasted_iota(jnp.int32, values.shape, 1) % 64
    in_time = lane < 16
    first = (lane < 8) | ((lane >= 16) & (lane < 28)) | ((lane >= 40) & (lane < 52))
    up = jnp.where(in_time, pltpu.roll(values, 120, 1), pltpu.roll(values, 116, 1))
    down = jnp.where(in_time, pltpu.roll(values, 8, 1), pltpu.roll(values, 12, 1))
    return jnp.where(first, up, down)


def split_heads(values):
    lane = lax.broadcasted_iota(jnp.int32, values.shape, 1)
    empty = jnp.zeros_like(values)
    return jnp.concatenate(
        [jnp.where(lane < 64, values, empty), jnp.where(lane < 64, empty, values)], axis=0
    )


def join_heads(turned):
    return jnp.concatenate([turned[:64, :256], turned[64:, 256:]], axis=0).T


def attend_frame(frame, query, keys, values, attended, log_total, scores):
    pair = split_heads(query[frame])
    row_max = None
    for block in range(frame + 1):
        block_scores = contract(keys[block], pair, 1, 1)
        scores[block] = block_scores
        block_max = jnp.max(block_scores, axis=0, keepdims=True)
        row_max = block_max if row_max is None else jnp.maximum(row_max, block_max)
    row_total = None
    weighted = None
    for block in range(frame + 1):
        exponent = jnp.exp(scores[block] - row_max)
        block_total = jnp.sum(exponent, axis=0, keepdims=True)
        block_sum = contract(values[block], exponent.astype(BF16), 0, 0)
        row_total = block_total if row_total is None else row_total + block_total
        weighted = block_sum if weighted is None else weighted + block_sum
    attended[frame] = join_heads(weighted / row_total).astype(BF16)
    log_total[frame] = row_max + jnp.log(row_total)


SQRT_TWO_OVER_PI = math.sqrt(2.0 / math.pi)


def gelu_parts(values):
    square = values * values
    bent = jnp.tanh(SQRT_TWO_OVER_PI * values * (1.0 + 0.044715 * square))
    half = 0.5 * (1.0 + bent)
    slope = half + 0.5 * values * (1.0 - bent * bent) * (
        SQRT_TWO_OVER_PI * (1.0 + 3.0 * 0.044715 * square)
    )
    return values * half, slope


def forward_kernel(
    x_ref,
    cotangent_ref,
    level_ref,
    table_ref,
    w_ada_ref,
    bias_ref,
    w_qkv_ref,
    w_out_ref,
    w_up_ref,
    w_down_ref,
    cosine_ref,
    sine_ref,
    layer_out_ref,
    wide_out,
    down_out,
    query_ref,
    keys_ref,
    values_ref,
    attended_ref,
    log_total_ref,
    attended_tokens,
    normed_one_ref,
    normed_two_ref,
    middle_ref,
    branch_one_ref,
    act_ref,
    slope_ref,
    modulation_ref,
    embedded_ref,
    one_hot_ref,
    gate_two_grad_ref,
    wide,
    down,
    levels,
    found,
    found_dp,
    found_sum,
    found_seq,
    partial_mod,
    mod_dp,
    mod_sum,
    mod_blocks,
    mod_seq,
    bias_dp,
    bias_sum,
    bias_seq,
    flat,
    scores,
    send_sems,
    recv_sems,
    back_send,
    back_recv,
    local_sems,
):
    place = Place()
    wire = Wire(send_sems, recv_sems)
    dp, seq, z, core = place.dp, place.seq, place.z, place.core
    device = dp * 8 + seq
    levels[dp, seq] = level_ref[...]
    for block in range(3):
        wide[block, dp, z, core] = low(w_qkv_ref[:, 1024 * block : 1024 * (block + 1)])
    place.greet()
    level_gather = SmallGather(wire, place, levels)
    level_gather.along_seq()
    pieces = [Gather(wire, place, wide.at[index]) for index in range(8)]
    pieces += [Gather(wire, place, down.at[index]) for index in range(4)]
    pieces[0].along_z()
    pieces[1].along_z()
    bias_copies = spread_dp(wire, place, lambda dp: bias_ref, bias_dp)
    wide[3, dp, z, core] = low(w_out_ref[...])
    for block in range(4):
        wide[4 + block, dp, z, core] = low(w_up_ref[:, 1024 * block : 1024 * (block + 1)])
    for block in range(4):
        down[block, dp, z, core] = low(w_down_ref[:, 256 * block : 256 * (block + 1)])
    pieces[2].along_z()
    saved = []

    def save(index):
        pieces[index].finish()
        source, target = (
            (wide.at[index], wide_out.at[index])
            if index < 8
            else (down.at[index - 8], down_out.at[index - 8])
        )
        copy = pltpu.make_async_copy(source, target, local_sems.at[index])
        copy.start()
        saved.append(copy)

    def tick(step, finish=True):
        if step + 2 < 12 and step > 0:
            pieces[step + 2].along_z()
        if step < 12:
            pieces[step].along_xy()
        if 0 <= step - 1 < 12:
            pieces[step - 1].across()
        if 0 <= step - 2 < 12:
            pieces[step - 2].to_sibling()
        if finish and 0 <= step - 3 < 12:
            save(step - 3)

    level_gather.along_dp()
    x = x_ref[...].astype(F32)
    normed, unused = norm_parts(x)
    flat[0] = normed
    level_gather.finish()
    level_rows = jnp.concatenate(
        [levels[group, frame, 0:1, :] for group in range(4) for frame in range(8)]
        + [jnp.full((96, 128), -1.0, F32)],
        axis=0,
    )
    lane = lax.broadcasted_iota(jnp.int32, (128, 128), 1)
    own_level = (lane + device * 32).astype(F32)
    one_hot = jnp.where((level_rows == own_level) & (lane < 32), 1.0, 0.0)
    one_hot_ref[...] = one_hot
    one_hot_turned = low(one_hot.T)[:32, :]
    found[...] = low(contract(low(table_ref[...]), one_hot_turned, 0, 0)).reshape(found.shape)
    found_copies = spread_dp(wire, place, lambda dp: found.at[dp], found_dp)
    pieces[0].along_xy()
    arrive(found_copies)
    found_sum[...] = low(total_of(found[dp].astype(F32), found_dp, 3))
    found_copies = spread_seq(wire, place, lambda seq: found_sum.at[seq], found_seq)
    tick(1)
    arrive(found_copies)
    embedded = total_of(found_sum[seq].astype(F32), found_seq, 7)
    embedded_ref[...] = embedded
    silu_in = low(embedded / (1.0 + jnp.exp(-embedded)))
    for block in range(6):
        part = contract(silu_in, low(w_ada_ref[:, 1024 * block : 1024 * (block + 1)]), 0, 0)
        for line in range(8):
            partial_mod[8 * block + line] = part[:32, 128 * line : 128 * (line + 1)].reshape(
                4, 8, 128
            )
    mod_copies = spread_dp(wire, place, lambda dp: partial_mod.at[:, dp], mod_dp)
    arrive(bias_copies)
    bias_sum[...] = low(total_of(bias_ref[...].astype(F32), bias_dp, 3))
    bias_copies = spread_seq(wire, place, lambda seq: bias_sum, bias_seq)
    tick(2)
    arrive(mod_copies)
    mod_sum[...] = total_of(partial_mod[:, dp], mod_dp, 3).reshape(384, 128)
    for frame in range(8):
        mod_blocks[frame] = mod_sum[pl.ds(frame, 48, stride=8), :]
    mod_copies = spread_seq(wire, place, lambda seq: mod_blocks.at[seq], mod_seq)
    tick(3)
    arrive(bias_copies)
    biases = total_of(bias_sum[...].astype(F32), bias_seq, 7)
    arrive(mod_copies)
    modulation = total_of(mod_blocks[seq], mod_seq, 7) + biases[72:120]
    for block in range(6):
        modulation_ref[block : block + 1, :] = row_of(modulation, 8 * block)
    shift_one = modulation_ref[0:1, :]
    scale_one = modulation_ref[1:2, :]
    gate_one = modulation_ref[2:3, :]
    shift_two = modulation_ref[3:4, :]
    scale_two = modulation_ref[4:5, :]
    gate_two = modulation_ref[5:6, :]
    normed_one_ref[...] = low(flat[0] * (1.0 + scale_one) + shift_one)
    cosine = cosine_ref[...]
    sine = sine_ref[...]
    head_copies = []

    def project(block, target):
        r = contract(normed_one_ref[...], whole_piece(wide.at[block]), 1, 0)
        r = r + row_of(biases, 8 * block)
        for group in range(8):
            part = r[:, 128 * group : 128 * (group + 1)]
            if block < 2:
                part = part * cosine + half_turn(part) * sine
            if block == 0:
                part = part * 0.125
            act_ref[:, 1024 * block + 128 * group : 1024 * block + 128 * (group + 1)] = low(part)
        for other in place.seq_peers:
            columns = pl.ds(pl.multiple_of(1024 * block + other * 128, 128), 128)
            head_copies.append(
                wire.send(act_ref.at[:, columns], target.at[seq], place.at_seq(other))
            )
        columns = pl.ds(pl.multiple_of(1024 * block + seq * 128, 128), 128)
        target[seq] = act_ref[:, columns]

    project(0, query_ref)
    tick(4)
    project(1, keys_ref)
    tick(5)
    project(2, values_ref)
    tick(6)
    arrive(head_copies)
    back_copies = []

    def send_back(frame):
        columns = pl.ds(pl.multiple_of(seq * 128, 128), 128)

        @pl.when(seq != frame)
        def _():
            pltpu.make_async_remote_copy(
                src_ref=attended_ref.at[frame],
                dst_ref=attended_tokens.at[:, columns],
                send_sem=back_send.at[frame],
                recv_sem=back_recv.at[seq],
                device_id=place.at_seq(frame),
                device_id_type=MESH_ID,
            ).start()

        @pl.when(seq == frame)
        def _():
            attended_tokens[:, columns] = attended_ref[frame]

    def back_copy(other):
        columns = pl.ds(pl.multiple_of(other * 128, 128), 128)
        return pltpu.make_async_remote_copy(
            src_ref=attended_ref.at[other],
            dst_ref=attended_tokens.at[:, columns],
            send_sem=back_send.at[other],
            recv_sem=back_recv.at[other],
            device_id=place.at_seq(other),
            device_id_type=MESH_ID,
        )

    for frame in range(8):
        attend_frame(
            frame, query_ref, keys_ref, values_ref, attended_ref, log_total_ref, scores
        )
        send_back(frame)
        if frame in (2, 5):
            tick(7 if frame == 2 else 8)
    tick(9)
    for other in place.seq_peers:
        back_copy(other).wait_recv()
    for other in place.seq_peers:
        back_copy(other).wait_send()
    for copy in head_copies:
        copy.wait_send()
    wire.sent = [copy for copy in wire.sent if not any(copy is done for done in head_copies)]
    branch_one = contract(attended_tokens[...], whole_piece(wide.at[3]), 1, 0)
    branch_one = branch_one + row_of(biases, 24)
    branch_one_ref[...] = branch_one
    middle = x_ref[...].astype(F32) + gate_one * branch_one
    middle_ref[...] = middle
    normed, unused = norm_parts(middle)
    normed_two_ref[...] = low(normed * (1.0 + scale_two) + shift_two)
    for block in range(4):
        if block == 3:
            tick(10)
        pre = contract(normed_two_ref[...], whole_piece(wide.at[4 + block]), 1, 0)
        act, slope = gelu_parts(pre + row_of(biases, 32 + 8 * block))
        act_ref[:, 1024 * block : 1024 * (block + 1)] = low(act)
        slope_ref[:, 1024 * block : 1024 * (block + 1)] = low(slope)
    for block in range(4):
        tick(11 + block)
        flat[0, :, 256 * block : 256 * (block + 1)] = contract(
            act_ref[...], whole_piece(down.at[block]), 1, 0
        )
    branch_two = flat[0] + row_of(biases, 64)
    layer_out_ref[...] = low(middle_ref[...] + gate_two * branch_two)
    gate_two_grad_ref[...] = jnp.sum(
        cotangent_ref[...].astype(F32) * branch_two, axis=0, keepdims=True
    )
    wire.drain()
    for copy in saved:
        copy.wait()


def vmem(shape, dtype=F32):
    return pltpu.VMEM(shape, dtype)


def run_forward(x, cotangent, level, table, w_ada, biases, w_qkv, w_out, w_up, w_down, cosine, sine):
    shape = jax.ShapeDtypeStruct
    heads = shape((8, 256, 128), BF16)
    outs = [
        ((256, 1024), BF16),
        ((8, 4, 4, 2, 32, 1024), BF16),
        ((4, 4, 4, 2, 128, 256), BF16),
        ((8, 256, 128), BF16),
        ((8, 256, 128), BF16),
        ((8, 256, 128), BF16),
        ((8, 256, 128), BF16),
        ((8, 1, 512), F32),
        ((256, 1024), BF16),
        ((256, 1024), BF16),
        ((256, 1024), BF16),
        ((256, 1024), F32),
        ((256, 1024), F32),
        ((256, 4096), BF16),
        ((256, 4096), BF16),
        ((8, 1024), F32),
        ((32, 128), F32),
        ((128, 128), F32),
        ((1, 1024), F32),
    ]
    in_vmem = pl.BlockSpec(memory_space=pltpu.VMEM)
    anywhere = pl.BlockSpec(memory_space=pl.ANY)
    scratch = [
        vmem((8, 4, 4, 2, 32, 1024), BF16),
        vmem((4, 4, 4, 2, 128, 256), BF16),
        vmem((4, 8, 8, 128)),
        vmem((4, 8, 32, 128), BF16),
        vmem((3, 8, 32, 128), BF16),
        vmem((8, 32, 128), BF16),
        vmem((7, 32, 128), BF16),
        vmem((48, 4, 8, 128)),
        vmem((3, 48, 8, 128)),
        vmem((384, 128)),
        vmem((8, 48, 128)),
        vmem((7, 48, 128)),
        vmem((3, 128, 128), BF16),
        vmem((128, 128), BF16),
        vmem((7, 128, 128), BF16),
        vmem((1, 256, 1024)),
        vmem((8, 256, 512)),
        pltpu.SemaphoreType.DMA((170,)),
        pltpu.SemaphoreType.DMA((170,)),
        pltpu.SemaphoreType.DMA((8,)),
        pltpu.SemaphoreType.DMA((8,)),
        pltpu.SemaphoreType.DMA((12,)),
    ]
    return pl.pallas_call(
        forward_kernel,
        out_shape=[shape(*out) for out in outs],
        in_specs=[in_vmem] * 12,
        out_specs=[in_vmem, anywhere, anywhere] + [in_vmem] * 16,
        scratch_shapes=scratch,
        compiler_params=pltpu.CompilerParams(
            collective_id=0, has_side_effects=True, vmem_limit_bytes=VMEM_LIMIT
        ),
        name="block_forward",
    )(x, cotangent, level, table, w_ada, biases, w_qkv, w_out, w_up, w_down, cosine, sine)


def rope_tables(head_dim):
    places = lax.axis_index("seq") * PATCHES + jnp.arange(PATCHES, dtype=jnp.int32)
    cosine, sine = angle_table(places, head_dim)
    lane = jnp.arange(head_dim)
    first = jnp.where(lane < 16, lane < 8, (lane - 16) % 24 < 12)
    sine = jnp.where(first, -sine, sine)
    return jnp.tile(cosine, (1, 2)), jnp.tile(sine, (1, 2))


def own_biases(shares):
    device = lax.axis_index("dp") * 8 + lax.axis_index("seq")
    parts = []
    for share in shares:
        whole = jnp.zeros((32,) + share.shape, BF16)
        parts.append(lax.dynamic_update_slice(whole, low(share)[None], (device, 0)).reshape(-1))
    lines = jnp.concatenate(parts).reshape(-1, 128)
    return jnp.pad(lines, ((0, 128 - lines.shape[0]), (0, 0)))


SLOTS = 5


class Scatter:
    def __init__(self, wire, place, index, terms, buffers, credit, finish):
        self.wire, self.place, self.index, self.terms = wire, place, index, terms
        from_core, from_far, from_xy, from_z = buffers
        self.from_core = from_core.at[index % SLOTS]
        self.from_far = from_far.at[index]
        self.from_xy = from_xy.at[index]
        self.from_z = from_z.at[index]
        self.credit, self.finish = credit, finish
        self.mine = []

    def send(self, source, target, device):
        copy = self.wire.send(source, target, device)
        self.mine.append(copy)
        return copy

    def to_sibling(self):
        place = self.place
        if self.index >= SLOTS:
            pl.semaphore_wait(self.credit, 1)
        self.coming = [
            self.send(self.terms.at[:, :, place.other], self.from_core, place.sibling)
        ]

    def across(self, last):
        place, terms, core = self.place, self.terms, self.place.core
        arrive(self.coming)
        far = place.far_dp
        terms[far, :, core] = terms[far, :, core] + self.from_core[far]
        self.coming = [
            self.send(
                terms.at[far, pl.ds(0, 2), core], self.from_far.at[0], place.at_dp(place.x_dp)
            ),
            self.send(
                terms.at[far, pl.ds(2, 2), core], self.from_far.at[1], place.at_dp(place.y_dp)
            ),
        ]
        for group in (place.x_dp, place.y_dp, place.dp):
            terms[group, :, core] = terms[group, :, core] + self.from_core[group]
        if not last:
            pl.semaphore_signal(
                self.credit, inc=1, device_id=place.sibling, device_id_type=MESH_ID
            )

    def along_xy(self):
        place, terms, core = self.place, self.terms, self.place.core
        arrive(self.coming)
        first, second = pl.ds(0, 2), pl.ds(2, 2)
        terms[place.y_dp, first, core] = terms[place.y_dp, first, core] + self.from_far[0]
        terms[place.x_dp, second, core] = terms[place.x_dp, second, core] + self.from_far[1]
        self.coming = [
            self.send(terms.at[dp, :, core], self.from_xy.at[slot], place.at_dp(dp))
            for slot, dp in enumerate((place.x_dp, place.y_dp))
        ]

    def along_z(self):
        place, terms, core = self.place, self.terms, self.place.core
        arrive(self.coming)
        own = terms[place.dp, :, core].astype(F32)
        terms[place.dp, :, core] = low(total_of(own, self.from_xy, 2))
        self.coming = []
        for step in (1, 2, 3):
            z = (place.z + step) % 4
            self.coming.append(
                self.send(
                    terms.at[place.dp, z, core],
                    self.from_z.at[step - 1],
                    place.at_seq(z * 2 + core),
                )
            )

    def end(self):
        place = self.place
        arrive(self.coming)
        own = self.terms[place.dp, place.z, place.core].astype(F32)
        self.finish(total_of(own, self.from_z, 3))
        for copy in self.mine:
            copy.wait_send()
        self.wire.sent = [
            copy for copy in self.wire.sent if not any(copy is done for done in self.mine)
        ]


def norm_back(normed, inverse, grad):
    mean = jnp.mean(grad, axis=1, keepdims=True)
    along = jnp.mean(grad * normed, axis=1, keepdims=True)
    return (grad - mean - normed * along) * inverse


def column_sum(values):
    return jnp.sum(values, axis=0, keepdims=True)


def attend_frame_back(frame, heads, attended, log_total, grad_heads, sums, outs):
    query, keys, values = heads
    keys_sum, values_sum = sums
    query_out, keys_out, values_out = outs
    pair = split_heads(query[frame])
    grad_pair = split_heads(grad_heads[frame])
    product = attended[frame].astype(F32) * grad_heads[frame].astype(F32)
    lane = lax.broadcasted_iota(jnp.int32, (8, 128), 1)
    line = lax.broadcasted_iota(jnp.int32, (8, 128), 0)
    picked = jnp.where(lane // 64 == line, 1.0, 0.0).astype(F32)
    deltas = contract(picked, product, 1, 1, precision=lax.Precision.HIGHEST)
    delta = jnp.concatenate([deltas[0:1], deltas[1:2]], axis=1)
    total = log_total[frame]
    query_sum = None
    for block in range(frame + 1):
        weights = jnp.exp(contract(keys[block], pair, 1, 1) - total)
        grad_weights = contract(values[block], grad_pair, 1, 1)
        grad_scores = low(weights * (grad_weights - delta))
        keys_part = contract(grad_scores, pair, 1, 0)
        values_part = contract(low(weights), grad_pair, 1, 0)
        if frame == 7:
            keys_sum[block] = keys_part
            values_sum[block] = values_part
        else:
            keys_sum[block] += keys_part
            values_sum[block] += values_part
        query_part = contract(keys[block], grad_scores, 0, 0)
        query_sum = query_part if query_sum is None else query_sum + query_part
    query_out[frame] = low(join_heads(query_sum * 0.125))
    keys_out[frame] = low(keys_sum[frame])
    values_out[frame] = low(values_sum[frame])


def backward_kernel(
    x_ref,
    cotangent_ref,
    w_ada_ref,
    wide,
    down,
    query_ref,
    keys_ref,
    values_ref,
    attended_ref,
    log_total_ref,
    attended_tokens,
    normed_one_ref,
    normed_two_ref,
    middle_ref,
    branch_one_ref,
    act_in,
    slope_ref,
    modulation_ref,
    embedded_ref,
    one_hot_ref,
    gate_two_grad_ref,
    cosine_ref,
    sine_ref,
    grad_hidden_ref,
    grad_table_ref,
    grad_ada_ref,
    grad_ada_bias_ref,
    grad_qkv_ref,
    grad_out_ref,
    grad_up_ref,
    grad_down_ref,
    grad_bias_ref,
    terms,
    from_core,
    from_far,
    from_xy,
    from_z,
    hidden,
    down_block,
    wide_block,
    grad_two,
    grad_one,
    grad_tokens,
    grad_heads,
    keys_sum,
    values_sum,
    query_back,
    keys_back,
    values_back,
    qkv_back,
    running,
    bias_lines,
    bias_dp,
    bias_sum,
    bias_seq,
    mod_grads,
    mod_lines,
    embedded_grads,
    send_sems,
    recv_sems,
    back_send,
    back_recv,
    local_sems,
    credit,
):
    place = Place()
    wire = Wire(send_sems, recv_sems)
    dp, seq, core = place.dp, place.seq, place.core
    loads = {}

    def load(name, source, target, sem):
        copy = pltpu.make_async_copy(source, target, local_sems.at[sem])
        copy.start()
        loads[name] = copy

    def load_down(block):
        load(("down", block), down.at[:, block], down_block.at[block % 2], block % 2)

    def load_wide(block):
        load(("wide", block), wide.at[block], wide_block.at[block % 2], 2 + block % 2)

    load("act", act_in, hidden, 4)
    load_down(0)
    load_down(1)
    load_wide(4)
    load_wide(5)
    place.greet()
    shift_one = modulation_ref[0:1, :]
    scale_one = modulation_ref[1:2, :]
    gate_one = modulation_ref[2:3, :]
    scale_two = modulation_ref[4:5, :]
    gate_two = modulation_ref[5:6, :]
    cotangent = cotangent_ref[...].astype(F32)
    grad_two[...] = low(cotangent * gate_two)

    def keep_bias(first, grad):
        bias_lines[first : first + 8, :] = lines_of(column_sum(grad.astype(F32)))

    keep_bias(64, grad_two[...])

    def finish(index):
        def store(total):
            if index < 4:
                grad_down_ref[32 * index : 32 * (index + 1), :] = total
            elif index < 8:
                grad_up_ref[:, 1024 * (index - 4) : 1024 * (index - 3)] = total
            elif index == 8:
                grad_out_ref[...] = total
            else:
                grad_qkv_ref[:, 1024 * (index - 9) : 1024 * (index - 8)] = total

        return store

    buffers = (from_core, from_far, from_xy, from_z)
    pieces = [
        Scatter(wire, place, index, terms.at[index % SLOTS], buffers, credit, finish(index))
        for index in range(12)
    ]
    loads["act"].wait()
    for chunk in range(16):
        part = low(contract(hidden[:, 256 * chunk : 256 * (chunk + 1)], grad_two[...], 0, 0))
        part = part.reshape(2, 4, 32, 1024)
        for index in range(4):
            terms[index, chunk // 4, chunk % 4] = part[:, index]

    def make_terms(index):
        if index < 4:
            return
        for group in range(4):
            rows = slice(256 * group, 256 * (group + 1))
            if index < 8:
                left = normed_two_ref[:, rows]
                right = hidden[:, 1024 * (index - 4) : 1024 * (index - 3)]
            elif index == 8:
                left, right = attended_tokens[:, rows], grad_one[...]
            else:
                left, right = normed_one_ref[:, rows], qkv_back[index - 9]
            part = low(contract(left, right, 0, 0))
            terms[index % SLOTS, group] = part.reshape(4, 2, 32, 1024)

    def tick(step):
        if 0 <= step - 1 < 12:
            pieces[step - 1].across(step - 1 + SLOTS >= 12)
        if 0 <= step - 3 < 12:
            pieces[step - 3].along_z()
        if 0 <= step - 2 < 12:
            pieces[step - 2].along_xy()
        if step < 12:
            make_terms(step)
            pieces[step].to_sibling()
        if 0 <= step - 4 < 12:
            pieces[step - 4].end()

    tick(0)
    tick(1)
    for block in range(4):
        loads[("down", block)].wait()
        grad_act = None
        for index in range(4):
            weight = down_block[block % 2, index].reshape(1024, 256)
            part = contract(grad_two[:, 256 * index : 256 * (index + 1)], weight, 1, 1)
            grad_act = part if grad_act is None else grad_act + part
        if block < 2:
            load_down(block + 2)
        columns = slice(1024 * block, 1024 * (block + 1))
        grad_pre = low(grad_act * slope_ref[:, columns].astype(F32))
        hidden[:, columns] = grad_pre
        keep_bias(32 + 8 * block, grad_pre)
        loads[("wide", 4 + block)].wait()
        part = contract(grad_pre, whole_piece(wide_block.at[block % 2]), 1, 1)
        running[...] = part if block == 0 else running[...] + part
        load_wide((6, 7, 2, 3)[block])
    tick(2)
    normed, inverse = norm_parts(middle_ref[...])
    grad_normed = running[...]
    grad_shift_two = column_sum(grad_normed)
    grad_scale_two = column_sum(grad_normed * normed)
    grad_middle = cotangent_ref[...].astype(F32) + norm_back(
        normed, inverse, grad_normed * (1.0 + scale_two)
    )
    running[...] = grad_middle
    grad_gate_one = column_sum(grad_middle * branch_one_ref[...])
    grad_one[...] = low(grad_middle * gate_one)
    keep_bias(24, grad_one[...])
    loads[("wide", 3)].wait()
    grad_tokens[...] = low(contract(grad_one[...], whole_piece(wide_block.at[1]), 1, 1))
    load_wide(1)
    head_copies = []
    for other in place.seq_peers:
        columns = pl.ds(pl.multiple_of(other * 128, 128), 128)
        head_copies.append(
            wire.send(grad_tokens.at[:, columns], grad_heads.at[seq], place.at_seq(other))
        )
    own_columns = pl.ds(pl.multiple_of(seq * 128, 128), 128)
    grad_heads[seq] = grad_tokens[:, own_columns]
    tick(3)
    arrive(head_copies)
    backs = (query_back, keys_back, values_back)

    def back_copy(part, frame, source):
        columns = pl.ds(pl.multiple_of(source * 128, 128), 128)
        return pltpu.make_async_remote_copy(
            src_ref=backs[part].at[frame],
            dst_ref=qkv_back.at[part, :, columns],
            send_sem=back_send.at[part, frame],
            recv_sem=back_recv.at[part, source],
            device_id=place.at_seq(frame),
            device_id_type=MESH_ID,
        )

    def send_back(frame):
        @pl.when(seq != frame)
        def _():
            for part in range(3):
                back_copy(part, frame, seq).start()

        @pl.when(seq == frame)
        def _():
            for part in range(3):
                qkv_back[part, :, own_columns] = backs[part][frame]

    for frame in range(7, -1, -1):
        attend_frame_back(
            frame,
            (query_ref, keys_ref, values_ref),
            attended_ref,
            log_total_ref,
            grad_heads,
            (keys_sum, values_sum),
            backs,
        )
        send_back(frame)
        if frame in (6, 3):
            tick(4 if frame == 6 else 5)
    tick(6)
    tick(7)
    tick(8)
    for part in range(3):
        for other in place.seq_peers:
            back_copy(part, other, other).wait_recv()
    cosine, sine = cosine_ref[...], sine_ref[...]
    grad_normed = None
    for part in range(3):
        if part < 2:
            for group in range(8):
                columns = slice(128 * group, 128 * (group + 1))
                grad = qkv_back[part, :, columns].astype(F32)
                qkv_back[part, :, columns] = low(grad * cosine - half_turn(grad) * sine)
        keep_bias(8 * part, qkv_back[part])
        index = (2, 1, 0)[part]
    for block, slot in ((2, 0), (1, 1), (0, 0)):
        loads[("wide", block)].wait()
        part = contract(qkv_back[block], whole_piece(wide_block.at[slot]), 1, 1)
        grad_normed = part if grad_normed is None else grad_normed + part
        if block == 2:
            load_wide(0)
    bias_copies = spread_dp(wire, place, lambda dp: bias_lines, bias_dp)
    normed, inverse = norm_parts(x_ref[...].astype(F32))
    grad_shift_one = column_sum(grad_normed)
    grad_scale_one = column_sum(grad_normed * normed)
    grad_hidden_ref[...] = low(
        running[...] + norm_back(normed, inverse, grad_normed * (1.0 + scale_one))
    )
    rows = (
        grad_shift_one,
        grad_scale_one,
        grad_gate_one,
        grad_shift_two,
        grad_scale_two,
        gate_two_grad_ref[...],
    )
    mod_grads[dp, seq] = low(jnp.concatenate([lines_of(row) for row in rows], axis=0))
    mod_gather = SmallGather(wire, place, mod_grads)
    mod_gather.along_seq()
    tick(9)
    mod_gather.along_dp()
    arrive(bias_copies)
    bias_sum[...] = total_of(bias_lines[...], bias_dp, 3)
    bias_copies = spread_seq(wire, place, lambda seq: bias_sum, bias_seq)
    tick(10)
    mod_gather.finish()
    lines = mod_grads[...].astype(F32).reshape(1536, 128)
    mod_lines[...] = lines
    grad_ada_bias_ref[...] = jnp.sum(lines.reshape(32, 48, 128), axis=0)
    embedded = embedded_ref[...]
    share = 1.0 / (1.0 + jnp.exp(-embedded))
    silu_in = low(embedded * share)[:, :32]
    empty = jnp.zeros((96, 128), BF16)
    grad_silu = None
    for block in range(6):
        parts = []
        for line in range(8):
            part = mod_lines[pl.ds(8 * block + line, 32, stride=48), :]
            parts.append(jnp.concatenate([low(part), empty], axis=0))
        every = jnp.concatenate(parts, axis=1)
        columns = slice(1024 * block, 1024 * (block + 1))
        grad_ada_ref[:, columns] = contract(silu_in, every[:32], 1, 0)
        part = contract(low(w_ada_ref[:, columns]), every, 1, 1)
        grad_silu = part if grad_silu is None else grad_silu + part
    embedded_grads[dp, seq] = grad_silu * share * (1.0 + embedded * (1.0 - share))
    embedded_gather = SmallGather(wire, place, embedded_grads)
    embedded_gather.along_seq()
    tick(11)
    embedded_gather.along_dp()
    tick(12)
    arrive(bias_copies)
    grad_bias_ref[...] = total_of(bias_sum[...], bias_seq, 7)
    tick(13)
    embedded_gather.finish()
    grad_table_ref[...] = contract(
        one_hot_ref[...],
        embedded_grads[...].reshape(1024, 128),
        0,
        1,
        precision=lax.Precision.HIGHEST,
    )[:32]
    tick(14)
    tick(15)
    for part in range(3):
        for other in place.seq_peers:
            back_copy(part, other, other).wait_send()
    wire.drain()


def run_backward(
    x, cotangent, w_ada, wide, down, heads, attended_tokens, tokens, act, slope, small, cosine, sine
):
    shape = jax.ShapeDtypeStruct
    outs = [
        ((256, 1024), BF16),
        ((32, 1024), F32),
        ((32, 6144), F32),
        ((48, 128), F32),
        ((32, 3072), F32),
        ((32, 1024), F32),
        ((32, 4096), F32),
        ((128, 1024), F32),
        ((72, 128), F32),
    ]
    in_vmem = pl.BlockSpec(memory_space=pltpu.VMEM)
    anywhere = pl.BlockSpec(memory_space=pl.ANY)
    scratch = [
        vmem((SLOTS, 4, 4, 2, 32, 1024), BF16),
        vmem((SLOTS, 4, 4, 32, 1024), BF16),
        vmem((12, 2, 2, 32, 1024), BF16),
        vmem((12, 2, 4, 32, 1024), BF16),
        vmem((12, 3, 32, 1024), BF16),
        vmem((256, 4096), BF16),
        vmem((2, 4, 4, 2, 128, 256), BF16),
        vmem((2, 4, 4, 2, 32, 1024), BF16),
        vmem((256, 1024), BF16),
        vmem((256, 1024), BF16),
        vmem((256, 1024), BF16),
        vmem((8, 256, 128), BF16),
        vmem((8, 256, 128)),
        vmem((8, 256, 128)),
        vmem((8, 256, 128), BF16),
        vmem((8, 256, 128), BF16),
        vmem((8, 256, 128), BF16),
        vmem((3, 256, 1024), BF16),
        vmem((256, 1024)),
        vmem((72, 128)),
        vmem((3, 72, 128)),
        vmem((72, 128)),
        vmem((7, 72, 128)),
        vmem((4, 8, 48, 128), BF16),
        vmem((1536, 128)),
        vmem((4, 8, 32, 128)),
        pltpu.SemaphoreType.DMA((150,)),
        pltpu.SemaphoreType.DMA((150,)),
        pltpu.SemaphoreType.DMA((3, 8)),
        pltpu.SemaphoreType.DMA((3, 8)),
        pltpu.SemaphoreType.DMA((5,)),
        pltpu.SemaphoreType.REGULAR,
    ]
    return pl.pallas_call(
        backward_kernel,
        out_shape=[shape(*out) for out in outs],
        in_specs=[in_vmem] * 3 + [anywhere] * 2 + [in_vmem] * 10 + [anywhere] + [in_vmem] * 7,
        out_specs=[in_vmem] * 9,
        scratch_shapes=scratch,
        compiler_params=pltpu.CompilerParams(
            collective_id=1, has_side_effects=True, vmem_limit_bytes=VMEM_LIMIT
        ),
        name="block_backward",
    )(
        x,
        cotangent,
        w_ada,
        wide,
        down,
        *heads,
        attended_tokens,
        *tokens,
        act,
        slope,
        *small,
        cosine,
        sine,
    )


def own_share(lines, first, share):
    device = lax.axis_index("dp") * 8 + lax.axis_index("seq")
    return lax.dynamic_slice(lines.reshape(-1), (first * 128 + device * share,), (share,))


def fast_body(
    hidden_in,
    noise_level,
    noise_table,
    w_ada,
    b_ada,
    w_qkv,
    b_qkv,
    w_out,
    b_out,
    w_up,
    b_up,
    w_down,
    b_down,
    grad_out,
):
    cosine, sine = rope_tables(64)
    level = jnp.broadcast_to(noise_level.astype(F32), (8, 128))
    biases = own_biases((b_qkv, b_out, b_up, b_down, b_ada))
    (
        layer_out,
        wide,
        down,
        query,
        keys,
        values,
        attended,
        log_total,
        attended_tokens,
        normed_one,
        normed_two,
        middle,
        branch_one,
        act,
        slope,
        modulation,
        embedded,
        one_hot,
        grad_gate_two,
    ) = run_forward(
        hidden_in[0],
        grad_out[0],
        level,
        noise_table,
        w_ada,
        biases,
        w_qkv,
        w_out,
        w_up,
        w_down,
        cosine,
        sine,
    )
    (
        grad_hidden,
        grad_table,
        grad_ada_w,
        grad_ada_lines,
        grad_qkv_w,
        grad_out_w,
        grad_up_w,
        grad_down_w,
        grad_lines,
    ) = run_backward(
        hidden_in[0],
        grad_out[0],
        w_ada,
        wide,
        down,
        (query, keys, values, attended, log_total),
        attended_tokens,
        (normed_one, normed_two, middle, branch_one),
        act,
        slope,
        (modulation, embedded, one_hot, grad_gate_two),
        cosine,
        sine,
    )
    return (
        layer_out[None],
        grad_hidden[None],
        grad_table,
        grad_ada_w,
        own_share(grad_ada_lines, 0, 192),
        grad_qkv_w,
        own_share(grad_lines, 0, 96),
        grad_out_w,
        own_share(grad_lines, 24, 32),
        grad_up_w,
        own_share(grad_lines, 32, 128),
        grad_down_w,
        own_share(grad_lines, 64, 32),
    )


def solution(mesh):
    tokens = P("dp", "seq", None)
    matrix = P(ALL, None)
    vector = P(ALL)
    parameters = (matrix,) + (matrix, vector) * 5
    chips = dict(mesh.shape) == {"dp": 4, "seq": 8}
    return jax.shard_map(
        fast_body if chips else general_body,
        mesh=mesh,
        in_specs=(tokens, P("dp", "seq")) + parameters + (tokens,),
        out_specs=(tokens, tokens) + parameters,
        check_vma=False,
    )
```

```python
from functools import partial
import math

import jax
import jax.numpy as jnp
from jax import lax
from jax.experimental import pallas as pl
from jax.experimental.pallas import tpu as pltpu
from jax.sharding import PartitionSpec as P

H = 16
GRID_W = 16
PATCHES = 256


norm_eps = 1e-06
masked_score = -1e30
ALL = ("dp", "seq")
F32 = jnp.float32
BF16 = jnp.bfloat16


def layer_norm(values):
    centred = values - jnp.mean(values, axis=-1, keepdims=True)
    spread = jnp.mean(centred * centred, axis=-1, keepdims=True)
    return centred * lax.rsqrt(spread + norm_eps)


def modulate(values, shift_term, scale_term):
    return layer_norm(values) * (1.0 + scale_term) + shift_term


def turn_half(values):
    extent = values.shape[-1]
    side_part = 2 * (3 * extent // 16)
    pieces = []
    offset = 0
    for part_size in (extent - 2 * side_part, side_part, side_part):
        half_size = part_size // 2
        pieces.append(-values[..., offset + half_size : offset + part_size])
        pieces.append(values[..., offset : offset + half_size])
        offset = offset + part_size
    return jnp.concatenate(pieces, axis=-1)


def part_angles(places, part_size):
    half_size = part_size // 2
    rates = jnp.exp(-math.log(10000.0) * jnp.arange(half_size, dtype=F32) / half_size)
    angles = places.astype(F32)[:, None] * rates[None, :]
    return jnp.concatenate([angles, angles], axis=1)


def angle_table(places, extent):
    side_part = 2 * (3 * extent // 16)
    patch_index = places % PATCHES
    angles = jnp.concatenate(
        [
            part_angles(places // PATCHES, extent - 2 * side_part),
            part_angles(patch_index // GRID_W, side_part),
            part_angles(patch_index % GRID_W, side_part),
        ],
        axis=1,
    )
    return (jnp.cos(angles), jnp.sin(angles))


def rotate(values, cosine_table, sine_table):
    return values * cosine_table + turn_half(values) * sine_table


def unrotate(values, cosine_table, sine_table):
    return values * cosine_table - turn_half(values * sine_table)


def low(values):
    return values.astype(BF16)


def dot(left, right):
    return jnp.dot(left, right, preferred_element_type=F32)


def gather_rows(share):
    return lax.all_gather(low(share), ALL, axis=0, tiled=True)


def scatter_rows(whole):
    return lax.psum_scatter(whole, ALL, scatter_dimension=0, tiled=True)


def frame_modulation(noise_level, noise_table, w_ada, b_ada):
    levels = lax.all_gather(noise_level.reshape(-1), ALL, axis=0, tiled=True)
    device = lax.axis_index("dp") * lax.axis_size("seq") + lax.axis_index("seq")
    share = noise_table.shape[0]
    own_levels = device * share + jnp.arange(share, dtype=jnp.int32)
    one_hot = levels[:, None] == own_levels[None, :]
    found = dot(low(one_hot), low(noise_table))
    embedded = lax.psum_scatter(low(found), ALL, scatter_dimension=1, tiled=True).astype(F32)
    silu_in = low(jax.nn.silu(embedded))
    modulation = lax.psum_scatter(
        dot(silu_in, low(w_ada)), ALL, scatter_dimension=0, tiled=True
    ) + gather_rows(b_ada).astype(F32)
    return one_hot, embedded, silu_in, modulation


def frame_gradients(grad_modulation, one_hot, embedded, silu_in, w_ada):
    every = lax.all_gather(grad_modulation, ALL, axis=0, tiled=True)
    grad_ada_w = lax.dot_general(
        silu_in, every, (((0,), (0,)), ((), ())), preferred_element_type=F32
    )
    share = w_ada.shape[1] // lax.axis_size(ALL)
    device = lax.axis_index("dp") * lax.axis_size("seq") + lax.axis_index("seq")
    columns = lax.dynamic_slice_in_dim(every, device * share, share, axis=1)
    grad_ada_b = jnp.sum(columns.astype(F32), axis=0)
    grad_silu = lax.dot_general(
        every, low(w_ada), (((1,), (1,)), ((), ())), preferred_element_type=F32
    )
    unused, silu_back = jax.vjp(jax.nn.silu, embedded)
    grad_embedded = lax.all_gather(silu_back(grad_silu)[0], ALL, axis=1, tiled=True)
    grad_table = jnp.dot(
        one_hot.astype(F32).T, grad_embedded, precision=lax.Precision.HIGHEST
    )
    return grad_table, grad_ada_w, grad_ada_b


def to_heads(values):
    return lax.all_to_all(values, "seq", split_axis=2, concat_axis=1, tiled=True)


def to_tokens(values):
    return lax.all_to_all(values, "seq", split_axis=1, concat_axis=2, tiled=True)


def as_heads(values):
    return values.reshape(*values.shape[:2], -1, 64)


def query_blocks(array, axis):
    blocks = array.shape[axis] // PATCHES
    split = array.shape[:axis] + (blocks, PATCHES) + array.shape[axis + 1 :]
    return jnp.moveaxis(array.reshape(split), axis, 0)


def block_scores(query_block, keys, frame, score_scale):
    scores = (
        jnp.einsum("cqhd,ckhd->chqk", query_block, keys, preferred_element_type=F32) * score_scale
    )
    allowed = jnp.arange(keys.shape[1], dtype=jnp.int32) // PATCHES <= frame
    return jnp.where(allowed, scores, masked_score)


def attend(query, keys, values, score_scale):
    def one_block(block_in):
        query_block, frame = block_in
        scores = block_scores(query_block, keys, frame, score_scale)
        row_max = jnp.max(scores, axis=-1, keepdims=True)
        exponent = jnp.exp(scores - row_max)
        row_total = jnp.sum(exponent, axis=-1, keepdims=True)
        weighted = jnp.einsum(
            "chqk,ckhd->cqhd", low(exponent / row_total), values, preferred_element_type=F32
        )
        return low(weighted), (row_max + jnp.log(row_total))[..., 0]

    frames = jnp.arange(query.shape[1] // PATCHES, dtype=jnp.int32)
    attended, log_total = lax.map(one_block, (query_blocks(query, 1), frames))
    return (
        jnp.moveaxis(attended, 0, 1).reshape(query.shape),
        jnp.moveaxis(log_total, 0, 2).reshape(query.shape[0], query.shape[2], query.shape[1]),
    )


def attend_back(query, keys, values, grad_heads, log_total, row_delta, score_scale):
    def one_block(carried, block_in):
        query_block, grad_block, total_block, delta_block, frame = block_in
        scores = block_scores(query_block, keys, frame, score_scale)
        softmax_weights = jnp.exp(scores - total_block[..., None])
        grad_soft = jnp.einsum("cqhd,ckhd->chqk", grad_block, values, preferred_element_type=F32)
        grad_scores = low(softmax_weights * (grad_soft - delta_block[..., None]))
        query_grad = jnp.einsum("chqk,ckhd->cqhd", grad_scores, keys, preferred_element_type=F32)
        keys_grad = jnp.einsum(
            "chqk,cqhd->ckhd", grad_scores, query_block, preferred_element_type=F32
        )
        values_grad = jnp.einsum(
            "chqk,cqhd->ckhd", low(softmax_weights), grad_block, preferred_element_type=F32
        )
        return (carried[0] + keys_grad, carried[1] + values_grad), query_grad

    frames = jnp.arange(query.shape[1] // PATCHES, dtype=jnp.int32)
    empty = jnp.zeros(keys.shape, F32)
    (grad_keys, grad_values), grad_query = lax.scan(
        one_block,
        (empty, empty),
        (
            query_blocks(query, 1),
            query_blocks(grad_heads, 1),
            query_blocks(log_total, 2),
            query_blocks(row_delta, 2),
            frames,
        ),
    )
    grad_query = jnp.moveaxis(grad_query, 0, 1).reshape(query.shape)
    return grad_query * score_scale, grad_keys * score_scale, grad_values


def general_body(
    hidden_in,
    noise_level,
    noise_table,
    w_ada,
    b_ada,
    w_qkv,
    b_qkv,
    w_out,
    b_out,
    w_up,
    b_up,
    w_down,
    b_down,
    grad_out,
):
    qkv_w, qkv_b, out_w, out_b, up_w, up_b, down_w, down_b = [
        gather_rows(share)
        for share in (w_qkv, b_qkv, w_out, b_out, w_up, b_up, w_down, b_down)
    ]
    clip_count, patches, model_width = hidden_in.shape
    head_dim = model_width // H
    score_scale = 1.0 / math.sqrt(head_dim)
    head_shape = (clip_count, patches, H, head_dim)
    inputs = hidden_in.astype(F32)
    one_hot, embedded, silu_in, modulation = frame_modulation(
        noise_level, noise_table, w_ada, b_ada
    )
    shift_one, scale_one, gate_one, shift_two, scale_two, gate_two = [
        modulation[:, None, column_block * model_width : (column_block + 1) * model_width]
        for column_block in range(6)
    ]
    normed_one = low(modulate(inputs, shift_one, scale_one))
    qkv_all = dot(normed_one, qkv_w) + qkv_b.astype(F32)
    frame_own = lax.axis_index("seq")
    places = frame_own * patches + jnp.arange(patches, dtype=jnp.int32)
    cosine_local, sine_local = angle_table(places, head_dim)
    cosine_wide = cosine_local[None, :, None, :]
    sine_wide = sine_local[None, :, None, :]
    flat_shape = (clip_count, patches, model_width)

    def turned(block):
        part = qkv_all[..., block * model_width : (block + 1) * model_width]
        return low(rotate(part.reshape(head_shape), cosine_wide, sine_wide)).reshape(flat_shape)

    query = as_heads(to_heads(turned(0)))
    keys = as_heads(to_heads(turned(1)))
    values = as_heads(to_heads(low(qkv_all[..., 2 * model_width :])))
    attended, log_total = attend(query, keys, values, score_scale)
    attended_low = to_tokens(attended.reshape(*attended.shape[:2], -1))
    branch_one = dot(attended_low, out_w) + out_b.astype(F32)
    middle = inputs + gate_one * branch_one
    normed_two = low(modulate(middle, shift_two, scale_two))
    hidden_pre = dot(normed_two, up_w) + up_b.astype(F32)
    hidden_act = low(jax.nn.gelu(hidden_pre, approximate=True))
    branch_two = dot(hidden_act, down_w) + down_b.astype(F32)
    outputs = middle + gate_two * branch_two
    cotangent = grad_out.astype(F32)
    grad_gate_two = jnp.sum(cotangent * branch_two, axis=1)
    grad_branch_two = low(cotangent * gate_two)

    def weight_grad(left, right):
        whole = jnp.einsum("cpi,cpo->io", left, right, preferred_element_type=F32)
        return scatter_rows(low(whole)).astype(F32)

    def bias_grad(grad):
        return scatter_rows(jnp.sum(grad.astype(F32), axis=(0, 1)))

    def back_dot(grad, weight):
        return jnp.einsum("cpo,io->cpi", grad, weight, preferred_element_type=F32)

    grad_down_w = weight_grad(hidden_act, grad_branch_two)
    grad_down_b = bias_grad(grad_branch_two)
    grad_act = back_dot(grad_branch_two, down_w)
    unused, gelu_back = jax.vjp(partial(jax.nn.gelu, approximate=True), hidden_pre)
    grad_pre = low(gelu_back(grad_act)[0])
    grad_up_w = weight_grad(normed_two, grad_pre)
    grad_up_b = bias_grad(grad_pre)
    grad_normed_two = back_dot(grad_pre, up_w)
    unused, norm_two_back = jax.vjp(modulate, middle, shift_two, scale_two)
    grad_middle_norm, grad_shift_two, grad_scale_two = norm_two_back(grad_normed_two)
    grad_middle = cotangent + grad_middle_norm
    grad_gate_one = jnp.sum(grad_middle * branch_one, axis=1)
    grad_branch_one = low(grad_middle * gate_one)
    grad_out_w = weight_grad(attended_low, grad_branch_one)
    grad_out_b = bias_grad(grad_branch_one)
    grad_attended = low(back_dot(grad_branch_one, out_w))
    grad_heads = as_heads(to_heads(grad_attended))
    row_delta = jnp.sum(grad_heads.astype(F32) * attended.astype(F32), axis=-1).transpose(0, 2, 1)
    grad_query, grad_keys, grad_values = attend_back(
        query, keys, values, grad_heads, log_total, row_delta, score_scale
    )

    def home(grad):
        return to_tokens(low(grad).reshape(*grad.shape[:2], -1))

    def unturned(grad):
        wide = home(grad).astype(F32).reshape(head_shape)
        return low(unrotate(wide, cosine_wide, sine_wide)).reshape(flat_shape)

    grad_qkv = jnp.concatenate(
        [unturned(grad_query), unturned(grad_keys), home(grad_values)], axis=-1
    )
    grad_qkv_w = weight_grad(normed_one, grad_qkv)
    grad_qkv_b = bias_grad(grad_qkv)
    grad_normed_one = back_dot(grad_qkv, qkv_w)
    unused, norm_one_back = jax.vjp(modulate, inputs, shift_one, scale_one)
    grad_input_norm, grad_shift_one, grad_scale_one = norm_one_back(grad_normed_one)
    grad_input = grad_middle + grad_input_norm
    grad_modulation = low(
        jnp.concatenate(
            [
                grad_shift_one[:, 0],
                grad_scale_one[:, 0],
                grad_gate_one,
                grad_shift_two[:, 0],
                grad_scale_two[:, 0],
                grad_gate_two,
            ],
            axis=-1,
        )
    )
    grad_table, grad_ada_w, grad_ada_b = frame_gradients(
        grad_modulation, one_hot, embedded, silu_in, w_ada
    )
    return (
        low(outputs),
        low(grad_input),
        grad_table,
        grad_ada_w,
        grad_ada_b,
        grad_qkv_w,
        grad_qkv_b,
        grad_out_w,
        grad_out_b,
        grad_up_w,
        grad_up_b,
        grad_down_w,
        grad_down_b,
    )


MESH_ID = pl.DeviceIdType.MESH
VMEM_LIMIT = 63 * 1024 * 1024
HEADS_WIDE = 128


def contract(left, right, left_dim, right_dim, precision=None):
    return lax.dot_general(
        left,
        right,
        (((left_dim,), (right_dim,)), ((), ())),
        preferred_element_type=F32,
        precision=precision,
    )


class Place:
    def __init__(self):
        self.dp = lax.axis_index("dp")
        self.seq = lax.axis_index("seq")
        self.z = self.seq // 2
        self.core = self.seq % 2
        self.other = 1 - self.core
        self.x_dp = self.dp + 1 - 2 * (self.dp % 2)
        self.y_dp = (self.dp + 2) % 4
        self.far_dp = 3 - self.dp
        self.dp_peers = (self.x_dp, self.y_dp, self.far_dp)
        self.seq_peers = [(self.seq + step) % 8 for step in range(1, 8)]
        self.sibling = (self.dp, self.z * 2 + self.other)

    def at_dp(self, dp):
        return (dp, self.seq)

    def at_seq(self, seq):
        return (self.dp, seq)

    def at_z(self, step):
        return (self.dp, ((self.z + step) % 4) * 2 + self.core)

    def greet(self):
        barrier = pltpu.get_barrier_semaphore()
        peers = [self.at_dp(dp) for dp in self.dp_peers]
        peers += [self.at_seq(seq) for seq in self.seq_peers]
        for peer in peers:
            pl.semaphore_signal(barrier, inc=1, device_id=peer, device_id_type=MESH_ID)
        pl.semaphore_wait(barrier, len(peers))


def guarded(only, act):
    if only is None:
        act()
    else:
        pl.when(only)(act)


class Copy:
    def __init__(self, wire, source, target, device, only, landing):
        self.only = only
        self.index = wire.used
        wire.used += 1
        self.copy = pltpu.make_async_remote_copy(
            src_ref=source,
            dst_ref=target,
            send_sem=wire.send_sems.at[self.index],
            recv_sem=wire.recv_sems.at[self.index if landing is None else landing.index],
            device_id=device,
            device_id_type=MESH_ID,
        )
        guarded(only, self.copy.start)

    def wait_send(self):
        guarded(self.only, self.copy.wait_send)

    def wait_recv(self):
        self.copy.wait_recv()


class Wire:
    def __init__(self, send_sems, recv_sems):
        self.send_sems = send_sems
        self.recv_sems = recv_sems
        self.used = 0
        self.sent = []

    def send(self, source, target, device, only=None, landing=None):
        copy = Copy(self, source, target, device, only, landing)
        self.sent.append(copy)
        return copy

    def drain(self, copies=None):
        copies = list(self.sent if copies is None else copies)
        for copy in copies:
            copy.wait_send()
        self.sent = [copy for copy in self.sent if not any(copy is done for done in copies)]


class Local:
    def __init__(self, sems):
        self.sems = sems
        self.used = 0

    def start(self, source, target):
        copy = pltpu.make_async_copy(source, target, self.sems.at[self.used])
        self.used += 1
        copy.start()
        return copy


def arrive(copies):
    for copy in copies:
        copy.wait_recv()


class Gather:
    def __init__(self, wire, place, ref):
        self.wire, self.place, self.ref = wire, place, ref
        self.early = []

    def along_z(self):
        place, ref = self.place, self.ref
        own = ref.at[place.dp, place.z, place.core]
        self.from_z = [
            self.wire.send(own, own, place.at_z(step), only)
            for step, only in ((1, place.z != 3), (2, None), (3, place.z != 0))
        ]

    def pass_z(self):
        place, ref = self.place, self.ref
        up, two, down = self.from_z
        arrive([two])
        first, last = ref.at[place.dp, 0, place.core], ref.at[place.dp, 3, place.core]
        self.wire.send(last, last, place.at_z(3), place.z == 1, landing=up)
        self.wire.send(first, first, place.at_z(1), place.z == 2, landing=down)
        self.coming = [up, down]

    def own_xy(self):
        place = self.place
        own = self.ref.at[place.dp, place.z, place.core]
        self.early = [
            self.wire.send(own, own, place.at_dp(dp)) for dp in (place.x_dp, place.y_dp)
        ]

    def along_xy(self):
        place = self.place
        if self.early:
            coming = list(self.early)
            for step, copy in ((2, None), (3, self.coming[0]), (1, self.coming[1])):
                if copy is not None:
                    arrive([copy])
                part = self.ref.at[place.dp, (place.z + step) % 4, place.core]
                coming += [
                    self.wire.send(part, part, place.at_dp(dp)) for dp in (place.x_dp, place.y_dp)
                ]
            self.coming = coming
            return
        arrive(self.coming)
        own = self.ref.at[place.dp, :, place.core]
        self.coming = [
            self.wire.send(own, own, place.at_dp(dp)) for dp in (place.x_dp, place.y_dp)
        ]

    def across(self):
        place = self.place
        arrive(self.coming)
        from_x = self.ref.at[place.x_dp, pl.ds(0, 2), place.core]
        from_y = self.ref.at[place.y_dp, pl.ds(2, 2), place.core]
        self.coming = [
            self.wire.send(from_x, from_x, place.at_dp(place.y_dp)),
            self.wire.send(from_y, from_y, place.at_dp(place.x_dp)),
        ]

    def to_sibling(self):
        place = self.place
        arrive(self.coming)
        mine = self.ref.at[:, :, place.core]
        self.coming = [self.wire.send(mine, mine, place.sibling)]

    def finish(self):
        arrive(self.coming)


class SmallGather:
    def __init__(self, wire, place, ref):
        self.wire, self.place, self.ref = wire, place, ref

    def along_seq(self):
        place = self.place
        own = self.ref.at[place.dp, place.seq]
        self.coming = [self.wire.send(own, own, place.at_seq(seq)) for seq in place.seq_peers]

    def along_dp(self):
        place = self.place
        arrive(self.coming)
        own = self.ref.at[place.dp]
        self.coming = [self.wire.send(own, own, place.at_dp(dp)) for dp in place.dp_peers]

    def finish(self):
        arrive(self.coming)


def spread_dp(wire, place, part_of, slots):
    return [
        wire.send(part_of(dp), slots.at[index], place.at_dp(dp))
        for index, dp in enumerate(place.dp_peers)
    ]


def spread_seq(wire, place, part_of, slots):
    return [
        wire.send(part_of(seq), slots.at[index], place.at_seq(seq))
        for index, seq in enumerate(place.seq_peers)
    ]


def total_of(own, slots, count):
    total = own
    for index in range(count):
        total = total + slots[index].astype(F32)
    return total


def row_of(lines, first):
    return jnp.concatenate([lines[first + line : first + line + 1, :] for line in range(8)], axis=1)


def lines_of(row):
    return jnp.concatenate([row[:, 128 * line : 128 * (line + 1)] for line in range(8)], axis=0)


def whole_piece(piece):
    value = piece[...]
    return value.reshape(-1, value.shape[-1])


def norm_parts(values):
    centred = values - jnp.mean(values, axis=1, keepdims=True)
    inverse = lax.rsqrt(jnp.mean(centred * centred, axis=1, keepdims=True) + norm_eps)
    return centred * inverse, inverse


def half_turn(values):
    lane = lax.broadcasted_iota(jnp.int32, values.shape, 1) % 64
    in_time = lane < 16
    first = (lane < 8) | ((lane >= 16) & (lane < 28)) | ((lane >= 40) & (lane < 52))
    up = jnp.where(in_time, pltpu.roll(values, 120, 1), pltpu.roll(values, 116, 1))
    down = jnp.where(in_time, pltpu.roll(values, 8, 1), pltpu.roll(values, 12, 1))
    return jnp.where(first, up, down)


def split_heads(values):
    lane = lax.broadcasted_iota(jnp.int32, values.shape, 1)
    empty = jnp.zeros_like(values)
    return jnp.concatenate(
        [jnp.where(lane < 64, values, empty), jnp.where(lane < 64, empty, values)], axis=0
    )


def join_heads(turned):
    return jnp.concatenate([turned[:64, :256], turned[64:, 256:]], axis=0).T


def attend_frame(frame, query, keys, values, attended, log_total, scores):
    pair = split_heads(query[frame])
    row_max = None
    for block in range(frame + 1):
        block_scores = contract(keys[block], pair, 1, 1)
        scores[block] = block_scores
        block_max = jnp.max(block_scores, axis=0, keepdims=True)
        row_max = block_max if row_max is None else jnp.maximum(row_max, block_max)
    row_total = None
    weighted = None
    for block in range(frame + 1):
        exponent = jnp.exp(scores[block] - row_max)
        block_total = jnp.sum(exponent, axis=0, keepdims=True)
        block_sum = contract(values[block], exponent.astype(BF16), 0, 0)
        row_total = block_total if row_total is None else row_total + block_total
        weighted = block_sum if weighted is None else weighted + block_sum
    attended[frame] = join_heads(weighted / row_total).astype(BF16)
    log_total[frame] = row_max + jnp.log(row_total)


SQRT_TWO_OVER_PI = math.sqrt(2.0 / math.pi)


def gelu_parts(values):
    square = values * values
    bent = jnp.tanh(SQRT_TWO_OVER_PI * values * (1.0 + 0.044715 * square))
    half = 0.5 * (1.0 + bent)
    slope = half + 0.5 * values * (1.0 - bent * bent) * (
        SQRT_TWO_OVER_PI * (1.0 + 3.0 * 0.044715 * square)
    )
    return values * half, slope


def rope_in_kernel(frame):
    lane = lax.broadcasted_iota(jnp.int32, (256, 128), 1) % 64
    patch = lax.broadcasted_iota(jnp.int32, (256, 128), 0)
    in_time, in_rows = lane < 16, lane < 40
    half = jnp.where(in_time, 8, 12)
    step = jnp.where(in_time, lane, jnp.where(in_rows, lane - 16, lane - 40))
    second = step >= half
    step = jnp.where(second, step - half, step).astype(F32)
    position = jnp.where(in_time, frame, jnp.where(in_rows, patch // GRID_W, patch % GRID_W))
    rate = jnp.exp(-math.log(10000.0) * step / half.astype(F32))
    angle = position.astype(F32) * rate
    sine = jnp.sin(angle)
    return jnp.cos(angle), jnp.where(second, sine, -sine)


BIAS_FIRST = (0, 24, 32, 64, 72)
BIAS_SHARE = (96, 32, 128, 32, 192)


def every_bias(blocks, lines):
    lane = lax.broadcasted_iota(jnp.int32, (8, 128), 1)

    def take(line, first, every):
        return blocks[pl.ds(8 * first + line, 32 // every, stride=8 * every), :]

    def moved(values, lanes):
        return pltpu.roll(values, lanes % 128, 1)

    mixed = [take(2, first, 4) for first in range(4)]
    lines[pl.ds(0, 8, stride=3), :] = jnp.where(lane < 96, mixed[0], moved(mixed[1], 96))
    lines[pl.ds(1, 8, stride=3), :] = jnp.where(lane < 64, moved(mixed[1], 96), moved(mixed[2], 64))
    lines[pl.ds(2, 8, stride=3), :] = jnp.where(lane < 32, moved(mixed[2], 64), moved(mixed[3], 32))

    def quarters(parts, first_lane):
        total = jnp.zeros((8, 128), F32)
        for index, part in enumerate(parts):
            here = (lane >= 32 * index) & (lane < 32 * (index + 1))
            total = jnp.where(here, moved(part, 32 * index - first_lane), total)
        return total

    lines[24:32, :] = quarters(mixed, 96)
    lines[32:64, :] = take(1, 0, 1)
    lines[64:72, :] = quarters([take(4, first, 4) for first in range(4)], 64)
    left = lax.broadcasted_iota(jnp.int32, (16, 128), 1) < 64
    even, odd = take(3, 0, 2), take(3, 1, 2)
    even_rest, odd_rest = take(4, 0, 2), take(4, 1, 2)
    lines[pl.ds(72, 16, stride=3), :] = even
    lines[pl.ds(73, 16, stride=3), :] = jnp.where(left, even_rest, moved(odd, 64))
    lines[pl.ds(74, 16, stride=3), :] = jnp.where(left, moved(odd, 64), moved(odd_rest, 64))


def pack_lanes(rows):
    packed = rows[:, 0]
    for part in range(1, 4):
        packed = packed + pltpu.roll(rows[:, part], 32 * part, 2)
    return packed


def unpack_lanes(packed):
    lane = lax.broadcasted_iota(jnp.int32, packed.shape, packed.ndim - 1)
    parts = [packed] + [pltpu.roll(packed, 128 - 32 * part, 1) for part in range(1, 4)]
    return jnp.concatenate([jnp.where(lane < 32, part, 0.0) for part in parts], axis=0)


def forward_kernel(
    x_ref,
    level_ref,
    table_ref,
    b_qkv_ref,
    b_out_ref,
    b_up_ref,
    b_down_ref,
    b_ada_ref,
    w_qkv_ref,
    w_out_in,
    w_up_in,
    w_down_in,
    w_ada_in,
    cotangent_in,
    layer_out_ref,
    log_total_ref,
    modulation_ref,
    embedded_ref,
    one_hot_ref,
    gate_two_grad_ref,
    wide_out,
    down_out,
    query_out,
    keys_out,
    values_out,
    attended_out,
    tokens_out,
    normed_one_out,
    normed_two_out,
    middle_out,
    branch_one_out,
    act_out,
    slope_out,
    cosine_out,
    sine_out,
    query_ref,
    keys_ref,
    values_ref,
    attended_ref,
    attended_tokens,
    normed_one_ref,
    normed_two_ref,
    middle_ref,
    branch_one_ref,
    act_ref,
    slope_ref,
    cosine_ref,
    sine_ref,
    w_out_ref,
    w_up_ref,
    w_down_ref,
    w_ada_ref,
    cotangent_ref,
    wide,
    down,
    levels,
    found,
    found_dp,
    found_sum,
    found_seq,
    partial_mod,
    mod_dp,
    mod_sum,
    mod_blocks,
    mod_seq,
    bias_lines,
    blocks,
    own_block,
    flat,
    scores,
    send_sems,
    recv_sems,
    back_send,
    back_recv,
    local_sems,
):
    place = Place()
    wire = Wire(send_sems, recv_sems)
    dp, seq, z, core = place.dp, place.seq, place.z, place.core
    device = dp * 8 + seq
    local = Local(local_sems)
    loads = [
        local.start(source, target)
        for source, target in (
            (w_ada_in, w_ada_ref),
            (w_out_in, w_out_ref),
            (w_up_in, w_up_ref),
            (w_down_in, w_down_ref),
            (cotangent_in, cotangent_ref),
        )
    ]
    own_block[...] = jnp.full((8, 128), level_ref[0, 0].astype(F32), F32)

    def place_bias(line, lane, ref, first, share):
        values = low(ref[first : first + share]).astype(F32)
        own_block[line : line + 1, lane : lane + share] = values.reshape(1, share)

    place_bias(1, 0, b_up_ref, 0, 128)
    place_bias(2, 0, b_qkv_ref, 0, 96)
    place_bias(2, 96, b_out_ref, 0, 32)
    place_bias(3, 0, b_ada_ref, 0, 128)
    place_bias(4, 0, b_ada_ref, 128, 64)
    place_bias(4, 64, b_down_ref, 0, 32)
    levels[dp, seq] = own_block[...]
    wide[0, dp, z, core] = low(w_qkv_ref[:, :1024])
    place.greet()
    level_gather = SmallGather(wire, place, levels)
    level_gather.along_seq()
    pieces = [Gather(wire, place, wide.at[index]) for index in range(8)]
    pieces += [Gather(wire, place, down.at[index]) for index in range(4)]
    pieces[0].along_z()
    pieces[0].own_xy()
    for block in (1, 2):
        wide[block, dp, z, core] = low(w_qkv_ref[:, 1024 * block : 1024 * (block + 1)])
        pieces[block].own_xy()
    saved = []

    def save(index):
        pieces[index].finish()
        source, target = (
            (wide.at[index], wide_out.at[index])
            if index < 8
            else (down.at[index - 8], down_out.at[index - 8])
        )
        saved.append(local.start(source, target))

    def keep(source, target):
        saved.append(local.start(source, target))

    started = [2]
    passed = [4]

    def start_z(last):
        while started[0] <= min(last, 11):
            pieces[started[0]].along_z()
            started[0] += 1

    def tick(step):
        start_z((0, 0, 0, 8, 8, 8, 10, 11)[min(step, 7)])
        while passed[0] <= min(11, max(step + 1, (0, 0, 0, 5, 6, 8)[min(step, 5)])):
            pieces[passed[0]].pass_z()
            passed[0] += 1
        if step < 12:
            pieces[step].along_xy()
        if step - 1 < 12:
            pieces[step - 1].across()
        if step - 2 < 12:
            pieces[step - 2].to_sibling()
        save(step - 3)

    x = x_ref[...].astype(F32)
    normed, unused = norm_parts(x)
    flat[0] = normed
    level_gather.along_dp()
    pieces[1].along_z()
    level_gather.finish()
    level_rows = jnp.concatenate(
        [levels[group, frame, 0:1, :] for group in range(4) for frame in range(8)]
        + [jnp.full((96, 128), -1.0, F32)],
        axis=0,
    )
    lane = lax.broadcasted_iota(jnp.int32, (128, 128), 1)
    own_level = (lane + device * 32).astype(F32)
    one_hot = jnp.where((level_rows == own_level) & (lane < 32), 1.0, 0.0)
    one_hot_ref[...] = one_hot
    one_hot_turned = low(one_hot.T)[:32, :]
    rows = contract(low(table_ref[...]), one_hot_turned, 0, 0).reshape(32, 4, 8, 128)
    found[...] = pack_lanes(rows).reshape(found.shape)
    found_copies = spread_dp(wire, place, lambda dp: found.at[dp], found_dp)
    for copy in loads:
        copy.wait()
    wide[3, dp, z, core] = low(w_out_ref[...])
    for block in range(4):
        wide[4 + block, dp, z, core] = low(w_up_ref[:, 1024 * block : 1024 * (block + 1)])
    for block in range(4):
        down[block, dp, z, core] = low(w_down_ref[:, 256 * block : 256 * (block + 1)])
    pieces[0].pass_z()
    pieces[0].along_xy()
    arrive(found_copies)
    found_sum[...] = total_of(found[dp], found_dp, 3)
    found_copies = spread_seq(wire, place, lambda seq: found_sum.at[seq], found_seq)
    start_z(4)
    cosine, sine = rope_in_kernel(seq)
    cosine_ref[...] = cosine
    sine_ref[...] = sine
    keep(cosine_ref, cosine_out)
    keep(sine_ref, sine_out)
    pieces[1].pass_z()
    pieces[1].along_xy()
    pieces[0].across()
    arrive(found_copies)
    embedded = unpack_lanes(total_of(found_sum[seq], found_seq, 7))
    embedded_ref[...] = embedded
    silu_in = low(embedded / (1.0 + jnp.exp(-embedded)))
    for block in range(6):
        part = contract(silu_in, low(w_ada_ref[:, 1024 * block : 1024 * (block + 1)]), 0, 0)
        lines = [part[:32, 128 * line : 128 * (line + 1)].reshape(4, 8, 128) for line in range(8)]
        for pair in range(4):
            both = jnp.concatenate(lines[2 * pair : 2 * pair + 2], axis=1)
            partial_mod[4 * block + pair] = low(both)
    mod_copies = spread_dp(wire, place, lambda dp: partial_mod.at[:, dp], mod_dp)
    blocks[...] = levels[...].reshape(256, 128)
    every_bias(blocks, bias_lines)
    start_z(5)
    pieces[2].pass_z()
    pieces[2].along_xy()
    pieces[1].across()
    pieces[0].to_sibling()
    arrive(mod_copies)
    mod_sum[...] = total_of(partial_mod[:, dp].astype(F32), mod_dp, 3).reshape(384, 128)
    for frame in range(8):
        mod_blocks[frame] = mod_sum[pl.ds(frame, 48, stride=8), :]
    mod_copies = spread_seq(wire, place, lambda seq: mod_blocks.at[seq], mod_seq)
    pieces[3].pass_z()
    tick(3)
    biases = bias_lines[...]
    arrive(mod_copies)
    modulation = total_of(mod_blocks[seq], mod_seq, 7) + biases[72:120]
    for block in range(6):
        modulation_ref[block : block + 1, :] = row_of(modulation, 8 * block)
    shift_one = modulation_ref[0:1, :]
    scale_one = modulation_ref[1:2, :]
    gate_one = modulation_ref[2:3, :]
    shift_two = modulation_ref[3:4, :]
    scale_two = modulation_ref[4:5, :]
    gate_two = modulation_ref[5:6, :]
    normed_one_ref[...] = low(flat[0] * (1.0 + scale_one) + shift_one)
    keep(normed_one_ref, normed_one_out)
    cosine = cosine_ref[...]
    sine = sine_ref[...]
    head_copies = []

    def project(block, target):
        r = contract(normed_one_ref[...], whole_piece(wide.at[block]), 1, 0)
        r = r + row_of(biases, 8 * block)
        for group in range(8):
            part = r[:, 128 * group : 128 * (group + 1)]
            if block < 2:
                part = part * cosine + half_turn(part) * sine
            if block == 0:
                part = part * 0.125
            act_ref[:, 1024 * block + 128 * group : 1024 * block + 128 * (group + 1)] = low(part)
        for other in place.seq_peers:
            columns = pl.ds(pl.multiple_of(1024 * block + other * 128, 128), 128)
            head_copies.append(
                wire.send(act_ref.at[:, columns], target.at[seq], place.at_seq(other))
            )
        columns = pl.ds(pl.multiple_of(1024 * block + seq * 128, 128), 128)
        target[seq] = act_ref[:, columns]

    project(0, query_ref)
    tick(4)
    project(1, keys_ref)
    tick(5)
    project(2, values_ref)
    tick(6)
    tick(7)
    arrive(head_copies)
    keep(query_ref, query_out)
    keep(keys_ref, keys_out)
    keep(values_ref, values_out)

    def back_copy(frame, source):
        columns = pl.ds(pl.multiple_of(source * 128, 128), 128)
        return pltpu.make_async_remote_copy(
            src_ref=attended_ref.at[frame],
            dst_ref=attended_tokens.at[:, columns],
            send_sem=back_send.at[frame],
            recv_sem=back_recv.at[source],
            device_id=place.at_seq(frame),
            device_id_type=MESH_ID,
        )

    def send_back(frame):
        @pl.when(seq != frame)
        def _():
            back_copy(frame, seq).start()

        @pl.when(seq == frame)
        def _():
            columns = pl.ds(pl.multiple_of(seq * 128, 128), 128)
            attended_tokens[:, columns] = attended_ref[frame]

    for frame in (7, 0, 6, 1, 5, 2, 4, 3):
        attend_frame(
            frame, query_ref, keys_ref, values_ref, attended_ref, log_total_ref, scores
        )
        send_back(frame)
        if frame == 1:
            tick(8)
    keep(attended_ref, attended_out)
    tick(9)
    for other in place.seq_peers:
        back_copy(other, other).wait_recv()
    for other in place.seq_peers:
        back_copy(other, other).wait_send()
    keep(attended_tokens, tokens_out)
    wire.drain(head_copies)
    branch_one = contract(attended_tokens[...], whole_piece(wide.at[3]), 1, 0)
    branch_one = branch_one + row_of(biases, 24)
    branch_one_ref[...] = branch_one
    keep(branch_one_ref, branch_one_out)
    middle = x_ref[...].astype(F32) + gate_one * branch_one
    middle_ref[...] = middle
    keep(middle_ref, middle_out)
    normed, unused = norm_parts(middle)
    normed_two_ref[...] = low(normed * (1.0 + scale_two) + shift_two)
    keep(normed_two_ref, normed_two_out)
    tick(10)
    for block in range(4):
        if block == 2:
            tick(11)
        pre = contract(normed_two_ref[...], whole_piece(wide.at[4 + block]), 1, 0)
        act, slope = gelu_parts(pre + row_of(biases, 32 + 8 * block))
        act_ref[:, 1024 * block : 1024 * (block + 1)] = low(act)
        slope_ref[:, 1024 * block : 1024 * (block + 1)] = low(slope)
    keep(act_ref, act_out)
    keep(slope_ref, slope_out)
    for block in range(4):
        if block:
            tick(11 + block)
        flat[0, :, 256 * block : 256 * (block + 1)] = contract(
            act_ref[...], whole_piece(down.at[block]), 1, 0
        )
    branch_two = flat[0] + row_of(biases, 64)
    layer_out_ref[...] = low(middle_ref[...] + gate_two * branch_two)
    gate_two_grad_ref[...] = jnp.sum(
        cotangent_ref[...].astype(F32) * branch_two, axis=0, keepdims=True
    )
    wire.drain()
    for copy in saved:
        copy.wait()


def vmem(shape, dtype=F32):
    return pltpu.VMEM(shape, dtype)


def run_forward(x, level, table, biases, w_qkv, w_out, w_up, w_down, w_ada, cotangent):
    shape = jax.ShapeDtypeStruct
    small = [
        ((256, 1024), BF16),
        ((8, 1, 512), F32),
        ((8, 1024), F32),
        ((32, 128), F32),
        ((128, 128), F32),
        ((1, 1024), F32),
    ]
    gathered = [((8, 4, 4, 2, 32, 1024), BF16), ((4, 4, 4, 2, 128, 256), BF16)]
    kept = (
        [((8, 256, 128), BF16)] * 4
        + [((256, 1024), BF16)] * 3
        + [((256, 1024), F32)] * 2
        + [((256, 4096), BF16)] * 2
        + [((256, 128), F32)] * 2
    )
    fetched = [
        ((32, 1024), F32),
        ((32, 4096), F32),
        ((128, 1024), F32),
        ((32, 6144), F32),
        ((256, 1024), BF16),
    ]
    in_vmem = pl.BlockSpec(memory_space=pltpu.VMEM)
    anywhere = pl.BlockSpec(memory_space=pl.ANY)
    scratch = [vmem(*array) for array in kept + fetched + gathered]
    scratch += [
        vmem((4, 8, 8, 128)),
        vmem((4, 8, 8, 128)),
        vmem((3, 8, 8, 128)),
        vmem((8, 8, 128)),
        vmem((7, 8, 128)),
        vmem((24, 4, 16, 128), BF16),
        vmem((3, 24, 16, 128), BF16),
        vmem((384, 128)),
        vmem((8, 48, 128)),
        vmem((7, 48, 128)),
        vmem((120, 128)),
        vmem((256, 128)),
        vmem((8, 128)),
        vmem((1, 256, 1024)),
        vmem((8, 256, 512)),
        pltpu.SemaphoreType.DMA((220,)),
        pltpu.SemaphoreType.DMA((220,)),
        pltpu.SemaphoreType.DMA((8,)),
        pltpu.SemaphoreType.DMA((8,)),
        pltpu.SemaphoreType.DMA((32,)),
    ]
    return pl.pallas_call(
        forward_kernel,
        out_shape=[shape(*out) for out in small + gathered + kept],
        in_specs=[in_vmem, pl.BlockSpec(memory_space=pltpu.SMEM)] + [in_vmem] * 7 + [anywhere] * 5,
        out_specs=[in_vmem] * len(small) + [anywhere] * len(gathered + kept),
        scratch_shapes=scratch,
        compiler_params=pltpu.CompilerParams(
            collective_id=0, has_side_effects=True, vmem_limit_bytes=VMEM_LIMIT
        ),
        name="block_forward",
    )(x, level, table, *biases, w_qkv, w_out, w_up, w_down, w_ada, cotangent)


SLOTS = 5


class Scatter:
    def __init__(self, wire, place, index, terms, buffers, share_sum, credit, finish):
        self.wire, self.place, self.index, self.terms = wire, place, index, terms
        from_core, from_far, from_xy, from_z = buffers
        self.from_core = from_core.at[index % SLOTS]
        self.from_far = from_far.at[index]
        self.from_xy = from_xy.at[index]
        self.from_z = from_z.at[index]
        self.share_sum, self.credit, self.finish = share_sum, credit, finish
        self.mine = []

    def send(self, source, target, device, only=None, landing=None):
        copy = self.wire.send(source, target, device, only, landing)
        self.mine.append(copy)
        return copy

    def to_sibling(self):
        place = self.place
        if self.index >= SLOTS:
            pl.semaphore_wait(self.credit, 1)
        self.coming = [
            self.send(self.terms.at[:, :, place.other], self.from_core, place.sibling)
        ]

    def across(self, last):
        place, terms, core = self.place, self.terms, self.place.core
        arrive(self.coming)
        far = place.far_dp
        terms[far, :, core] = terms[far, :, core] + self.from_core[far]
        self.coming = [
            self.send(
                terms.at[far, pl.ds(0, 2), core], self.from_far.at[0], place.at_dp(place.x_dp)
            ),
            self.send(
                terms.at[far, pl.ds(2, 2), core], self.from_far.at[1], place.at_dp(place.y_dp)
            ),
        ]
        for group in (place.x_dp, place.y_dp, place.dp):
            terms[group, :, core] = terms[group, :, core] + self.from_core[group]
        if not last:
            pl.semaphore_signal(
                self.credit, inc=1, device_id=place.sibling, device_id_type=MESH_ID
            )

    def along_xy(self):
        place, terms, core = self.place, self.terms, self.place.core
        arrive(self.coming)
        first, second = pl.ds(0, 2), pl.ds(2, 2)
        terms[place.y_dp, first, core] = terms[place.y_dp, first, core] + self.from_far[0]
        terms[place.x_dp, second, core] = terms[place.x_dp, second, core] + self.from_far[1]
        self.coming = [
            self.send(terms.at[dp, :, core], self.from_xy.at[slot], place.at_dp(dp))
            for slot, dp in enumerate((place.x_dp, place.y_dp))
        ]

    def gather_shares(self):
        place, terms, core = self.place, self.terms, self.place.core
        arrive(self.coming)
        own = terms[place.dp, :, core].astype(F32)
        self.shares = self.from_xy.at[0]
        self.shares[...] = low(total_of(own, self.from_xy, 2))
        self.wire.drain(self.mine)
        self.mine = []

    def along_z(self):
        place = self.place

        def share(step):
            return self.shares.at[(place.z + step) % 4]

        self.at_end = (place.z == 0) | (place.z == 3)
        self.up = self.send(share(1), self.from_z.at[0], place.at_z(1), place.z != 3)
        self.down = self.send(share(3), self.from_z.at[2], place.at_z(3), place.z != 0)
        self.over = self.send(share(3), self.from_z.at[3], place.at_z(1), place.z == 0)
        self.send(share(1), self.from_z.at[3], place.at_z(3), place.z == 3, landing=self.over)
        self.two = self.send(share(2), self.from_z.at[1], place.at_z(2), self.at_end)

    def pass_z(self):
        place = self.place
        far = self.shares.at[(place.z + 2) % 4]

        @pl.when(jnp.logical_not(self.at_end))
        def _():
            self.over.wait_recv()
            far[...] = far[...] + self.from_z[3]

        self.send(
            far,
            self.from_z.at[1],
            place.at_z(2),
            jnp.logical_not(self.at_end),
            landing=self.two,
        )

    def end(self):
        place, share_sum = self.place, self.share_sum
        arrive([self.two])
        own = self.shares[place.z].astype(F32)
        share_sum[...] = own + self.from_z[1].astype(F32)

        @pl.when(place.z != 0)
        def _():
            self.up.wait_recv()
            share_sum[...] += self.from_z[0].astype(F32)

        @pl.when(place.z != 3)
        def _():
            self.down.wait_recv()
            share_sum[...] += self.from_z[2].astype(F32)

        self.finish(share_sum[...])
        self.wire.drain(self.mine)


def norm_back(normed, inverse, grad):
    mean = jnp.mean(grad, axis=1, keepdims=True)
    along = jnp.mean(grad * normed, axis=1, keepdims=True)
    return (grad - mean - normed * along) * inverse


def column_sum(values):
    return jnp.sum(values, axis=0, keepdims=True)


def pair_deltas(attended, grad_heads, deltas):
    lane = lax.broadcasted_iota(jnp.int32, (8, 128), 1)
    line = lax.broadcasted_iota(jnp.int32, (8, 128), 0)
    picked = jnp.where(lane // 64 == line, 1.0, 0.0).astype(F32)
    for frame in range(8):
        product = attended[frame].astype(F32) * grad_heads[frame].astype(F32)
        sums = contract(picked, product, 1, 1, precision=lax.Precision.HIGHEST)
        deltas[frame] = jnp.concatenate([sums[0:1], sums[1:2]], axis=1)


def frame_pairs():
    for first in range(4):
        last = 7 - first
        yield [(query, first) for query in range(first, last + 1)], first
        yield [(last, key) for key in range(first + 1, last + 1)], last


def attend_pair_back(query_frame, key_frame, heads, log_total, grad_heads, deltas, sums, fresh):
    query, keys, values = heads
    pair = split_heads(query[query_frame])
    grad_pair = split_heads(grad_heads[query_frame])
    weights = jnp.exp(contract(keys[key_frame], pair, 1, 1) - log_total[query_frame])
    grad_weights = contract(values[key_frame], grad_pair, 1, 1)
    grad_scores = low(weights * (grad_weights - deltas[query_frame]))
    turned = contract(keys[key_frame], grad_scores, 0, 0)
    parts = (
        (query_frame, jnp.concatenate([turned[:64, :256], turned[64:, 256:]], axis=0)),
        (key_frame, contract(grad_scores, pair, 1, 0)),
        (key_frame, contract(low(weights), grad_pair, 1, 0)),
    )
    for total, (frame, part), started in zip(sums, parts, fresh):
        if frame in started:
            total[frame] += part
        else:
            started.add(frame)
            total[frame] = part


def backward_kernel(
    cotangent_ref,
    log_total_ref,
    modulation_ref,
    embedded_ref,
    one_hot_ref,
    gate_two_grad_ref,
    wide,
    down,
    act_in,
    slope_in,
    normed_two_in,
    middle_in,
    branch_one_in,
    query_in,
    keys_in,
    values_in,
    attended_in,
    tokens_in,
    x_in,
    normed_one_in,
    cosine_in,
    sine_in,
    w_ada_in,
    grad_hidden_ref,
    grad_table_ref,
    grad_ada_ref,
    grad_ada_bias_ref,
    grad_qkv_ref,
    grad_out_ref,
    grad_up_ref,
    grad_down_ref,
    grad_bias_ref,
    hidden,
    slope_ref,
    normed_two_ref,
    middle_ref,
    branch_one_ref,
    query_ref,
    keys_ref,
    values_ref,
    attended_ref,
    attended_tokens,
    x_ref,
    normed_one_ref,
    cosine_ref,
    sine_ref,
    w_ada_ref,
    terms,
    from_core,
    from_far,
    from_xy,
    from_z,
    share_sum,
    down_block,
    wide_block,
    grad_two,
    grad_one,
    grad_tokens,
    grad_heads,
    deltas,
    query_sum,
    keys_sum,
    values_sum,
    query_back,
    keys_back,
    values_back,
    qkv_back,
    running,
    bias_lines,
    bias_dp,
    bias_sum,
    bias_seq,
    mod_grads,
    mod_lines,
    embedded_grads,
    send_sems,
    recv_sems,
    back_send,
    back_recv,
    local_sems,
    credit,
):
    place = Place()
    wire = Wire(send_sems, recv_sems)
    dp, seq, core = place.dp, place.seq, place.core
    loads = {}
    local = Local(local_sems)

    def load(name, source, target):
        loads[name] = local.start(source, target)

    def load_down(block):
        load(("down", block), down.at[:, block], down_block)

    def load_wide(block):
        load(("wide", block), wide.at[block], wide_block.at[block % 2])

    load("act", act_in, hidden)
    load_down(0)
    load("slope", slope_in, slope_ref)
    load_wide(4)
    load_wide(5)
    later = (
        (normed_two_in, normed_two_ref),
        (middle_in, middle_ref),
        (branch_one_in, branch_one_ref),
        (query_in, query_ref),
        (keys_in, keys_ref),
        (values_in, values_ref),
        (attended_in, attended_ref),
        (tokens_in, attended_tokens),
        (x_in, x_ref),
        (normed_one_in, normed_one_ref),
        (cosine_in, cosine_ref),
        (sine_in, sine_ref),
        (w_ada_in, w_ada_ref),
    )
    for index, (source, target) in enumerate(later):
        load(index, source, target)
    place.greet()
    scale_one = modulation_ref[1:2, :]
    gate_one = modulation_ref[2:3, :]
    scale_two = modulation_ref[4:5, :]
    gate_two = modulation_ref[5:6, :]
    cotangent = cotangent_ref[...].astype(F32)
    grad_two[...] = low(cotangent * gate_two)

    def keep_bias(first, grad):
        bias_lines[first : first + 8, :] = lines_of(column_sum(grad.astype(F32)))

    bias_lines[72:80, :] = jnp.zeros((8, 128), F32)
    keep_bias(64, grad_two[...])

    def finish(index):
        def store(total):
            if index < 4:
                grad_down_ref[32 * index : 32 * (index + 1), :] = total
            elif index < 8:
                grad_up_ref[:, 1024 * (index - 4) : 1024 * (index - 3)] = total
            elif index == 8:
                grad_out_ref[...] = total
            else:
                grad_qkv_ref[:, 1024 * (index - 9) : 1024 * (index - 8)] = total

        return store

    buffers = (from_core, from_far, from_xy, from_z)
    pieces = [
        Scatter(
            wire, place, index, terms.at[index % SLOTS], buffers, share_sum, credit, finish(index)
        )
        for index in range(12)
    ]
    loads["act"].wait()
    for chunk in range(16):
        part = low(contract(hidden[:, 256 * chunk : 256 * (chunk + 1)], grad_two[...], 0, 0))
        part = part.reshape(2, 4, 32, 1024)
        for index in range(4):
            terms[index, chunk // 4, chunk % 4] = part[:, index]

    def make_terms(index):
        if index < 4:
            return
        for group in range(4):
            rows = slice(256 * group, 256 * (group + 1))
            if index < 8:
                left = normed_two_ref[:, rows]
                right = hidden[:, 1024 * (index - 4) : 1024 * (index - 3)]
            elif index == 8:
                left, right = attended_tokens[:, rows], grad_one[...]
            else:
                left, right = normed_one_ref[:, rows], qkv_back[index - 9]
            part = low(contract(left, right, 0, 0))
            terms[index % SLOTS, group] = part.reshape(4, 2, 32, 1024)

    done = [0, 0, 0]

    def tick(step):
        if 0 <= step - 1 < 12:
            pieces[step - 1].across(step - 1 + SLOTS >= 12)
        if 0 <= step - 3 < 12:
            pieces[step - 3].along_xy()
        if 0 <= step - 5 < 12:
            pieces[step - 5].gather_shares()
        if step < 12:
            make_terms(step)
            pieces[step].to_sibling()

    def settle(sent, passed, ended):
        for stage, last in enumerate((sent, passed, ended)):
            while done[stage] <= min(last, 11):
                piece = pieces[done[stage]]
                (piece.along_z, piece.pass_z, piece.end)[stage]()
                done[stage] += 1

    tick(0)
    tick(1)
    loads["slope"].wait()
    for block in range(4):
        loads[("down", block)].wait()
        grad_act = None
        for index in range(4):
            weight = down_block[index].reshape(1024, 256)
            part = contract(grad_two[:, 256 * index : 256 * (index + 1)], weight, 1, 1)
            grad_act = part if grad_act is None else grad_act + part
        if block < 3:
            load_down(block + 1)
        columns = slice(1024 * block, 1024 * (block + 1))
        grad_pre = low(grad_act * slope_ref[:, columns].astype(F32))
        hidden[:, columns] = grad_pre
        keep_bias(32 + 8 * block, grad_pre)
        loads[("wide", 4 + block)].wait()
        part = contract(grad_pre, whole_piece(wide_block.at[block % 2]), 1, 1)
        running[...] = part if block == 0 else running[...] + part
        load_wide((6, 7, 2, 3)[block])
        if block == 1:
            tick(2)
    for index in range(len(later)):
        loads[index].wait()
    normed, inverse = norm_parts(middle_ref[...])
    grad_normed = running[...]
    grad_shift_two = column_sum(grad_normed)
    grad_scale_two = column_sum(grad_normed * normed)
    grad_middle = cotangent_ref[...].astype(F32) + norm_back(
        normed, inverse, grad_normed * (1.0 + scale_two)
    )
    running[...] = grad_middle
    grad_gate_one = column_sum(grad_middle * branch_one_ref[...])
    grad_one[...] = low(grad_middle * gate_one)
    keep_bias(24, grad_one[...])
    loads[("wide", 3)].wait()
    grad_tokens[...] = low(contract(grad_one[...], whole_piece(wide_block.at[1]), 1, 1))
    load_wide(1)
    head_copies = []
    for other in place.seq_peers:
        columns = pl.ds(pl.multiple_of(other * 128, 128), 128)
        head_copies.append(
            wire.send(grad_tokens.at[:, columns], grad_heads.at[seq], place.at_seq(other))
        )
    own_columns = pl.ds(pl.multiple_of(seq * 128, 128), 128)
    grad_heads[seq] = grad_tokens[:, own_columns]
    tick(3)
    tick(4)
    arrive(head_copies)
    backs = (query_back, keys_back, values_back)

    def back_copy(part, frame, source):
        columns = pl.ds(pl.multiple_of(source * 128, 128), 128)
        return pltpu.make_async_remote_copy(
            src_ref=backs[part].at[frame],
            dst_ref=qkv_back.at[part, :, columns],
            send_sem=back_send.at[part, frame],
            recv_sem=back_recv.at[part, source],
            device_id=place.at_seq(frame),
            device_id_type=MESH_ID,
        )

    def send_back(frame):
        @pl.when(seq != frame)
        def _():
            for part in range(3):
                back_copy(part, frame, seq).start()

        @pl.when(seq == frame)
        def _():
            for part in range(3):
                qkv_back[part, :, own_columns] = backs[part][frame]

    pair_deltas(attended_ref, grad_heads, deltas)
    heads = (query_ref, keys_ref, values_ref)
    fresh = (set(), set(), set())
    for pairs, frame in frame_pairs():
        for query_frame, key_frame in pairs:
            attend_pair_back(
                query_frame,
                key_frame,
                heads,
                log_total_ref,
                grad_heads,
                deltas,
                (query_sum, keys_sum, values_sum),
                fresh,
            )
        query_back[frame] = low(query_sum[frame].T * 0.125)
        keys_back[frame] = low(keys_sum[frame])
        values_back[frame] = low(values_sum[frame])
        send_back(frame)
        if frame in (7, 2):
            tick(5 if frame == 7 else 6)
    tick(7)
    tick(8)
    for part in range(3):
        for other in place.seq_peers:
            back_copy(part, other, other).wait_recv()
    cosine, sine = cosine_ref[...], sine_ref[...]
    grad_normed = None
    for part in range(3):
        if part < 2:
            for group in range(8):
                columns = slice(128 * group, 128 * (group + 1))
                grad = qkv_back[part, :, columns].astype(F32)
                qkv_back[part, :, columns] = low(grad * cosine - half_turn(grad) * sine)
        keep_bias(8 * part, qkv_back[part])
        index = (2, 1, 0)[part]
    for block, slot in ((2, 0), (1, 1), (0, 0)):
        loads[("wide", block)].wait()
        part = contract(qkv_back[block], whole_piece(wide_block.at[slot]), 1, 1)
        grad_normed = part if grad_normed is None else grad_normed + part
        if block == 2:
            load_wide(0)
    bias_copies = spread_dp(wire, place, lambda dp: bias_lines, bias_dp)
    normed, inverse = norm_parts(x_ref[...].astype(F32))
    grad_shift_one = column_sum(grad_normed)
    grad_scale_one = column_sum(grad_normed * normed)
    grad_hidden_ref[...] = low(
        running[...] + norm_back(normed, inverse, grad_normed * (1.0 + scale_one))
    )
    rows = (
        grad_shift_one,
        grad_scale_one,
        grad_gate_one,
        grad_shift_two,
        grad_scale_two,
        gate_two_grad_ref[...],
    )
    mod_grads[dp, seq] = low(jnp.concatenate([lines_of(row) for row in rows], axis=0))
    mod_gather = SmallGather(wire, place, mod_grads)
    mod_gather.along_seq()
    tick(9)
    settle(3, -1, -1)
    tick(10)
    settle(4, -1, -1)
    tick(11)
    settle(5, 2, -1)
    mod_gather.along_dp()
    arrive(bias_copies)
    bias_sum[...] = total_of(bias_lines[...], bias_dp, 3)
    bias_copies = spread_seq(wire, place, lambda seq: bias_sum, bias_seq)
    tick(12)
    settle(7, 4, -1)
    tick(13)
    settle(8, 6, 3)
    tick(14)
    settle(9, 7, 5)
    mod_gather.finish()
    lines = mod_grads[...].astype(F32).reshape(1536, 128)
    mod_lines[...] = lines
    grad_ada_bias_ref[...] = jnp.sum(lines.reshape(32, 48, 128), axis=0)
    embedded = embedded_ref[...]
    share = 1.0 / (1.0 + jnp.exp(-embedded))
    silu_in = low(embedded * share)[:, :32]
    empty = jnp.zeros((96, 128), BF16)
    grad_silu = None
    for block in range(6):
        parts = []
        for line in range(8):
            part = mod_lines[pl.ds(8 * block + line, 32, stride=48), :]
            parts.append(jnp.concatenate([low(part), empty], axis=0))
        every = jnp.concatenate(parts, axis=1)
        columns = slice(1024 * block, 1024 * (block + 1))
        grad_ada_ref[:, columns] = contract(silu_in, every[:32], 1, 0)
        part = contract(low(w_ada_ref[:, columns]), every, 1, 1)
        grad_silu = part if grad_silu is None else grad_silu + part
    grad_embedded = grad_silu * share * (1.0 + embedded * (1.0 - share))
    embedded_grads[dp, seq] = pack_lanes(grad_embedded.reshape(1, 4, 8, 128))[0]
    embedded_gather = SmallGather(wire, place, embedded_grads)
    embedded_gather.along_seq()
    tick(15)
    settle(10, 9, 7)
    embedded_gather.along_dp()
    arrive(bias_copies)
    grad_bias_ref[...] = total_of(bias_sum[...], bias_seq, 7)
    tick(16)
    settle(11, 10, 9)
    embedded_gather.finish()
    every_grad = jnp.concatenate(
        [unpack_lanes(embedded_grads[group, frame]) for group in range(4) for frame in range(8)],
        axis=0,
    )
    grad_table_ref[...] = contract(
        one_hot_ref[...],
        every_grad,
        0,
        1,
        precision=lax.Precision.HIGHEST,
    )[:32]
    settle(11, 11, 10)
    settle(11, 11, 11)
    for part in range(3):
        for other in place.seq_peers:
            back_copy(part, other, other).wait_send()
    wire.drain()


def run_backward(cotangent, small, gathered, kept, x, w_ada):
    shape = jax.ShapeDtypeStruct
    outs = [
        ((256, 1024), BF16),
        ((32, 1024), F32),
        ((32, 6144), F32),
        ((48, 128), F32),
        ((32, 3072), F32),
        ((32, 1024), F32),
        ((32, 4096), F32),
        ((128, 1024), F32),
        ((80, 128), F32),
    ]
    query, keys, values, attended, tokens, normed_one, normed_two = kept[:7]
    middle, branch_one, act, slope, cosine, sine = kept[7:]
    fetched = (act, slope, normed_two, middle, branch_one, query, keys, values, attended)
    fetched += (tokens, x, normed_one, cosine, sine, w_ada)
    in_vmem = pl.BlockSpec(memory_space=pltpu.VMEM)
    anywhere = pl.BlockSpec(memory_space=pl.ANY)
    scratch = [vmem(array.shape, array.dtype) for array in fetched]
    scratch += [
        vmem((SLOTS, 4, 4, 2, 32, 1024), BF16),
        vmem((SLOTS, 4, 4, 32, 1024), BF16),
        vmem((12, 2, 2, 32, 1024), BF16),
        vmem((12, 2, 4, 32, 1024), BF16),
        vmem((12, 4, 32, 1024), BF16),
        vmem((32, 1024)),
        vmem((4, 4, 2, 128, 256), BF16),
        vmem((2, 4, 4, 2, 32, 1024), BF16),
        vmem((256, 1024), BF16),
        vmem((256, 1024), BF16),
        vmem((256, 1024), BF16),
        vmem((8, 256, 128), BF16),
        vmem((8, 1, 512)),
        vmem((8, 128, 256)),
        vmem((8, 256, 128)),
        vmem((8, 256, 128)),
        vmem((8, 256, 128), BF16),
        vmem((8, 256, 128), BF16),
        vmem((8, 256, 128), BF16),
        vmem((3, 256, 1024), BF16),
        vmem((256, 1024)),
        vmem((80, 128)),
        vmem((3, 80, 128)),
        vmem((80, 128)),
        vmem((7, 80, 128)),
        vmem((4, 8, 48, 128), BF16),
        vmem((1536, 128)),
        vmem((4, 8, 8, 128)),
        pltpu.SemaphoreType.DMA((200,)),
        pltpu.SemaphoreType.DMA((200,)),
        pltpu.SemaphoreType.DMA((3, 8)),
        pltpu.SemaphoreType.DMA((3, 8)),
        pltpu.SemaphoreType.DMA((32,)),
        pltpu.SemaphoreType.REGULAR,
    ]
    return pl.pallas_call(
        backward_kernel,
        out_shape=[shape(*out) for out in outs],
        in_specs=[in_vmem] * 6 + [anywhere] * 17,
        out_specs=[in_vmem] * 9,
        scratch_shapes=scratch,
        compiler_params=pltpu.CompilerParams(
            collective_id=1, has_side_effects=True, vmem_limit_bytes=VMEM_LIMIT
        ),
        name="block_backward",
    )(cotangent, *small, *gathered, *fetched)


def finish_kernel(lines_ref, ada_lines_ref, *refs):
    device = lax.axis_index("dp") * 8 + lax.axis_index("seq")
    for index in range(8):
        refs[8 + index][...] = refs[index][...]
    for index, share in enumerate(BIAS_SHARE):
        lines, first = (lines_ref, BIAS_FIRST[index]) if index < 4 else (ada_lines_ref, 0)
        offset = device * share
        line = first + offset // 128
        pair = jnp.concatenate([lines[pl.ds(line, 1), :], lines[pl.ds(line + 1, 1), :]], axis=1)
        part = pltpu.roll(pair, (256 - offset % 128) % 256, 1)
        refs[16 + index][...] = part[:, :share].reshape(share)


def run_finish(lines, ada_lines, arrays):
    shape = jax.ShapeDtypeStruct
    in_vmem = pl.BlockSpec(memory_space=pltpu.VMEM)
    return pl.pallas_call(
        finish_kernel,
        out_shape=[shape(array.shape, array.dtype) for array in arrays]
        + [shape((share,), F32) for share in BIAS_SHARE],
        in_specs=[in_vmem] * 10,
        out_specs=[in_vmem] * 13,
        name="block_outputs",
    )(lines, ada_lines, *arrays)


def fast_body(
    hidden_in,
    noise_level,
    noise_table,
    w_ada,
    b_ada,
    w_qkv,
    b_qkv,
    w_out,
    b_out,
    w_up,
    b_up,
    w_down,
    b_down,
    grad_out,
):
    biases = (b_qkv, b_out, b_up, b_down, b_ada)
    x, cotangent = hidden_in[0], grad_out[0]
    results = run_forward(
        x, noise_level, noise_table, biases, w_qkv, w_out, w_up, w_down, w_ada, cotangent
    )
    layer_out, small, gathered, kept = results[0], results[1:6], results[6:8], results[8:]
    grads = run_backward(cotangent, small, gathered, kept, x, w_ada)
    grad_hidden, grad_table, grad_ada_w, ada_lines, *weight_grads, lines = grads
    outs = run_finish(
        lines, ada_lines, (layer_out, grad_hidden, grad_table, grad_ada_w, *weight_grads)
    )
    layer_out, grad_hidden, grad_table, grad_ada_w, qkv_w, out_w, up_w, down_w = outs[:8]
    qkv_b, out_b, up_b, down_b, ada_b = outs[8:]
    return (
        layer_out[None],
        grad_hidden[None],
        grad_table,
        grad_ada_w,
        ada_b,
        qkv_w,
        qkv_b,
        out_w,
        out_b,
        up_w,
        up_b,
        down_w,
        down_b,
    )


def solution(mesh):
    tokens = P("dp", "seq", None)
    matrix = P(ALL, None)
    vector = P(ALL)
    parameters = (matrix,) + (matrix, vector) * 5
    chips = dict(mesh.shape) == {"dp": 4, "seq": 8}
    return jax.shard_map(
        fast_body if chips else general_body,
        mesh=mesh,
        in_specs=(tokens, P("dp", "seq")) + parameters + (tokens,),
        out_specs=(tokens, tokens) + parameters,
        check_vma=False,
    )
```

```python
from functools import partial
import math

import jax
import jax.numpy as jnp
from jax import lax
from jax.experimental import pallas as pl
from jax.experimental.pallas import tpu as pltpu
from jax.sharding import PartitionSpec as P

H = 16
GRID_W = 16
PATCHES = 256


norm_eps = 1e-06
masked_score = -1e30
ALL = ("dp", "seq")
F32 = jnp.float32
BF16 = jnp.bfloat16


def layer_norm(values):
    centred = values - jnp.mean(values, axis=-1, keepdims=True)
    spread = jnp.mean(centred * centred, axis=-1, keepdims=True)
    return centred * lax.rsqrt(spread + norm_eps)


def modulate(values, shift_term, scale_term):
    return layer_norm(values) * (1.0 + scale_term) + shift_term


def turn_half(values):
    extent = values.shape[-1]
    side_part = 2 * (3 * extent // 16)
    pieces = []
    offset = 0
    for part_size in (extent - 2 * side_part, side_part, side_part):
        half_size = part_size // 2
        pieces.append(-values[..., offset + half_size : offset + part_size])
        pieces.append(values[..., offset : offset + half_size])
        offset = offset + part_size
    return jnp.concatenate(pieces, axis=-1)


def part_angles(places, part_size):
    half_size = part_size // 2
    rates = jnp.exp(-math.log(10000.0) * jnp.arange(half_size, dtype=F32) / half_size)
    angles = places.astype(F32)[:, None] * rates[None, :]
    return jnp.concatenate([angles, angles], axis=1)


def angle_table(places, extent):
    side_part = 2 * (3 * extent // 16)
    patch_index = places % PATCHES
    angles = jnp.concatenate(
        [
            part_angles(places // PATCHES, extent - 2 * side_part),
            part_angles(patch_index // GRID_W, side_part),
            part_angles(patch_index % GRID_W, side_part),
        ],
        axis=1,
    )
    return (jnp.cos(angles), jnp.sin(angles))


def rotate(values, cosine_table, sine_table):
    return values * cosine_table + turn_half(values) * sine_table


def unrotate(values, cosine_table, sine_table):
    return values * cosine_table - turn_half(values * sine_table)


def low(values):
    return values.astype(BF16)


def dot(left, right):
    return jnp.dot(left, right, preferred_element_type=F32)


def gather_rows(share):
    return lax.all_gather(low(share), ALL, axis=0, tiled=True)


def scatter_rows(whole):
    return lax.psum_scatter(whole, ALL, scatter_dimension=0, tiled=True)


def frame_modulation(noise_level, noise_table, w_ada, b_ada):
    levels = lax.all_gather(noise_level.reshape(-1), ALL, axis=0, tiled=True)
    device = lax.axis_index("dp") * lax.axis_size("seq") + lax.axis_index("seq")
    share = noise_table.shape[0]
    own_levels = device * share + jnp.arange(share, dtype=jnp.int32)
    one_hot = levels[:, None] == own_levels[None, :]
    found = dot(low(one_hot), low(noise_table))
    embedded = lax.psum_scatter(low(found), ALL, scatter_dimension=1, tiled=True).astype(F32)
    silu_in = low(jax.nn.silu(embedded))
    modulation = lax.psum_scatter(
        dot(silu_in, low(w_ada)), ALL, scatter_dimension=0, tiled=True
    ) + gather_rows(b_ada).astype(F32)
    return one_hot, embedded, silu_in, modulation


def frame_gradients(grad_modulation, one_hot, embedded, silu_in, w_ada):
    every = lax.all_gather(grad_modulation, ALL, axis=0, tiled=True)
    grad_ada_w = lax.dot_general(
        silu_in, every, (((0,), (0,)), ((), ())), preferred_element_type=F32
    )
    share = w_ada.shape[1] // lax.axis_size(ALL)
    device = lax.axis_index("dp") * lax.axis_size("seq") + lax.axis_index("seq")
    columns = lax.dynamic_slice_in_dim(every, device * share, share, axis=1)
    grad_ada_b = jnp.sum(columns.astype(F32), axis=0)
    grad_silu = lax.dot_general(
        every, low(w_ada), (((1,), (1,)), ((), ())), preferred_element_type=F32
    )
    unused, silu_back = jax.vjp(jax.nn.silu, embedded)
    grad_embedded = lax.all_gather(silu_back(grad_silu)[0], ALL, axis=1, tiled=True)
    grad_table = jnp.dot(
        one_hot.astype(F32).T, grad_embedded, precision=lax.Precision.HIGHEST
    )
    return grad_table, grad_ada_w, grad_ada_b


def to_heads(values):
    return lax.all_to_all(values, "seq", split_axis=2, concat_axis=1, tiled=True)


def to_tokens(values):
    return lax.all_to_all(values, "seq", split_axis=1, concat_axis=2, tiled=True)


def as_heads(values):
    return values.reshape(*values.shape[:2], -1, 64)


def query_blocks(array, axis):
    blocks = array.shape[axis] // PATCHES
    split = array.shape[:axis] + (blocks, PATCHES) + array.shape[axis + 1 :]
    return jnp.moveaxis(array.reshape(split), axis, 0)


def block_scores(query_block, keys, frame, score_scale):
    scores = (
        jnp.einsum("cqhd,ckhd->chqk", query_block, keys, preferred_element_type=F32) * score_scale
    )
    allowed = jnp.arange(keys.shape[1], dtype=jnp.int32) // PATCHES <= frame
    return jnp.where(allowed, scores, masked_score)


def attend(query, keys, values, score_scale):
    def one_block(block_in):
        query_block, frame = block_in
        scores = block_scores(query_block, keys, frame, score_scale)
        row_max = jnp.max(scores, axis=-1, keepdims=True)
        exponent = jnp.exp(scores - row_max)
        row_total = jnp.sum(exponent, axis=-1, keepdims=True)
        weighted = jnp.einsum(
            "chqk,ckhd->cqhd", low(exponent / row_total), values, preferred_element_type=F32
        )
        return low(weighted), (row_max + jnp.log(row_total))[..., 0]

    frames = jnp.arange(query.shape[1] // PATCHES, dtype=jnp.int32)
    attended, log_total = lax.map(one_block, (query_blocks(query, 1), frames))
    return (
        jnp.moveaxis(attended, 0, 1).reshape(query.shape),
        jnp.moveaxis(log_total, 0, 2).reshape(query.shape[0], query.shape[2], query.shape[1]),
    )


def attend_back(query, keys, values, grad_heads, log_total, row_delta, score_scale):
    def one_block(carried, block_in):
        query_block, grad_block, total_block, delta_block, frame = block_in
        scores = block_scores(query_block, keys, frame, score_scale)
        softmax_weights = jnp.exp(scores - total_block[..., None])
        grad_soft = jnp.einsum("cqhd,ckhd->chqk", grad_block, values, preferred_element_type=F32)
        grad_scores = low(softmax_weights * (grad_soft - delta_block[..., None]))
        query_grad = jnp.einsum("chqk,ckhd->cqhd", grad_scores, keys, preferred_element_type=F32)
        keys_grad = jnp.einsum(
            "chqk,cqhd->ckhd", grad_scores, query_block, preferred_element_type=F32
        )
        values_grad = jnp.einsum(
            "chqk,cqhd->ckhd", low(softmax_weights), grad_block, preferred_element_type=F32
        )
        return (carried[0] + keys_grad, carried[1] + values_grad), query_grad

    frames = jnp.arange(query.shape[1] // PATCHES, dtype=jnp.int32)
    empty = jnp.zeros(keys.shape, F32)
    (grad_keys, grad_values), grad_query = lax.scan(
        one_block,
        (empty, empty),
        (
            query_blocks(query, 1),
            query_blocks(grad_heads, 1),
            query_blocks(log_total, 2),
            query_blocks(row_delta, 2),
            frames,
        ),
    )
    grad_query = jnp.moveaxis(grad_query, 0, 1).reshape(query.shape)
    return grad_query * score_scale, grad_keys * score_scale, grad_values


def general_body(
    hidden_in,
    noise_level,
    noise_table,
    w_ada,
    b_ada,
    w_qkv,
    b_qkv,
    w_out,
    b_out,
    w_up,
    b_up,
    w_down,
    b_down,
    grad_out,
):
    qkv_w, qkv_b, out_w, out_b, up_w, up_b, down_w, down_b = [
        gather_rows(share)
        for share in (w_qkv, b_qkv, w_out, b_out, w_up, b_up, w_down, b_down)
    ]
    clip_count, patches, model_width = hidden_in.shape
    head_dim = model_width // H
    score_scale = 1.0 / math.sqrt(head_dim)
    head_shape = (clip_count, patches, H, head_dim)
    inputs = hidden_in.astype(F32)
    one_hot, embedded, silu_in, modulation = frame_modulation(
        noise_level, noise_table, w_ada, b_ada
    )
    shift_one, scale_one, gate_one, shift_two, scale_two, gate_two = [
        modulation[:, None, column_block * model_width : (column_block + 1) * model_width]
        for column_block in range(6)
    ]
    normed_one = low(modulate(inputs, shift_one, scale_one))
    qkv_all = dot(normed_one, qkv_w) + qkv_b.astype(F32)
    frame_own = lax.axis_index("seq")
    places = frame_own * patches + jnp.arange(patches, dtype=jnp.int32)
    cosine_local, sine_local = angle_table(places, head_dim)
    cosine_wide = cosine_local[None, :, None, :]
    sine_wide = sine_local[None, :, None, :]
    flat_shape = (clip_count, patches, model_width)

    def turned(block):
        part = qkv_all[..., block * model_width : (block + 1) * model_width]
        return low(rotate(part.reshape(head_shape), cosine_wide, sine_wide)).reshape(flat_shape)

    query = as_heads(to_heads(turned(0)))
    keys = as_heads(to_heads(turned(1)))
    values = as_heads(to_heads(low(qkv_all[..., 2 * model_width :])))
    attended, log_total = attend(query, keys, values, score_scale)
    attended_low = to_tokens(attended.reshape(*attended.shape[:2], -1))
    branch_one = dot(attended_low, out_w) + out_b.astype(F32)
    middle = inputs + gate_one * branch_one
    normed_two = low(modulate(middle, shift_two, scale_two))
    hidden_pre = dot(normed_two, up_w) + up_b.astype(F32)
    hidden_act = low(jax.nn.gelu(hidden_pre, approximate=True))
    branch_two = dot(hidden_act, down_w) + down_b.astype(F32)
    outputs = middle + gate_two * branch_two
    cotangent = grad_out.astype(F32)
    grad_gate_two = jnp.sum(cotangent * branch_two, axis=1)
    grad_branch_two = low(cotangent * gate_two)

    def weight_grad(left, right):
        whole = jnp.einsum("cpi,cpo->io", left, right, preferred_element_type=F32)
        return scatter_rows(low(whole)).astype(F32)

    def bias_grad(grad):
        return scatter_rows(jnp.sum(grad.astype(F32), axis=(0, 1)))

    def back_dot(grad, weight):
        return jnp.einsum("cpo,io->cpi", grad, weight, preferred_element_type=F32)

    grad_down_w = weight_grad(hidden_act, grad_branch_two)
    grad_down_b = bias_grad(grad_branch_two)
    grad_act = back_dot(grad_branch_two, down_w)
    unused, gelu_back = jax.vjp(partial(jax.nn.gelu, approximate=True), hidden_pre)
    grad_pre = low(gelu_back(grad_act)[0])
    grad_up_w = weight_grad(normed_two, grad_pre)
    grad_up_b = bias_grad(grad_pre)
    grad_normed_two = back_dot(grad_pre, up_w)
    unused, norm_two_back = jax.vjp(modulate, middle, shift_two, scale_two)
    grad_middle_norm, grad_shift_two, grad_scale_two = norm_two_back(grad_normed_two)
    grad_middle = cotangent + grad_middle_norm
    grad_gate_one = jnp.sum(grad_middle * branch_one, axis=1)
    grad_branch_one = low(grad_middle * gate_one)
    grad_out_w = weight_grad(attended_low, grad_branch_one)
    grad_out_b = bias_grad(grad_branch_one)
    grad_attended = low(back_dot(grad_branch_one, out_w))
    grad_heads = as_heads(to_heads(grad_attended))
    row_delta = jnp.sum(grad_heads.astype(F32) * attended.astype(F32), axis=-1).transpose(0, 2, 1)
    grad_query, grad_keys, grad_values = attend_back(
        query, keys, values, grad_heads, log_total, row_delta, score_scale
    )

    def home(grad):
        return to_tokens(low(grad).reshape(*grad.shape[:2], -1))

    def unturned(grad):
        wide = home(grad).astype(F32).reshape(head_shape)
        return low(unrotate(wide, cosine_wide, sine_wide)).reshape(flat_shape)

    grad_qkv = jnp.concatenate(
        [unturned(grad_query), unturned(grad_keys), home(grad_values)], axis=-1
    )
    grad_qkv_w = weight_grad(normed_one, grad_qkv)
    grad_qkv_b = bias_grad(grad_qkv)
    grad_normed_one = back_dot(grad_qkv, qkv_w)
    unused, norm_one_back = jax.vjp(modulate, inputs, shift_one, scale_one)
    grad_input_norm, grad_shift_one, grad_scale_one = norm_one_back(grad_normed_one)
    grad_input = grad_middle + grad_input_norm
    grad_modulation = low(
        jnp.concatenate(
            [
                grad_shift_one[:, 0],
                grad_scale_one[:, 0],
                grad_gate_one,
                grad_shift_two[:, 0],
                grad_scale_two[:, 0],
                grad_gate_two,
            ],
            axis=-1,
        )
    )
    grad_table, grad_ada_w, grad_ada_b = frame_gradients(
        grad_modulation, one_hot, embedded, silu_in, w_ada
    )
    return (
        low(outputs),
        low(grad_input),
        grad_table,
        grad_ada_w,
        grad_ada_b,
        grad_qkv_w,
        grad_qkv_b,
        grad_out_w,
        grad_out_b,
        grad_up_w,
        grad_up_b,
        grad_down_w,
        grad_down_b,
    )


MESH_ID = pl.DeviceIdType.MESH
VMEM_LIMIT = 63 * 1024 * 1024
HEADS_WIDE = 128


def contract(left, right, left_dim, right_dim, precision=None):
    return lax.dot_general(
        left,
        right,
        (((left_dim,), (right_dim,)), ((), ())),
        preferred_element_type=F32,
        precision=precision,
    )


class Place:
    def __init__(self):
        self.dp = lax.axis_index("dp")
        self.seq = lax.axis_index("seq")
        self.z = self.seq // 2
        self.core = self.seq % 2
        self.other = 1 - self.core
        self.x_dp = self.dp + 1 - 2 * (self.dp % 2)
        self.y_dp = (self.dp + 2) % 4
        self.far_dp = 3 - self.dp
        self.dp_peers = (self.x_dp, self.y_dp, self.far_dp)
        self.seq_peers = [(self.seq + step) % 8 for step in range(1, 8)]
        self.sibling = (self.dp, self.z * 2 + self.other)
        self.z_pair = self.z + 1 - 2 * (self.z % 2)
        self.z_end = (self.z == 0) | (self.z == 3)
        self.z_middle = (self.z == 1) | (self.z == 2)
        self.z_beyond = 2 - 2 * (self.z // 2)

    def at_dp(self, dp):
        return (dp, self.seq)

    def at_seq(self, seq):
        return (self.dp, seq)

    def at_z_chip(self, z):
        return (self.dp, z * 2 + self.core)

    def greet(self):
        barrier = pltpu.get_barrier_semaphore()
        peers = [self.at_dp(dp) for dp in self.dp_peers]
        peers += [self.at_seq(seq) for seq in self.seq_peers]
        for peer in peers:
            pl.semaphore_signal(barrier, inc=1, device_id=peer, device_id_type=MESH_ID)
        pl.semaphore_wait(barrier, len(peers))


def guarded(only, act):
    if only is None:
        act()
    else:
        pl.when(only)(act)


class Copy:
    def __init__(self, wire, source, target, device, only, landing):
        self.wire, self.only = wire, only
        self.sending = wire.take_send()
        self.landing = wire.take_recv() if landing is None else landing.landing
        self.copy = wire.describe(source, target, device, self.sending, self.landing)
        guarded(only, self.copy.start)

    def wait_send(self):
        guarded(self.only, self.copy.wait_send)
        self.wire.free.append(self.sending)

    def wait_recv(self):
        self.copy.wait_recv()


class Batch:
    def __init__(self, wire, copies, whole):
        self.wire, self.copies, self.whole = wire, copies, whole
        self.landing = copies[0].landing

    def wait_recv(self):
        first = self.copies[0]
        place = self.wire.place
        self.wire.describe(
            self.whole, self.whole, place.sibling, first.sending, self.landing
        ).wait_recv()


class Wire:
    def __init__(self, place, send_sems, recv_sems):
        self.place = place
        self.send_sems = send_sems
        self.recv_sems = recv_sems
        self.sends = 0
        self.recvs = 0
        self.free = []
        self.sent = []

    def take_send(self):
        if self.free:
            return self.free.pop(0)
        self.sends += 1
        return self.sends - 1

    def take_recv(self):
        self.recvs += 1
        return self.recvs - 1

    def describe(self, source, target, device, sending, landing):
        return pltpu.make_async_remote_copy(
            src_ref=source,
            dst_ref=target,
            send_sem=self.send_sems.at[sending],
            recv_sem=self.recv_sems.at[landing],
            device_id=device,
            device_id_type=MESH_ID,
        )

    def send(self, source, target, device, only=None, landing=None):
        copy = Copy(self, source, target, device, only, landing)
        self.sent.append(copy)
        return copy

    def send_all(self, whole, parts, landing=None):
        copies = []
        for source, target, device in parts:
            copies.append(self.send(source, target, device, None, landing))
            landing = copies[0] if landing is None else landing
        return Batch(self, copies, whole)

    def drain(self, copies=None):
        copies = list(self.sent if copies is None else copies)
        for copy in copies:
            copy.wait_send()
        self.sent = [copy for copy in self.sent if not any(copy is done for done in copies)]


class Local:
    def __init__(self, sems):
        self.sems = sems
        self.used = 0

    def start(self, source, target):
        copy = pltpu.make_async_copy(source, target, self.sems.at[self.used])
        self.used += 1
        copy.start()
        return copy


def arrive(copies):
    for copy in copies:
        copy.wait_recv()


class Gather:
    def __init__(self, wire, place, ref):
        self.wire, self.place, self.ref = wire, place, ref
        self.early = None
        self.mine = []

    def send(self, source, device, only=None, landing=None):
        copy = self.wire.send(source, source, device, only, landing)
        self.mine.append(copy)
        return copy

    def batch(self, whole, parts, landing=None):
        batch = self.wire.send_all(
            whole, [(part, part, device) for part, device in parts], landing
        )
        self.mine += batch.copies
        return batch

    def along_z(self):
        place = self.place
        own = self.ref.at[place.dp, place.z, place.core]
        across = place.at_z_chip(2 - place.z // 2)
        self.paired = self.send(own, place.at_z_chip(place.z_pair))
        self.crossed = self.send(own, across)

    def pass_z(self):
        place = self.place
        two = self.ref.at[place.dp, pl.ds(place.z_beyond, 2), place.core]
        both = Batch(self.wire, [self.crossed], two)
        guarded(place.z_middle, both.wait_recv)
        self.passed = self.send(two, place.at_z_chip(place.z_pair), place.z_middle)

    def all_z(self):
        arrive([self.paired])
        guarded(self.place.z_end, self.passed.wait_recv)

    def xy_devices(self):
        place = self.place
        return [place.at_dp(dp) for dp in (place.x_dp, place.y_dp)]

    def own_xy(self):
        place = self.place
        own = self.ref.at[place.dp, place.z, place.core]
        whole = self.ref.at[pl.ds(0, 2), :, place.core]
        self.early = self.batch(whole, [(own, device) for device in self.xy_devices()])

    def along_xy(self):
        place = self.place
        self.all_z()
        if self.early:
            parts = []
            for step in (1, 2, 3):
                part = self.ref.at[place.dp, (place.z + step) % 4, place.core]
                parts += [(part, device) for device in self.xy_devices()]
            self.batch(None, parts, self.early)
            self.coming = self.early
            return
        own = self.ref.at[place.dp, :, place.core]
        whole = self.ref.at[pl.ds(0, 2), :, place.core]
        self.coming = self.batch(whole, [(own, device) for device in self.xy_devices()])

    def across(self):
        place = self.place
        arrive([self.coming])
        from_x = self.ref.at[place.x_dp, pl.ds(0, 2), place.core]
        from_y = self.ref.at[place.y_dp, pl.ds(2, 2), place.core]
        whole = self.ref.at[0, :, place.core]
        to_x, to_y = self.xy_devices()
        self.coming = self.batch(whole, [(from_x, to_y), (from_y, to_x)])

    def to_sibling(self):
        place = self.place
        arrive([self.coming])
        self.coming = self.send(self.ref.at[:, :, place.core], place.sibling)

    def finish(self):
        arrive([self.coming])
        self.wire.drain(self.mine)


class SmallGather:
    def __init__(self, wire, place, ref):
        self.wire, self.place, self.ref = wire, place, ref

    def along_seq(self):
        place = self.place
        own = self.ref.at[place.dp, place.seq]
        self.seq_coming = self.wire.send_all(
            self.ref.at[0, pl.ds(0, 7)],
            [(own, own, place.at_seq(seq)) for seq in place.seq_peers],
        )

    def along_dp(self):
        place = self.place
        arrive([self.seq_coming])
        own = self.ref.at[place.dp]
        self.dp_coming = self.wire.send_all(
            self.ref.at[pl.ds(0, 3)], [(own, own, place.at_dp(dp)) for dp in place.dp_peers]
        )

    def finish(self):
        arrive([self.dp_coming])
        self.wire.drain(self.seq_coming.copies + self.dp_coming.copies)


def spread_dp(wire, place, part_of, slots):
    parts = [
        (part_of(dp), slots.at[index], place.at_dp(dp)) for index, dp in enumerate(place.dp_peers)
    ]
    return wire.send_all(slots, parts)


def spread_seq(wire, place, part_of, slots):
    parts = [
        (part_of(seq), slots.at[index], place.at_seq(seq))
        for index, seq in enumerate(place.seq_peers)
    ]
    return wire.send_all(slots, parts)


def collect(batch):
    arrive([batch])
    batch.wire.drain(batch.copies)


def total_of(own, slots, count):
    total = own
    for index in range(count):
        total = total + slots[index].astype(F32)
    return total


def row_of(lines, first):
    return jnp.concatenate([lines[first + line : first + line + 1, :] for line in range(8)], axis=1)


def lines_of(row):
    return jnp.concatenate([row[:, 128 * line : 128 * (line + 1)] for line in range(8)], axis=0)


def whole_piece(piece):
    value = piece[...]
    return value.reshape(-1, value.shape[-1])


def norm_parts(values):
    centred = values - jnp.mean(values, axis=1, keepdims=True)
    inverse = lax.rsqrt(jnp.mean(centred * centred, axis=1, keepdims=True) + norm_eps)
    return centred * inverse, inverse


def half_turn(values):
    lane = lax.broadcasted_iota(jnp.int32, values.shape, 1) % 64
    in_time = lane < 16
    first = (lane < 8) | ((lane >= 16) & (lane < 28)) | ((lane >= 40) & (lane < 52))
    up = jnp.where(in_time, pltpu.roll(values, 120, 1), pltpu.roll(values, 116, 1))
    down = jnp.where(in_time, pltpu.roll(values, 8, 1), pltpu.roll(values, 12, 1))
    return jnp.where(first, up, down)


def split_heads(values):
    lane = lax.broadcasted_iota(jnp.int32, values.shape, 1)
    empty = jnp.zeros_like(values)
    return jnp.concatenate(
        [jnp.where(lane < 64, values, empty), jnp.where(lane < 64, empty, values)], axis=0
    )


def join_heads(turned):
    return jnp.concatenate([turned[:64, :256], turned[64:, 256:]], axis=0).T


def attend_frame(frame, query, keys, values, attended, log_total, scores):
    pair = split_heads(query[frame])
    row_max = None
    for block in range(frame + 1):
        block_scores = contract(keys[block], pair, 1, 1)
        scores[block] = block_scores
        block_max = jnp.max(block_scores, axis=0, keepdims=True)
        row_max = block_max if row_max is None else jnp.maximum(row_max, block_max)
    row_total = None
    weighted = None
    for block in range(frame + 1):
        exponent = jnp.exp(scores[block] - row_max)
        block_total = jnp.sum(exponent, axis=0, keepdims=True)
        block_sum = contract(values[block], exponent.astype(BF16), 0, 0)
        row_total = block_total if row_total is None else row_total + block_total
        weighted = block_sum if weighted is None else weighted + block_sum
    attended[frame] = join_heads(weighted / row_total).astype(BF16)
    log_total[frame] = row_max + jnp.log(row_total)


SQRT_TWO_OVER_PI = math.sqrt(2.0 / math.pi)


def gelu_parts(values):
    square = values * values
    bent = jnp.tanh(SQRT_TWO_OVER_PI * values * (1.0 + 0.044715 * square))
    half = 0.5 * (1.0 + bent)
    slope = half + 0.5 * values * (1.0 - bent * bent) * (
        SQRT_TWO_OVER_PI * (1.0 + 3.0 * 0.044715 * square)
    )
    return values * half, slope


def rope_in_kernel(frame):
    lane = lax.broadcasted_iota(jnp.int32, (256, 128), 1) % 64
    patch = lax.broadcasted_iota(jnp.int32, (256, 128), 0)
    in_time, in_rows = lane < 16, lane < 40
    half = jnp.where(in_time, 8, 12)
    step = jnp.where(in_time, lane, jnp.where(in_rows, lane - 16, lane - 40))
    second = step >= half
    step = jnp.where(second, step - half, step).astype(F32)
    position = jnp.where(in_time, frame, jnp.where(in_rows, patch // GRID_W, patch % GRID_W))
    rate = jnp.exp(-math.log(10000.0) * step / half.astype(F32))
    angle = position.astype(F32) * rate
    sine = jnp.sin(angle)
    return jnp.cos(angle), jnp.where(second, sine, -sine)


BIAS_FIRST = (0, 24, 32, 64, 72)
BIAS_SHARE = (96, 32, 128, 32, 192)


def every_bias(blocks, lines):
    lane = lax.broadcasted_iota(jnp.int32, (8, 128), 1)

    def take(line, first, every):
        return blocks[pl.ds(8 * first + line, 32 // every, stride=8 * every), :]

    def moved(values, lanes):
        return pltpu.roll(values, lanes % 128, 1)

    mixed = [take(2, first, 4) for first in range(4)]
    lines[pl.ds(0, 8, stride=3), :] = jnp.where(lane < 96, mixed[0], moved(mixed[1], 96))
    lines[pl.ds(1, 8, stride=3), :] = jnp.where(lane < 64, moved(mixed[1], 96), moved(mixed[2], 64))
    lines[pl.ds(2, 8, stride=3), :] = jnp.where(lane < 32, moved(mixed[2], 64), moved(mixed[3], 32))

    def quarters(parts, first_lane):
        total = jnp.zeros((8, 128), F32)
        for index, part in enumerate(parts):
            here = (lane >= 32 * index) & (lane < 32 * (index + 1))
            total = jnp.where(here, moved(part, 32 * index - first_lane), total)
        return total

    lines[24:32, :] = quarters(mixed, 96)
    lines[32:64, :] = take(1, 0, 1)
    lines[64:72, :] = quarters([take(4, first, 4) for first in range(4)], 64)
    left = lax.broadcasted_iota(jnp.int32, (16, 128), 1) < 64
    even, odd = take(3, 0, 2), take(3, 1, 2)
    even_rest, odd_rest = take(4, 0, 2), take(4, 1, 2)
    lines[pl.ds(72, 16, stride=3), :] = even
    lines[pl.ds(73, 16, stride=3), :] = jnp.where(left, even_rest, moved(odd, 64))
    lines[pl.ds(74, 16, stride=3), :] = jnp.where(left, moved(odd, 64), moved(odd_rest, 64))


def pack_lanes(rows):
    packed = rows[:, 0]
    for part in range(1, 4):
        packed = packed + pltpu.roll(rows[:, part], 32 * part, 2)
    return packed


def unpack_lanes(packed):
    lane = lax.broadcasted_iota(jnp.int32, packed.shape, packed.ndim - 1)
    parts = [packed] + [pltpu.roll(packed, 128 - 32 * part, 1) for part in range(1, 4)]
    return jnp.concatenate([jnp.where(lane < 32, part, 0.0) for part in parts], axis=0)


def forward_kernel(
    x_ref,
    level_ref,
    table_ref,
    b_qkv_ref,
    b_out_ref,
    b_up_ref,
    b_down_ref,
    b_ada_ref,
    w_qkv_ref,
    w_out_in,
    w_up_in,
    w_down_in,
    w_ada_in,
    cotangent_in,
    layer_out_ref,
    log_total_ref,
    modulation_ref,
    embedded_ref,
    one_hot_ref,
    gate_two_grad_ref,
    wide_out,
    down_out,
    query_out,
    keys_out,
    values_out,
    attended_out,
    tokens_out,
    normed_one_out,
    normed_two_out,
    middle_out,
    branch_one_out,
    act_out,
    slope_out,
    cosine_out,
    sine_out,
    query_ref,
    keys_ref,
    values_ref,
    attended_ref,
    attended_tokens,
    normed_one_ref,
    normed_two_ref,
    middle_ref,
    branch_one_ref,
    act_ref,
    slope_ref,
    cosine_ref,
    sine_ref,
    w_out_ref,
    w_up_ref,
    w_down_ref,
    w_ada_ref,
    cotangent_ref,
    wide,
    down,
    levels,
    found,
    found_dp,
    found_sum,
    found_seq,
    partial_mod,
    mod_dp,
    mod_sum,
    mod_blocks,
    mod_seq,
    bias_lines,
    blocks,
    own_block,
    flat,
    scores,
    send_sems,
    recv_sems,
    back_send,
    back_recv,
    local_sems,
):
    place = Place()
    wire = Wire(place, send_sems, recv_sems)
    dp, seq, z, core = place.dp, place.seq, place.z, place.core
    device = dp * 8 + seq
    local = Local(local_sems)
    loads = [
        local.start(source, target)
        for source, target in (
            (w_ada_in, w_ada_ref),
            (w_out_in, w_out_ref),
            (w_up_in, w_up_ref),
            (w_down_in, w_down_ref),
            (cotangent_in, cotangent_ref),
        )
    ]
    own_block[...] = jnp.full((8, 128), level_ref[0, 0].astype(F32), F32)

    def place_bias(line, lane, ref, first, share):
        values = low(ref[first : first + share]).astype(F32)
        own_block[line : line + 1, lane : lane + share] = values.reshape(1, share)

    place_bias(1, 0, b_up_ref, 0, 128)
    place_bias(2, 0, b_qkv_ref, 0, 96)
    place_bias(2, 96, b_out_ref, 0, 32)
    place_bias(3, 0, b_ada_ref, 0, 128)
    place_bias(4, 0, b_ada_ref, 128, 64)
    place_bias(4, 64, b_down_ref, 0, 32)
    levels[dp, seq] = own_block[...]
    wide[0, dp, z, core] = low(w_qkv_ref[:, :1024])
    place.greet()
    level_gather = SmallGather(wire, place, levels)
    level_gather.along_seq()
    pieces = [Gather(wire, place, wide.at[index]) for index in range(8)]
    pieces += [Gather(wire, place, down.at[index]) for index in range(4)]
    pieces[0].along_z()
    pieces[0].own_xy()
    for block in (1, 2):
        wide[block, dp, z, core] = low(w_qkv_ref[:, 1024 * block : 1024 * (block + 1)])
        pieces[block].own_xy()
    saved = []

    def save(index):
        pieces[index].finish()
        source, target = (
            (wide.at[index], wide_out.at[index])
            if index < 8
            else (down.at[index - 8], down_out.at[index - 8])
        )
        saved.append(local.start(source, target))

    def keep(source, target):
        saved.append(local.start(source, target))

    started = [2]
    passed = [4]

    def start_z(last):
        while started[0] <= min(last, 11):
            pieces[started[0]].along_z()
            started[0] += 1

    def pass_z(last):
        while passed[0] <= min(last, 11):
            pieces[passed[0]].pass_z()
            passed[0] += 1

    def links(step):
        pass_z((0, 0, 0, 5, 7, 8, 9, 9)[step] if step < 8 else step)
        start_z((0, 0, 0, 9, 9, 9, 9, 9, 10, 11)[min(step, 9)])
        if step < 12:
            pieces[step].along_xy()
        if step - 1 < 12:
            pieces[step - 1].across()
        if step > 8:
            pass_z(step + 1)

    def tick(step):
        links(step)
        pieces[step - 2].to_sibling()
        save(step - 3)

    x = x_ref[...].astype(F32)
    normed, unused = norm_parts(x)
    flat[0] = normed
    level_gather.along_dp()
    pieces[1].along_z()
    start_z(2)
    level_gather.finish()
    level_rows = jnp.concatenate(
        [levels[group, frame, 0:1, :] for group in range(4) for frame in range(8)]
        + [jnp.full((96, 128), -1.0, F32)],
        axis=0,
    )
    lane = lax.broadcasted_iota(jnp.int32, (128, 128), 1)
    own_level = (lane + device * 32).astype(F32)
    one_hot = jnp.where((level_rows == own_level) & (lane < 32), 1.0, 0.0)
    one_hot_ref[...] = one_hot
    one_hot_turned = low(one_hot.T)[:32, :]
    rows = contract(low(table_ref[...]), one_hot_turned, 0, 0).reshape(32, 4, 8, 128)
    found[...] = pack_lanes(rows).reshape(found.shape)
    found_copies = spread_dp(wire, place, lambda dp: found.at[dp], found_dp)
    for copy in loads:
        copy.wait()
    wide[3, dp, z, core] = low(w_out_ref[...])
    for block in range(4):
        wide[4 + block, dp, z, core] = low(w_up_ref[:, 1024 * block : 1024 * (block + 1)])
    for block in range(4):
        down[block, dp, z, core] = low(w_down_ref[:, 256 * block : 256 * (block + 1)])
    start_z(3)
    for block in (3, 4, 5):
        pieces[block].own_xy()
    pieces[0].pass_z()
    pieces[0].along_xy()
    collect(found_copies)
    found_sum[...] = total_of(found[dp], found_dp, 3)
    found_copies = spread_seq(wire, place, lambda seq: found_sum.at[seq], found_seq)
    pieces[1].pass_z()
    start_z(5)
    pieces[1].along_xy()
    cosine, sine = rope_in_kernel(seq)
    cosine_ref[...] = cosine
    sine_ref[...] = sine
    keep(cosine_ref, cosine_out)
    keep(sine_ref, sine_out)
    pieces[0].across()
    collect(found_copies)
    embedded = unpack_lanes(total_of(found_sum[seq], found_seq, 7))
    embedded_ref[...] = embedded
    silu_in = low(embedded / (1.0 + jnp.exp(-embedded)))
    for block in range(6):
        part = contract(silu_in, low(w_ada_ref[:, 1024 * block : 1024 * (block + 1)]), 0, 0)
        lines = [part[:32, 128 * line : 128 * (line + 1)].reshape(4, 8, 128) for line in range(8)]
        for pair in range(4):
            both = jnp.concatenate(lines[2 * pair : 2 * pair + 2], axis=1)
            partial_mod[4 * block + pair] = low(both)
    mod_copies = spread_dp(wire, place, lambda dp: partial_mod.at[:, dp], mod_dp)
    blocks[...] = levels[...].reshape(256, 128)
    every_bias(blocks, bias_lines)
    pieces[2].pass_z()
    pieces[3].pass_z()
    start_z(7)
    pieces[2].along_xy()
    pieces[1].across()
    pieces[0].to_sibling()
    collect(mod_copies)
    mod_sum[...] = total_of(partial_mod[:, dp].astype(F32), mod_dp, 3).reshape(384, 128)
    for frame in range(8):
        mod_blocks[frame] = mod_sum[pl.ds(frame, 48, stride=8), :]
    mod_copies = spread_seq(wire, place, lambda seq: mod_blocks.at[seq], mod_seq)
    tick(3)
    biases = bias_lines[...]
    collect(mod_copies)
    modulation = total_of(mod_blocks[seq], mod_seq, 7) + biases[72:120]
    for block in range(6):
        modulation_ref[block : block + 1, :] = row_of(modulation, 8 * block)
    shift_one = modulation_ref[0:1, :]
    scale_one = modulation_ref[1:2, :]
    gate_one = modulation_ref[2:3, :]
    shift_two = modulation_ref[3:4, :]
    scale_two = modulation_ref[4:5, :]
    gate_two = modulation_ref[5:6, :]
    normed_one_ref[...] = low(flat[0] * (1.0 + scale_one) + shift_one)
    keep(normed_one_ref, normed_one_out)
    cosine = cosine_ref[...]
    sine = sine_ref[...]
    head_copies = []

    def project(block, target):
        r = contract(normed_one_ref[...], whole_piece(wide.at[block]), 1, 0)
        r = r + row_of(biases, 8 * block)
        for group in range(8):
            part = r[:, 128 * group : 128 * (group + 1)]
            if block < 2:
                part = part * cosine + half_turn(part) * sine
            if block == 0:
                part = part * 0.125
            act_ref[:, 1024 * block + 128 * group : 1024 * block + 128 * (group + 1)] = low(part)
        parts = []
        for other in place.seq_peers:
            columns = pl.ds(pl.multiple_of(1024 * block + other * 128, 128), 128)
            parts.append((act_ref.at[:, columns], target.at[seq], place.at_seq(other)))
        head_copies.append(wire.send_all(target.at[pl.ds(0, 7)], parts))
        columns = pl.ds(pl.multiple_of(1024 * block + seq * 128, 128), 128)
        target[seq] = act_ref[:, columns]

    project(0, query_ref)
    tick(4)
    project(1, keys_ref)
    tick(5)
    project(2, values_ref)
    tick(6)
    tick(7)
    tick(8)
    arrive(head_copies)
    keep(query_ref, query_out)
    keep(keys_ref, keys_out)
    keep(values_ref, values_out)

    def back_copy(frame, source):
        columns = pl.ds(pl.multiple_of(source * 128, 128), 128)
        return pltpu.make_async_remote_copy(
            src_ref=attended_ref.at[frame],
            dst_ref=attended_tokens.at[:, columns],
            send_sem=back_send.at[frame],
            recv_sem=back_recv.at[source],
            device_id=place.at_seq(frame),
            device_id_type=MESH_ID,
        )

    def send_back(frame):
        @pl.when(seq != frame)
        def _():
            back_copy(frame, seq).start()

        @pl.when(seq == frame)
        def _():
            columns = pl.ds(pl.multiple_of(seq * 128, 128), 128)
            attended_tokens[:, columns] = attended_ref[frame]

    for frame in (7, 0, 6, 1, 5, 2, 4, 3):
        attend_frame(
            frame, query_ref, keys_ref, values_ref, attended_ref, log_total_ref, scores
        )
        send_back(frame)
        if frame == 1:
            links(9)
    keep(attended_ref, attended_out)
    links(10)
    pieces[7].to_sibling()
    save(6)
    for other in place.seq_peers:
        back_copy(other, other).wait_recv()
    for other in place.seq_peers:
        back_copy(other, other).wait_send()
    keep(attended_tokens, tokens_out)
    for batch in head_copies:
        wire.drain(batch.copies)
    branch_one = contract(attended_tokens[...], whole_piece(wide.at[3]), 1, 0)
    branch_one = branch_one + row_of(biases, 24)
    branch_one_ref[...] = branch_one
    keep(branch_one_ref, branch_one_out)
    middle = x_ref[...].astype(F32) + gate_one * branch_one
    middle_ref[...] = middle
    keep(middle_ref, middle_out)
    normed, unused = norm_parts(middle)
    normed_two_ref[...] = low(normed * (1.0 + scale_two) + shift_two)
    keep(normed_two_ref, normed_two_out)
    links(11)
    pieces[8].to_sibling()
    save(7)
    for block in range(4):
        if block == 3:
            links(12)
            pieces[9].to_sibling()
            save(8)
        pre = contract(normed_two_ref[...], whole_piece(wide.at[4 + block]), 1, 0)
        act, slope = gelu_parts(pre + row_of(biases, 32 + 8 * block))
        act_ref[:, 1024 * block : 1024 * (block + 1)] = low(act)
        slope_ref[:, 1024 * block : 1024 * (block + 1)] = low(slope)
    keep(act_ref, act_out)
    keep(slope_ref, slope_out)
    for block in range(4):
        if block == 0:
            pieces[10].to_sibling()
        elif block == 1:
            pieces[11].to_sibling()
            save(9)
        else:
            save(8 + block)
        flat[0, :, 256 * block : 256 * (block + 1)] = contract(
            act_ref[...], whole_piece(down.at[block]), 1, 0
        )
    branch_two = flat[0] + row_of(biases, 64)
    layer_out_ref[...] = low(middle_ref[...] + gate_two * branch_two)
    gate_two_grad_ref[...] = jnp.sum(
        cotangent_ref[...].astype(F32) * branch_two, axis=0, keepdims=True
    )
    wire.drain()
    for copy in saved:
        copy.wait()


def vmem(shape, dtype=F32):
    return pltpu.VMEM(shape, dtype)


def run_forward(x, level, table, biases, w_qkv, w_out, w_up, w_down, w_ada, cotangent):
    shape = jax.ShapeDtypeStruct
    small = [
        ((256, 1024), BF16),
        ((8, 1, 512), F32),
        ((8, 1024), F32),
        ((32, 128), F32),
        ((128, 128), F32),
        ((1, 1024), F32),
    ]
    gathered = [((8, 4, 4, 2, 32, 1024), BF16), ((4, 4, 4, 2, 128, 256), BF16)]
    kept = (
        [((8, 256, 128), BF16)] * 4
        + [((256, 1024), BF16)] * 3
        + [((256, 1024), F32)] * 2
        + [((256, 4096), BF16)] * 2
        + [((256, 128), F32)] * 2
    )
    fetched = [
        ((32, 1024), F32),
        ((32, 4096), F32),
        ((128, 1024), F32),
        ((32, 6144), F32),
        ((256, 1024), BF16),
    ]
    in_vmem = pl.BlockSpec(memory_space=pltpu.VMEM)
    anywhere = pl.BlockSpec(memory_space=pl.ANY)
    scratch = [vmem(*array) for array in kept + fetched + gathered]
    scratch += [
        vmem((4, 8, 8, 128)),
        vmem((4, 8, 8, 128)),
        vmem((3, 8, 8, 128)),
        vmem((8, 8, 128)),
        vmem((7, 8, 128)),
        vmem((24, 4, 16, 128), BF16),
        vmem((3, 24, 16, 128), BF16),
        vmem((384, 128)),
        vmem((8, 48, 128)),
        vmem((7, 48, 128)),
        vmem((120, 128)),
        vmem((256, 128)),
        vmem((8, 128)),
        vmem((1, 256, 1024)),
        vmem((8, 256, 512)),
        pltpu.SemaphoreType.DMA((78,)),
        pltpu.SemaphoreType.DMA((82,)),
        pltpu.SemaphoreType.DMA((8,)),
        pltpu.SemaphoreType.DMA((8,)),
        pltpu.SemaphoreType.DMA((32,)),
    ]
    return pl.pallas_call(
        forward_kernel,
        out_shape=[shape(*out) for out in small + gathered + kept],
        in_specs=[in_vmem, pl.BlockSpec(memory_space=pltpu.SMEM)] + [in_vmem] * 7 + [anywhere] * 5,
        out_specs=[in_vmem] * len(small) + [anywhere] * len(gathered + kept),
        scratch_shapes=scratch,
        compiler_params=pltpu.CompilerParams(
            collective_id=0, has_side_effects=True, vmem_limit_bytes=VMEM_LIMIT
        ),
        name="block_forward",
    )(x, level, table, *biases, w_qkv, w_out, w_up, w_down, w_ada, cotangent)


SLOTS = 5


class Scatter:
    def __init__(self, wire, place, index, terms, buffers, credit, finish):
        self.wire, self.place, self.index, self.terms = wire, place, index, terms
        from_core, from_far, from_xy, from_z = buffers
        self.from_core = from_core.at[index % SLOTS]
        self.from_far = from_far.at[index]
        self.from_xy = from_xy.at[index]
        self.from_z = from_z.at[index]
        self.credit, self.finish = credit, finish
        self.mine = []

    def send(self, source, target, device, only=None, landing=None):
        copy = self.wire.send(source, target, device, only, landing)
        self.mine.append(copy)
        return copy

    def batch(self, whole, parts, landing=None):
        batch = self.wire.send_all(whole, parts, landing)
        self.mine += batch.copies
        return batch

    def to_sibling(self):
        place = self.place
        if self.index >= SLOTS:
            pl.semaphore_wait(self.credit, 1)
        self.coming = [
            self.send(self.terms.at[:, :, place.other], self.from_core, place.sibling)
        ]

    def across(self, last):
        place, terms, core = self.place, self.terms, self.place.core
        arrive(self.coming)
        far = place.far_dp
        terms[far, :, core] = terms[far, :, core] + self.from_core[far]
        to_x, to_y = place.at_dp(place.x_dp), place.at_dp(place.y_dp)
        parts = [
            (terms.at[far, pl.ds(0, 2), core], self.from_far.at[0], to_x),
            (terms.at[far, pl.ds(2, 2), core], self.from_far.at[1], to_y),
        ]
        self.coming = [self.batch(self.from_far, parts)]
        for group in (place.x_dp, place.y_dp, place.dp):
            terms[group, :, core] = terms[group, :, core] + self.from_core[group]
        if not last:
            pl.semaphore_signal(
                self.credit, inc=1, device_id=place.sibling, device_id_type=MESH_ID
            )

    def along_xy(self):
        place, terms, core = self.place, self.terms, self.place.core
        arrive(self.coming)
        first, second = pl.ds(0, 2), pl.ds(2, 2)
        terms[place.y_dp, first, core] = terms[place.y_dp, first, core] + self.from_far[0]
        terms[place.x_dp, second, core] = terms[place.x_dp, second, core] + self.from_far[1]
        parts = [
            (terms.at[dp, :, core], self.from_xy.at[slot], place.at_dp(dp))
            for slot, dp in enumerate((place.x_dp, place.y_dp))
        ]
        self.coming = [self.batch(self.from_xy, parts)]

    def gather_shares(self):
        place, terms, core = self.place, self.terms, self.place.core
        arrive(self.coming)
        own = terms[place.dp, :, core].astype(F32)
        self.shares = self.from_xy.at[0]
        self.shares[...] = low(total_of(own, self.from_xy, 2))
        self.wire.drain(self.mine)
        self.mine = []

    def along_z(self):
        place, shares = self.place, self.shares
        pair = place.at_z_chip(place.z_pair)
        beyond = shares.at[pl.ds(place.z_beyond, 2)]
        self.first = self.send(shares.at[place.z_pair], self.from_z.at[0], pair)
        self.carried = self.send(beyond, self.from_z.at[pl.ds(2, 2)], pair, place.z_end)

    def pass_z(self):
        place, shares = self.place, self.shares

        @pl.when(place.z_middle)
        def _():
            self.carried.wait_recv()
            beyond = shares.at[pl.ds(place.z_beyond, 2)]
            beyond[...] = beyond[...] + self.from_z[2:4]

        self.second = None
        for z in ((place.z + 2) % 4, 3 - place.z):
            self.second = self.send(
                shares.at[z],
                self.from_z.at[1],
                place.at_z_chip(z),
                place.z_middle,
                landing=self.second,
            )

    def end(self):
        arrive([self.first, self.second])
        own = self.shares[self.place.z].astype(F32)
        self.finish(total_of(own, self.from_z, 2))
        self.wire.drain(self.mine)


def norm_back(normed, inverse, grad):
    mean = jnp.mean(grad, axis=1, keepdims=True)
    along = jnp.mean(grad * normed, axis=1, keepdims=True)
    return (grad - mean - normed * along) * inverse


def column_sum(values):
    return jnp.sum(values, axis=0, keepdims=True)


def pair_deltas(attended, grad_heads, deltas):
    lane = lax.broadcasted_iota(jnp.int32, (8, 128), 1)
    line = lax.broadcasted_iota(jnp.int32, (8, 128), 0)
    picked = jnp.where(lane // 64 == line, 1.0, 0.0).astype(F32)
    for frame in range(8):
        product = attended[frame].astype(F32) * grad_heads[frame].astype(F32)
        sums = contract(picked, product, 1, 1, precision=lax.Precision.HIGHEST)
        deltas[frame] = jnp.concatenate([sums[0:1], sums[1:2]], axis=1)


def frame_pairs():
    for first in range(4):
        last = 7 - first
        yield [(query, first) for query in range(first, last + 1)], first
        yield [(last, key) for key in range(first + 1, last + 1)], last


def attend_pair_back(query_frame, key_frame, heads, log_total, grad_heads, deltas, sums, fresh):
    query, keys, values = heads
    pair = split_heads(query[query_frame])
    grad_pair = split_heads(grad_heads[query_frame])
    weights = jnp.exp(contract(keys[key_frame], pair, 1, 1) - log_total[query_frame])
    grad_weights = contract(values[key_frame], grad_pair, 1, 1)
    grad_scores = low(weights * (grad_weights - deltas[query_frame]))
    turned = contract(keys[key_frame], grad_scores, 0, 0)
    parts = (
        (query_frame, jnp.concatenate([turned[:64, :256], turned[64:, 256:]], axis=0)),
        (key_frame, contract(grad_scores, pair, 1, 0)),
        (key_frame, contract(low(weights), grad_pair, 1, 0)),
    )
    for total, (frame, part), started in zip(sums, parts, fresh):
        if frame in started:
            total[frame] += part
        else:
            started.add(frame)
            total[frame] = part


def backward_kernel(
    cotangent_ref,
    log_total_ref,
    modulation_ref,
    embedded_ref,
    one_hot_ref,
    gate_two_grad_ref,
    wide,
    down,
    act_in,
    slope_in,
    normed_two_in,
    middle_in,
    branch_one_in,
    query_in,
    keys_in,
    values_in,
    attended_in,
    tokens_in,
    x_in,
    normed_one_in,
    cosine_in,
    sine_in,
    w_ada_in,
    grad_hidden_ref,
    grad_table_ref,
    grad_ada_ref,
    grad_ada_bias_ref,
    grad_qkv_ref,
    grad_out_ref,
    grad_up_ref,
    grad_down_ref,
    grad_bias_ref,
    hidden,
    slope_ref,
    normed_two_ref,
    middle_ref,
    branch_one_ref,
    query_ref,
    keys_ref,
    values_ref,
    attended_ref,
    attended_tokens,
    x_ref,
    normed_one_ref,
    cosine_ref,
    sine_ref,
    w_ada_ref,
    terms,
    from_core,
    from_far,
    from_xy,
    from_z,
    down_block,
    wide_block,
    grad_two,
    grad_one,
    grad_tokens,
    grad_heads,
    deltas,
    query_sum,
    keys_sum,
    values_sum,
    query_back,
    keys_back,
    values_back,
    qkv_back,
    running,
    bias_lines,
    bias_dp,
    bias_sum,
    bias_seq,
    mod_grads,
    mod_lines,
    embedded_grads,
    send_sems,
    recv_sems,
    back_send,
    back_recv,
    local_sems,
    credit,
):
    place = Place()
    wire = Wire(place, send_sems, recv_sems)
    dp, seq, core = place.dp, place.seq, place.core
    loads = {}
    local = Local(local_sems)

    def load(name, source, target):
        loads[name] = local.start(source, target)

    def load_down(block):
        load(("down", block), down.at[:, block], down_block)

    def load_wide(block):
        load(("wide", block), wide.at[block], wide_block.at[block % 2])

    load("act", act_in, hidden)
    load_down(0)
    load("slope", slope_in, slope_ref)
    load_wide(4)
    load_wide(5)
    later = (
        (normed_two_in, normed_two_ref),
        (middle_in, middle_ref),
        (branch_one_in, branch_one_ref),
        (query_in, query_ref),
        (keys_in, keys_ref),
        (values_in, values_ref),
        (attended_in, attended_ref),
        (tokens_in, attended_tokens),
        (x_in, x_ref),
        (normed_one_in, normed_one_ref),
        (cosine_in, cosine_ref),
        (sine_in, sine_ref),
        (w_ada_in, w_ada_ref),
    )
    for index, (source, target) in enumerate(later):
        load(index, source, target)
    place.greet()
    scale_one = modulation_ref[1:2, :]
    gate_one = modulation_ref[2:3, :]
    scale_two = modulation_ref[4:5, :]
    gate_two = modulation_ref[5:6, :]
    cotangent = cotangent_ref[...].astype(F32)
    grad_two[...] = low(cotangent * gate_two)

    def keep_bias(first, grad):
        bias_lines[first : first + 8, :] = lines_of(column_sum(grad.astype(F32)))

    bias_lines[72:80, :] = jnp.zeros((8, 128), F32)
    keep_bias(64, grad_two[...])

    def finish(index):
        def store(total):
            if index < 4:
                grad_down_ref[32 * index : 32 * (index + 1), :] = total
            elif index < 8:
                grad_up_ref[:, 1024 * (index - 4) : 1024 * (index - 3)] = total
            elif index == 8:
                grad_out_ref[...] = total
            else:
                grad_qkv_ref[:, 1024 * (index - 9) : 1024 * (index - 8)] = total

        return store

    buffers = (from_core, from_far, from_xy, from_z)
    pieces = [
        Scatter(
            wire, place, index, terms.at[index % SLOTS], buffers, credit, finish(index)
        )
        for index in range(12)
    ]
    loads["act"].wait()
    for chunk in range(16):
        part = low(contract(hidden[:, 256 * chunk : 256 * (chunk + 1)], grad_two[...], 0, 0))
        part = part.reshape(2, 4, 32, 1024)
        for index in range(4):
            terms[index, chunk // 4, chunk % 4] = part[:, index]

    def make_terms(index):
        if index < 4:
            return
        for group in range(4):
            rows = slice(256 * group, 256 * (group + 1))
            if index < 8:
                left = normed_two_ref[:, rows]
                right = hidden[:, 1024 * (index - 4) : 1024 * (index - 3)]
            elif index == 8:
                left, right = attended_tokens[:, rows], grad_one[...]
            else:
                left, right = normed_one_ref[:, rows], qkv_back[index - 9]
            part = low(contract(left, right, 0, 0))
            terms[index % SLOTS, group] = part.reshape(4, 2, 32, 1024)

    done = [0, 0, 0]

    def tick(step):
        if 0 <= step - 1 < 12:
            pieces[step - 1].across(step - 1 + SLOTS >= 12)
        if 0 <= step - 3 < 12:
            pieces[step - 3].along_xy()
        if 0 <= step - 5 < 12:
            pieces[step - 5].gather_shares()
        if step < 12:
            make_terms(step)
            pieces[step].to_sibling()

    def settle(sent, passed, ended):
        for stage, last in enumerate((sent, passed, ended)):
            while done[stage] <= min(last, 11):
                piece = pieces[done[stage]]
                (piece.along_z, piece.pass_z, piece.end)[stage]()
                done[stage] += 1

    tick(0)
    tick(1)
    loads["slope"].wait()
    for block in range(4):
        loads[("down", block)].wait()
        grad_act = None
        for index in range(4):
            weight = down_block[index].reshape(1024, 256)
            part = contract(grad_two[:, 256 * index : 256 * (index + 1)], weight, 1, 1)
            grad_act = part if grad_act is None else grad_act + part
        if block < 3:
            load_down(block + 1)
        columns = slice(1024 * block, 1024 * (block + 1))
        grad_pre = low(grad_act * slope_ref[:, columns].astype(F32))
        hidden[:, columns] = grad_pre
        keep_bias(32 + 8 * block, grad_pre)
        loads[("wide", 4 + block)].wait()
        part = contract(grad_pre, whole_piece(wide_block.at[block % 2]), 1, 1)
        running[...] = part if block == 0 else running[...] + part
        load_wide((6, 7, 2, 3)[block])
        if block == 1:
            tick(2)
    for index in range(len(later)):
        loads[index].wait()
    normed, inverse = norm_parts(middle_ref[...])
    grad_normed = running[...]
    grad_shift_two = column_sum(grad_normed)
    grad_scale_two = column_sum(grad_normed * normed)
    grad_middle = cotangent_ref[...].astype(F32) + norm_back(
        normed, inverse, grad_normed * (1.0 + scale_two)
    )
    running[...] = grad_middle
    grad_gate_one = column_sum(grad_middle * branch_one_ref[...])
    grad_one[...] = low(grad_middle * gate_one)
    keep_bias(24, grad_one[...])
    loads[("wide", 3)].wait()
    grad_tokens[...] = low(contract(grad_one[...], whole_piece(wide_block.at[1]), 1, 1))
    load_wide(1)
    parts = []
    for other in place.seq_peers:
        columns = pl.ds(pl.multiple_of(other * 128, 128), 128)
        parts.append((grad_tokens.at[:, columns], grad_heads.at[seq], place.at_seq(other)))
    head_copies = wire.send_all(grad_heads.at[pl.ds(0, 7)], parts)
    own_columns = pl.ds(pl.multiple_of(seq * 128, 128), 128)
    grad_heads[seq] = grad_tokens[:, own_columns]
    tick(3)
    tick(4)
    collect(head_copies)
    backs = (query_back, keys_back, values_back)

    def back_copy(part, frame, source):
        columns = pl.ds(pl.multiple_of(source * 128, 128), 128)
        return pltpu.make_async_remote_copy(
            src_ref=backs[part].at[frame],
            dst_ref=qkv_back.at[part, :, columns],
            send_sem=back_send.at[part, frame],
            recv_sem=back_recv.at[part, source],
            device_id=place.at_seq(frame),
            device_id_type=MESH_ID,
        )

    def send_back(frame):
        @pl.when(seq != frame)
        def _():
            for part in range(3):
                back_copy(part, frame, seq).start()

        @pl.when(seq == frame)
        def _():
            for part in range(3):
                qkv_back[part, :, own_columns] = backs[part][frame]

    pair_deltas(attended_ref, grad_heads, deltas)
    heads = (query_ref, keys_ref, values_ref)
    fresh = (set(), set(), set())
    for pairs, frame in frame_pairs():
        for query_frame, key_frame in pairs:
            attend_pair_back(
                query_frame,
                key_frame,
                heads,
                log_total_ref,
                grad_heads,
                deltas,
                (query_sum, keys_sum, values_sum),
                fresh,
            )
        query_back[frame] = low(query_sum[frame].T * 0.125)
        keys_back[frame] = low(keys_sum[frame])
        values_back[frame] = low(values_sum[frame])
        send_back(frame)
        if frame in (7, 2):
            tick(5 if frame == 7 else 6)
    tick(7)
    tick(8)
    for part in range(3):
        for other in place.seq_peers:
            back_copy(part, other, other).wait_recv()
    cosine, sine = cosine_ref[...], sine_ref[...]
    grad_normed = None
    for part in range(3):
        if part < 2:
            for group in range(8):
                columns = slice(128 * group, 128 * (group + 1))
                grad = qkv_back[part, :, columns].astype(F32)
                qkv_back[part, :, columns] = low(grad * cosine - half_turn(grad) * sine)
        keep_bias(8 * part, qkv_back[part])
        index = (2, 1, 0)[part]
    for block, slot in ((2, 0), (1, 1), (0, 0)):
        loads[("wide", block)].wait()
        part = contract(qkv_back[block], whole_piece(wide_block.at[slot]), 1, 1)
        grad_normed = part if grad_normed is None else grad_normed + part
        if block == 2:
            load_wide(0)
    bias_copies = spread_dp(wire, place, lambda dp: bias_lines, bias_dp)
    normed, inverse = norm_parts(x_ref[...].astype(F32))
    grad_shift_one = column_sum(grad_normed)
    grad_scale_one = column_sum(grad_normed * normed)
    grad_hidden_ref[...] = low(
        running[...] + norm_back(normed, inverse, grad_normed * (1.0 + scale_one))
    )
    rows = (
        grad_shift_one,
        grad_scale_one,
        grad_gate_one,
        grad_shift_two,
        grad_scale_two,
        gate_two_grad_ref[...],
    )
    mod_grads[dp, seq] = low(jnp.concatenate([lines_of(row) for row in rows], axis=0))
    mod_gather = SmallGather(wire, place, mod_grads)
    mod_gather.along_seq()
    tick(9)
    settle(3, -1, -1)
    tick(10)
    settle(4, -1, -1)
    tick(11)
    settle(5, 2, -1)
    mod_gather.along_dp()
    collect(bias_copies)
    bias_sum[...] = total_of(bias_lines[...], bias_dp, 3)
    bias_copies = spread_seq(wire, place, lambda seq: bias_sum, bias_seq)
    tick(12)
    settle(7, 4, -1)
    tick(13)
    settle(8, 6, -1)
    tick(14)
    settle(9, 7, 2)
    mod_gather.finish()
    lines = mod_grads[...].astype(F32).reshape(1536, 128)
    mod_lines[...] = lines
    grad_ada_bias_ref[...] = jnp.sum(lines.reshape(32, 48, 128), axis=0)
    embedded = embedded_ref[...]
    share = 1.0 / (1.0 + jnp.exp(-embedded))
    silu_in = low(embedded * share)[:, :32]
    empty = jnp.zeros((96, 128), BF16)
    grad_silu = None
    for block in range(6):
        parts = []
        for line in range(8):
            part = mod_lines[pl.ds(8 * block + line, 32, stride=48), :]
            parts.append(jnp.concatenate([low(part), empty], axis=0))
        every = jnp.concatenate(parts, axis=1)
        columns = slice(1024 * block, 1024 * (block + 1))
        grad_ada_ref[:, columns] = contract(silu_in, every[:32], 1, 0)
        part = contract(low(w_ada_ref[:, columns]), every, 1, 1)
        grad_silu = part if grad_silu is None else grad_silu + part
    grad_embedded = grad_silu * share * (1.0 + embedded * (1.0 - share))
    embedded_grads[dp, seq] = pack_lanes(grad_embedded.reshape(1, 4, 8, 128))[0]
    embedded_gather = SmallGather(wire, place, embedded_grads)
    embedded_gather.along_seq()
    tick(15)
    settle(10, 8, 4)
    embedded_gather.along_dp()
    collect(bias_copies)
    grad_bias_ref[...] = total_of(bias_sum[...], bias_seq, 7)
    tick(16)
    settle(11, 9, 6)
    embedded_gather.finish()
    every_grad = jnp.concatenate(
        [unpack_lanes(embedded_grads[group, frame]) for group in range(4) for frame in range(8)],
        axis=0,
    )
    grad_table_ref[...] = contract(
        one_hot_ref[...],
        every_grad,
        0,
        1,
        precision=lax.Precision.HIGHEST,
    )[:32]
    settle(11, 11, 11)
    for part in range(3):
        for other in place.seq_peers:
            back_copy(part, other, other).wait_send()
    wire.drain()


def run_backward(cotangent, small, gathered, kept, x, w_ada):
    shape = jax.ShapeDtypeStruct
    outs = [
        ((256, 1024), BF16),
        ((32, 1024), F32),
        ((32, 6144), F32),
        ((48, 128), F32),
        ((32, 3072), F32),
        ((32, 1024), F32),
        ((32, 4096), F32),
        ((128, 1024), F32),
        ((80, 128), F32),
    ]
    query, keys, values, attended, tokens, normed_one, normed_two = kept[:7]
    middle, branch_one, act, slope, cosine, sine = kept[7:]
    fetched = (act, slope, normed_two, middle, branch_one, query, keys, values, attended)
    fetched += (tokens, x, normed_one, cosine, sine, w_ada)
    in_vmem = pl.BlockSpec(memory_space=pltpu.VMEM)
    anywhere = pl.BlockSpec(memory_space=pl.ANY)
    scratch = [vmem(array.shape, array.dtype) for array in fetched]
    scratch += [
        vmem((SLOTS, 4, 4, 2, 32, 1024), BF16),
        vmem((SLOTS, 4, 4, 32, 1024), BF16),
        vmem((12, 2, 2, 32, 1024), BF16),
        vmem((12, 2, 4, 32, 1024), BF16),
        vmem((12, 4, 32, 1024), BF16),
        vmem((4, 4, 2, 128, 256), BF16),
        vmem((2, 4, 4, 2, 32, 1024), BF16),
        vmem((256, 1024), BF16),
        vmem((256, 1024), BF16),
        vmem((256, 1024), BF16),
        vmem((8, 256, 128), BF16),
        vmem((8, 1, 512)),
        vmem((8, 128, 256)),
        vmem((8, 256, 128)),
        vmem((8, 256, 128)),
        vmem((8, 256, 128), BF16),
        vmem((8, 256, 128), BF16),
        vmem((8, 256, 128), BF16),
        vmem((3, 256, 1024), BF16),
        vmem((256, 1024)),
        vmem((80, 128)),
        vmem((3, 80, 128)),
        vmem((80, 128)),
        vmem((7, 80, 128)),
        vmem((4, 8, 48, 128), BF16),
        vmem((1536, 128)),
        vmem((4, 8, 8, 128)),
        pltpu.SemaphoreType.DMA((66,)),
        pltpu.SemaphoreType.DMA((80,)),
        pltpu.SemaphoreType.DMA((3, 8)),
        pltpu.SemaphoreType.DMA((3, 8)),
        pltpu.SemaphoreType.DMA((32,)),
        pltpu.SemaphoreType.REGULAR,
    ]
    return pl.pallas_call(
        backward_kernel,
        out_shape=[shape(*out) for out in outs],
        in_specs=[in_vmem] * 6 + [anywhere] * 17,
        out_specs=[in_vmem] * 9,
        scratch_shapes=scratch,
        compiler_params=pltpu.CompilerParams(
            collective_id=1, has_side_effects=True, vmem_limit_bytes=VMEM_LIMIT
        ),
        name="block_backward",
    )(cotangent, *small, *gathered, *fetched)


def finish_kernel(lines_ref, ada_lines_ref, *refs):
    device = lax.axis_index("dp") * 8 + lax.axis_index("seq")
    for index in range(8):
        refs[8 + index][...] = refs[index][...]
    for index, share in enumerate(BIAS_SHARE):
        lines, first = (lines_ref, BIAS_FIRST[index]) if index < 4 else (ada_lines_ref, 0)
        offset = device * share
        line = first + offset // 128
        pair = jnp.concatenate([lines[pl.ds(line, 1), :], lines[pl.ds(line + 1, 1), :]], axis=1)
        part = pltpu.roll(pair, (256 - offset % 128) % 256, 1)
        refs[16 + index][...] = part[:, :share].reshape(share)


def run_finish(lines, ada_lines, arrays):
    shape = jax.ShapeDtypeStruct
    in_vmem = pl.BlockSpec(memory_space=pltpu.VMEM)
    return pl.pallas_call(
        finish_kernel,
        out_shape=[shape(array.shape, array.dtype) for array in arrays]
        + [shape((share,), F32) for share in BIAS_SHARE],
        in_specs=[in_vmem] * 10,
        out_specs=[in_vmem] * 13,
        name="block_outputs",
    )(lines, ada_lines, *arrays)


def fast_body(
    hidden_in,
    noise_level,
    noise_table,
    w_ada,
    b_ada,
    w_qkv,
    b_qkv,
    w_out,
    b_out,
    w_up,
    b_up,
    w_down,
    b_down,
    grad_out,
):
    biases = (b_qkv, b_out, b_up, b_down, b_ada)
    x, cotangent = hidden_in[0], grad_out[0]
    results = run_forward(
        x, noise_level, noise_table, biases, w_qkv, w_out, w_up, w_down, w_ada, cotangent
    )
    layer_out, small, gathered, kept = results[0], results[1:6], results[6:8], results[8:]
    grads = run_backward(cotangent, small, gathered, kept, x, w_ada)
    grad_hidden, grad_table, grad_ada_w, ada_lines, *weight_grads, lines = grads
    outs = run_finish(
        lines, ada_lines, (layer_out, grad_hidden, grad_table, grad_ada_w, *weight_grads)
    )
    layer_out, grad_hidden, grad_table, grad_ada_w, qkv_w, out_w, up_w, down_w = outs[:8]
    qkv_b, out_b, up_b, down_b, ada_b = outs[8:]
    return (
        layer_out[None],
        grad_hidden[None],
        grad_table,
        grad_ada_w,
        ada_b,
        qkv_w,
        qkv_b,
        out_w,
        out_b,
        up_w,
        up_b,
        down_w,
        down_b,
    )


def solution(mesh):
    tokens = P("dp", "seq", None)
    matrix = P(ALL, None)
    vector = P(ALL)
    parameters = (matrix,) + (matrix, vector) * 5
    chips = dict(mesh.shape) == {"dp": 4, "seq": 8}
    return jax.shard_map(
        fast_body if chips else general_body,
        mesh=mesh,
        in_specs=(tokens, P("dp", "seq")) + parameters + (tokens,),
        out_specs=(tokens, tokens) + parameters,
        check_vma=False,
    )
```

```python
from functools import partial
import math

import jax
import jax.numpy as jnp
from jax import lax
from jax.experimental import pallas as pl
from jax.experimental.pallas import tpu as pltpu
from jax.sharding import PartitionSpec as P

H = 16
GRID_W = 16
PATCHES = 256


norm_eps = 1e-06
masked_score = -1e30
ALL = ("dp", "seq")
F32 = jnp.float32
BF16 = jnp.bfloat16


def layer_norm(values):
    centred = values - jnp.mean(values, axis=-1, keepdims=True)
    spread = jnp.mean(centred * centred, axis=-1, keepdims=True)
    return centred * lax.rsqrt(spread + norm_eps)


def modulate(values, shift_term, scale_term):
    return layer_norm(values) * (1.0 + scale_term) + shift_term


def turn_half(values):
    extent = values.shape[-1]
    side_part = 2 * (3 * extent // 16)
    pieces = []
    offset = 0
    for part_size in (extent - 2 * side_part, side_part, side_part):
        half_size = part_size // 2
        pieces.append(-values[..., offset + half_size : offset + part_size])
        pieces.append(values[..., offset : offset + half_size])
        offset = offset + part_size
    return jnp.concatenate(pieces, axis=-1)


def part_angles(places, part_size):
    half_size = part_size // 2
    rates = jnp.exp(-math.log(10000.0) * jnp.arange(half_size, dtype=F32) / half_size)
    angles = places.astype(F32)[:, None] * rates[None, :]
    return jnp.concatenate([angles, angles], axis=1)


def angle_table(places, extent):
    side_part = 2 * (3 * extent // 16)
    patch_index = places % PATCHES
    angles = jnp.concatenate(
        [
            part_angles(places // PATCHES, extent - 2 * side_part),
            part_angles(patch_index // GRID_W, side_part),
            part_angles(patch_index % GRID_W, side_part),
        ],
        axis=1,
    )
    return (jnp.cos(angles), jnp.sin(angles))


def rotate(values, cosine_table, sine_table):
    return values * cosine_table + turn_half(values) * sine_table


def unrotate(values, cosine_table, sine_table):
    return values * cosine_table - turn_half(values * sine_table)


def low(values):
    return values.astype(BF16)


def dot(left, right):
    return jnp.dot(left, right, preferred_element_type=F32)


def gather_rows(share):
    return lax.all_gather(low(share), ALL, axis=0, tiled=True)


def scatter_rows(whole):
    return lax.psum_scatter(whole, ALL, scatter_dimension=0, tiled=True)


def frame_modulation(noise_level, noise_table, w_ada, b_ada):
    levels = lax.all_gather(noise_level.reshape(-1), ALL, axis=0, tiled=True)
    device = lax.axis_index("dp") * lax.axis_size("seq") + lax.axis_index("seq")
    share = noise_table.shape[0]
    own_levels = device * share + jnp.arange(share, dtype=jnp.int32)
    one_hot = levels[:, None] == own_levels[None, :]
    found = dot(low(one_hot), low(noise_table))
    embedded = lax.psum_scatter(low(found), ALL, scatter_dimension=1, tiled=True).astype(F32)
    silu_in = low(jax.nn.silu(embedded))
    modulation = lax.psum_scatter(
        dot(silu_in, low(w_ada)), ALL, scatter_dimension=0, tiled=True
    ) + gather_rows(b_ada).astype(F32)
    return one_hot, embedded, silu_in, modulation


def frame_gradients(grad_modulation, one_hot, embedded, silu_in, w_ada):
    every = lax.all_gather(grad_modulation, ALL, axis=0, tiled=True)
    grad_ada_w = lax.dot_general(
        silu_in, every, (((0,), (0,)), ((), ())), preferred_element_type=F32
    )
    share = w_ada.shape[1] // lax.axis_size(ALL)
    device = lax.axis_index("dp") * lax.axis_size("seq") + lax.axis_index("seq")
    columns = lax.dynamic_slice_in_dim(every, device * share, share, axis=1)
    grad_ada_b = jnp.sum(columns.astype(F32), axis=0)
    grad_silu = lax.dot_general(
        every, low(w_ada), (((1,), (1,)), ((), ())), preferred_element_type=F32
    )
    unused, silu_back = jax.vjp(jax.nn.silu, embedded)
    grad_embedded = lax.all_gather(silu_back(grad_silu)[0], ALL, axis=1, tiled=True)
    grad_table = jnp.dot(
        one_hot.astype(F32).T, grad_embedded, precision=lax.Precision.HIGHEST
    )
    return grad_table, grad_ada_w, grad_ada_b


def to_heads(values):
    return lax.all_to_all(values, "seq", split_axis=2, concat_axis=1, tiled=True)


def to_tokens(values):
    return lax.all_to_all(values, "seq", split_axis=1, concat_axis=2, tiled=True)


def as_heads(values):
    return values.reshape(*values.shape[:2], -1, 64)


def query_blocks(array, axis):
    blocks = array.shape[axis] // PATCHES
    split = array.shape[:axis] + (blocks, PATCHES) + array.shape[axis + 1 :]
    return jnp.moveaxis(array.reshape(split), axis, 0)


def block_scores(query_block, keys, frame, score_scale):
    scores = (
        jnp.einsum("cqhd,ckhd->chqk", query_block, keys, preferred_element_type=F32) * score_scale
    )
    allowed = jnp.arange(keys.shape[1], dtype=jnp.int32) // PATCHES <= frame
    return jnp.where(allowed, scores, masked_score)


def attend(query, keys, values, score_scale):
    def one_block(block_in):
        query_block, frame = block_in
        scores = block_scores(query_block, keys, frame, score_scale)
        row_max = jnp.max(scores, axis=-1, keepdims=True)
        exponent = jnp.exp(scores - row_max)
        row_total = jnp.sum(exponent, axis=-1, keepdims=True)
        weighted = jnp.einsum(
            "chqk,ckhd->cqhd", low(exponent / row_total), values, preferred_element_type=F32
        )
        return low(weighted), (row_max + jnp.log(row_total))[..., 0]

    frames = jnp.arange(query.shape[1] // PATCHES, dtype=jnp.int32)
    attended, log_total = lax.map(one_block, (query_blocks(query, 1), frames))
    return (
        jnp.moveaxis(attended, 0, 1).reshape(query.shape),
        jnp.moveaxis(log_total, 0, 2).reshape(query.shape[0], query.shape[2], query.shape[1]),
    )


def attend_back(query, keys, values, grad_heads, log_total, row_delta, score_scale):
    def one_block(carried, block_in):
        query_block, grad_block, total_block, delta_block, frame = block_in
        scores = block_scores(query_block, keys, frame, score_scale)
        softmax_weights = jnp.exp(scores - total_block[..., None])
        grad_soft = jnp.einsum("cqhd,ckhd->chqk", grad_block, values, preferred_element_type=F32)
        grad_scores = low(softmax_weights * (grad_soft - delta_block[..., None]))
        query_grad = jnp.einsum("chqk,ckhd->cqhd", grad_scores, keys, preferred_element_type=F32)
        keys_grad = jnp.einsum(
            "chqk,cqhd->ckhd", grad_scores, query_block, preferred_element_type=F32
        )
        values_grad = jnp.einsum(
            "chqk,cqhd->ckhd", low(softmax_weights), grad_block, preferred_element_type=F32
        )
        return (carried[0] + keys_grad, carried[1] + values_grad), query_grad

    frames = jnp.arange(query.shape[1] // PATCHES, dtype=jnp.int32)
    empty = jnp.zeros(keys.shape, F32)
    (grad_keys, grad_values), grad_query = lax.scan(
        one_block,
        (empty, empty),
        (
            query_blocks(query, 1),
            query_blocks(grad_heads, 1),
            query_blocks(log_total, 2),
            query_blocks(row_delta, 2),
            frames,
        ),
    )
    grad_query = jnp.moveaxis(grad_query, 0, 1).reshape(query.shape)
    return grad_query * score_scale, grad_keys * score_scale, grad_values


def general_body(
    hidden_in,
    noise_level,
    noise_table,
    w_ada,
    b_ada,
    w_qkv,
    b_qkv,
    w_out,
    b_out,
    w_up,
    b_up,
    w_down,
    b_down,
    grad_out,
):
    qkv_w, qkv_b, out_w, out_b, up_w, up_b, down_w, down_b = [
        gather_rows(share)
        for share in (w_qkv, b_qkv, w_out, b_out, w_up, b_up, w_down, b_down)
    ]
    clip_count, patches, model_width = hidden_in.shape
    head_dim = model_width // H
    score_scale = 1.0 / math.sqrt(head_dim)
    head_shape = (clip_count, patches, H, head_dim)
    inputs = hidden_in.astype(F32)
    one_hot, embedded, silu_in, modulation = frame_modulation(
        noise_level, noise_table, w_ada, b_ada
    )
    shift_one, scale_one, gate_one, shift_two, scale_two, gate_two = [
        modulation[:, None, column_block * model_width : (column_block + 1) * model_width]
        for column_block in range(6)
    ]
    normed_one = low(modulate(inputs, shift_one, scale_one))
    qkv_all = dot(normed_one, qkv_w) + qkv_b.astype(F32)
    frame_own = lax.axis_index("seq")
    places = frame_own * patches + jnp.arange(patches, dtype=jnp.int32)
    cosine_local, sine_local = angle_table(places, head_dim)
    cosine_wide = cosine_local[None, :, None, :]
    sine_wide = sine_local[None, :, None, :]
    flat_shape = (clip_count, patches, model_width)

    def turned(block):
        part = qkv_all[..., block * model_width : (block + 1) * model_width]
        return low(rotate(part.reshape(head_shape), cosine_wide, sine_wide)).reshape(flat_shape)

    query = as_heads(to_heads(turned(0)))
    keys = as_heads(to_heads(turned(1)))
    values = as_heads(to_heads(low(qkv_all[..., 2 * model_width :])))
    attended, log_total = attend(query, keys, values, score_scale)
    attended_low = to_tokens(attended.reshape(*attended.shape[:2], -1))
    branch_one = dot(attended_low, out_w) + out_b.astype(F32)
    middle = inputs + gate_one * branch_one
    normed_two = low(modulate(middle, shift_two, scale_two))
    hidden_pre = dot(normed_two, up_w) + up_b.astype(F32)
    hidden_act = low(jax.nn.gelu(hidden_pre, approximate=True))
    branch_two = dot(hidden_act, down_w) + down_b.astype(F32)
    outputs = middle + gate_two * branch_two
    cotangent = grad_out.astype(F32)
    grad_gate_two = jnp.sum(cotangent * branch_two, axis=1)
    grad_branch_two = low(cotangent * gate_two)

    def weight_grad(left, right):
        whole = jnp.einsum("cpi,cpo->io", left, right, preferred_element_type=F32)
        return scatter_rows(low(whole)).astype(F32)

    def bias_grad(grad):
        return scatter_rows(jnp.sum(grad.astype(F32), axis=(0, 1)))

    def back_dot(grad, weight):
        return jnp.einsum("cpo,io->cpi", grad, weight, preferred_element_type=F32)

    grad_down_w = weight_grad(hidden_act, grad_branch_two)
    grad_down_b = bias_grad(grad_branch_two)
    grad_act = back_dot(grad_branch_two, down_w)
    unused, gelu_back = jax.vjp(partial(jax.nn.gelu, approximate=True), hidden_pre)
    grad_pre = low(gelu_back(grad_act)[0])
    grad_up_w = weight_grad(normed_two, grad_pre)
    grad_up_b = bias_grad(grad_pre)
    grad_normed_two = back_dot(grad_pre, up_w)
    unused, norm_two_back = jax.vjp(modulate, middle, shift_two, scale_two)
    grad_middle_norm, grad_shift_two, grad_scale_two = norm_two_back(grad_normed_two)
    grad_middle = cotangent + grad_middle_norm
    grad_gate_one = jnp.sum(grad_middle * branch_one, axis=1)
    grad_branch_one = low(grad_middle * gate_one)
    grad_out_w = weight_grad(attended_low, grad_branch_one)
    grad_out_b = bias_grad(grad_branch_one)
    grad_attended = low(back_dot(grad_branch_one, out_w))
    grad_heads = as_heads(to_heads(grad_attended))
    row_delta = jnp.sum(grad_heads.astype(F32) * attended.astype(F32), axis=-1).transpose(0, 2, 1)
    grad_query, grad_keys, grad_values = attend_back(
        query, keys, values, grad_heads, log_total, row_delta, score_scale
    )

    def home(grad):
        return to_tokens(low(grad).reshape(*grad.shape[:2], -1))

    def unturned(grad):
        wide = home(grad).astype(F32).reshape(head_shape)
        return low(unrotate(wide, cosine_wide, sine_wide)).reshape(flat_shape)

    grad_qkv = jnp.concatenate(
        [unturned(grad_query), unturned(grad_keys), home(grad_values)], axis=-1
    )
    grad_qkv_w = weight_grad(normed_one, grad_qkv)
    grad_qkv_b = bias_grad(grad_qkv)
    grad_normed_one = back_dot(grad_qkv, qkv_w)
    unused, norm_one_back = jax.vjp(modulate, inputs, shift_one, scale_one)
    grad_input_norm, grad_shift_one, grad_scale_one = norm_one_back(grad_normed_one)
    grad_input = grad_middle + grad_input_norm
    grad_modulation = low(
        jnp.concatenate(
            [
                grad_shift_one[:, 0],
                grad_scale_one[:, 0],
                grad_gate_one,
                grad_shift_two[:, 0],
                grad_scale_two[:, 0],
                grad_gate_two,
            ],
            axis=-1,
        )
    )
    grad_table, grad_ada_w, grad_ada_b = frame_gradients(
        grad_modulation, one_hot, embedded, silu_in, w_ada
    )
    return (
        low(outputs),
        low(grad_input),
        grad_table,
        grad_ada_w,
        grad_ada_b,
        grad_qkv_w,
        grad_qkv_b,
        grad_out_w,
        grad_out_b,
        grad_up_w,
        grad_up_b,
        grad_down_w,
        grad_down_b,
    )


MESH_ID = pl.DeviceIdType.MESH
VMEM_LIMIT = 63 * 1024 * 1024
HEADS_WIDE = 128


def contract(left, right, left_dim, right_dim, precision=None):
    return lax.dot_general(
        left,
        right,
        (((left_dim,), (right_dim,)), ((), ())),
        preferred_element_type=F32,
        precision=precision,
    )


class Place:
    def __init__(self):
        self.dp = lax.axis_index("dp")
        self.seq = lax.axis_index("seq")
        self.z = self.seq // 2
        self.core = self.seq % 2
        self.other = 1 - self.core
        self.x_dp = self.dp + 1 - 2 * (self.dp % 2)
        self.y_dp = (self.dp + 2) % 4
        self.far_dp = 3 - self.dp
        self.dp_peers = (self.x_dp, self.y_dp, self.far_dp)
        self.seq_peers = [(self.seq + step) % 8 for step in range(1, 8)]
        self.sibling = (self.dp, self.z * 2 + self.other)
        self.z_pair = self.z + 1 - 2 * (self.z % 2)
        self.z_end = (self.z == 0) | (self.z == 3)
        self.z_middle = (self.z == 1) | (self.z == 2)
        self.z_beyond = 2 - 2 * (self.z // 2)

    def at_dp(self, dp):
        return (dp, self.seq)

    def at_seq(self, seq):
        return (self.dp, seq)

    def at_z_chip(self, z):
        return (self.dp, z * 2 + self.core)

    def greet(self):
        barrier = pltpu.get_barrier_semaphore()
        peers = [self.at_dp(dp) for dp in self.dp_peers]
        peers += [self.at_seq(seq) for seq in self.seq_peers]
        for peer in peers:
            pl.semaphore_signal(barrier, inc=1, device_id=peer, device_id_type=MESH_ID)
        pl.semaphore_wait(barrier, len(peers))


def guarded(only, act):
    if only is None:
        act()
    else:
        pl.when(only)(act)


class Copy:
    def __init__(self, wire, source, target, device, only, landing):
        self.wire, self.only = wire, only
        self.sending = wire.take_send()
        self.landing = wire.take_recv() if landing is None else landing.landing
        self.copy = wire.describe(source, target, device, self.sending, self.landing)
        guarded(only, self.copy.start)

    def wait_send(self):
        guarded(self.only, self.copy.wait_send)
        self.wire.free.append(self.sending)

    def wait_recv(self):
        self.copy.wait_recv()


class Batch:
    def __init__(self, wire, copies, whole):
        self.wire, self.copies, self.whole = wire, copies, whole
        self.landing = copies[0].landing

    def wait_recv(self):
        first = self.copies[0]
        place = self.wire.place
        self.wire.describe(
            self.whole, self.whole, place.sibling, first.sending, self.landing
        ).wait_recv()


class Wire:
    def __init__(self, place, send_sems, recv_sems):
        self.place = place
        self.send_sems = send_sems
        self.recv_sems = recv_sems
        self.sends = 0
        self.recvs = 0
        self.free = []
        self.sent = []

    def take_send(self):
        if self.free:
            return self.free.pop(0)
        self.sends += 1
        assert self.sends <= self.send_sems.shape[0]
        return self.sends - 1

    def take_recv(self):
        self.recvs += 1
        assert self.recvs <= self.recv_sems.shape[0]
        return self.recvs - 1

    def describe(self, source, target, device, sending, landing):
        return pltpu.make_async_remote_copy(
            src_ref=source,
            dst_ref=target,
            send_sem=self.send_sems.at[sending],
            recv_sem=self.recv_sems.at[landing],
            device_id=device,
            device_id_type=MESH_ID,
        )

    def send(self, source, target, device, only=None, landing=None):
        copy = Copy(self, source, target, device, only, landing)
        self.sent.append(copy)
        return copy

    def send_all(self, whole, parts, landing=None):
        copies = []
        for source, target, device in parts:
            copies.append(self.send(source, target, device, None, landing))
            landing = copies[0] if landing is None else landing
        return Batch(self, copies, whole)

    def drain(self, copies=None):
        copies = list(self.sent if copies is None else copies)
        for copy in copies:
            copy.wait_send()
        self.sent = [copy for copy in self.sent if not any(copy is done for done in copies)]


class Local:
    def __init__(self, sems):
        self.sems = sems
        self.used = 0

    def start(self, source, target):
        copy = pltpu.make_async_copy(source, target, self.sems.at[self.used])
        self.used += 1
        assert self.used <= self.sems.shape[0]
        copy.start()
        return copy


def arrive(copies):
    for copy in copies:
        copy.wait_recv()


class Gather:
    def __init__(self, wire, place, ref):
        self.wire, self.place, self.ref = wire, place, ref
        self.early = None
        self.mine = []

    def send(self, source, device, only=None, landing=None):
        copy = self.wire.send(source, source, device, only, landing)
        self.mine.append(copy)
        return copy

    def batch(self, whole, parts, landing=None):
        batch = self.wire.send_all(
            whole, [(part, part, device) for part, device in parts], landing
        )
        self.mine += batch.copies
        return batch

    def along_z(self):
        place = self.place
        own = self.ref.at[place.dp, place.z, place.core]
        across = place.at_z_chip(2 - place.z // 2)
        self.paired = self.send(own, place.at_z_chip(place.z_pair))
        self.crossed = self.send(own, across)

    def pass_z(self):
        place = self.place
        two = self.ref.at[place.dp, pl.ds(place.z_beyond, 2), place.core]
        both = Batch(self.wire, [self.crossed], two)
        guarded(place.z_middle, both.wait_recv)
        self.passed = self.send(two, place.at_z_chip(place.z_pair), place.z_middle)

    def all_z(self):
        arrive([self.paired])
        guarded(self.place.z_end, self.passed.wait_recv)

    def xy_devices(self):
        place = self.place
        return [place.at_dp(dp) for dp in (place.x_dp, place.y_dp)]

    def own_xy(self):
        place = self.place
        own = self.ref.at[place.dp, place.z, place.core]
        whole = self.ref.at[pl.ds(0, 2), :, place.core]
        self.early = self.batch(whole, [(own, device) for device in self.xy_devices()])

    def along_xy(self):
        place = self.place
        self.all_z()
        if self.early:
            parts = []
            for step in (1, 2, 3):
                part = self.ref.at[place.dp, (place.z + step) % 4, place.core]
                parts += [(part, device) for device in self.xy_devices()]
            self.batch(None, parts, self.early)
            self.coming = self.early
            return
        own = self.ref.at[place.dp, :, place.core]
        whole = self.ref.at[pl.ds(0, 2), :, place.core]
        self.coming = self.batch(whole, [(own, device) for device in self.xy_devices()])

    def across(self):
        place = self.place
        arrive([self.coming])
        from_x = self.ref.at[place.x_dp, pl.ds(0, 2), place.core]
        from_y = self.ref.at[place.y_dp, pl.ds(2, 2), place.core]
        whole = self.ref.at[0, :, place.core]
        to_x, to_y = self.xy_devices()
        self.coming = self.batch(whole, [(from_x, to_y), (from_y, to_x)])

    def to_sibling(self):
        place = self.place
        arrive([self.coming])
        self.coming = self.send(self.ref.at[:, :, place.core], place.sibling)

    def finish(self):
        arrive([self.coming])
        self.wire.drain(self.mine)


class SmallGather:
    def __init__(self, wire, place, ref):
        self.wire, self.place, self.ref = wire, place, ref

    def along_seq(self):
        place = self.place
        own = self.ref.at[place.dp, place.seq]
        self.seq_coming = self.wire.send_all(
            self.ref.at[0, pl.ds(0, 7)],
            [(own, own, place.at_seq(seq)) for seq in place.seq_peers],
        )

    def along_dp(self):
        place = self.place
        arrive([self.seq_coming])
        own = self.ref.at[place.dp]
        self.dp_coming = self.wire.send_all(
            self.ref.at[pl.ds(0, 3)], [(own, own, place.at_dp(dp)) for dp in place.dp_peers]
        )

    def finish(self):
        arrive([self.dp_coming])
        self.wire.drain(self.seq_coming.copies + self.dp_coming.copies)


def spread_dp(wire, place, part_of, slots):
    parts = [
        (part_of(dp), slots.at[index], place.at_dp(dp)) for index, dp in enumerate(place.dp_peers)
    ]
    return wire.send_all(slots, parts)


def spread_seq(wire, place, part_of, slots):
    parts = [
        (part_of(seq), slots.at[index], place.at_seq(seq))
        for index, seq in enumerate(place.seq_peers)
    ]
    return wire.send_all(slots, parts)


def collect(batch):
    arrive([batch])
    batch.wire.drain(batch.copies)


def total_of(own, slots, count):
    total = own
    for index in range(count):
        total = total + slots[index].astype(F32)
    return total


def row_of(lines, first):
    return jnp.concatenate([lines[first + line : first + line + 1, :] for line in range(8)], axis=1)


def lines_of(row):
    return jnp.concatenate([row[:, 128 * line : 128 * (line + 1)] for line in range(8)], axis=0)


def whole_piece(piece):
    value = piece[...]
    return value.reshape(-1, value.shape[-1])


def norm_parts(values):
    centred = values - jnp.mean(values, axis=1, keepdims=True)
    inverse = lax.rsqrt(jnp.mean(centred * centred, axis=1, keepdims=True) + norm_eps)
    return centred * inverse, inverse


def half_turn(values):
    lane = lax.broadcasted_iota(jnp.int32, values.shape, 1) % 64
    in_time = lane < 16
    first = (lane < 8) | ((lane >= 16) & (lane < 28)) | ((lane >= 40) & (lane < 52))
    up = jnp.where(in_time, pltpu.roll(values, 120, 1), pltpu.roll(values, 116, 1))
    down = jnp.where(in_time, pltpu.roll(values, 8, 1), pltpu.roll(values, 12, 1))
    return jnp.where(first, up, down)


def split_heads(values):
    lane = lax.broadcasted_iota(jnp.int32, values.shape, 1)
    empty = jnp.zeros_like(values)
    return jnp.concatenate(
        [jnp.where(lane < 64, values, empty), jnp.where(lane < 64, empty, values)], axis=0
    )


def join_heads(turned):
    return jnp.concatenate([turned[:64, :256], turned[64:, 256:]], axis=0).T


def attend_frame(frame, query, keys, values, attended, log_total, scores):
    pair = split_heads(query[frame])
    row_max = None
    for block in range(frame + 1):
        block_scores = contract(keys[block], pair, 1, 1)
        scores[block] = block_scores
        block_max = jnp.max(block_scores, axis=0, keepdims=True)
        row_max = block_max if row_max is None else jnp.maximum(row_max, block_max)
    row_total = None
    weighted = None
    for block in range(frame + 1):
        exponent = jnp.exp(scores[block] - row_max)
        block_total = jnp.sum(exponent, axis=0, keepdims=True)
        block_sum = contract(values[block], exponent.astype(BF16), 0, 0)
        row_total = block_total if row_total is None else row_total + block_total
        weighted = block_sum if weighted is None else weighted + block_sum
    attended[frame] = join_heads(weighted / row_total).astype(BF16)
    log_total[frame] = row_max + jnp.log(row_total)


SQRT_TWO_OVER_PI = math.sqrt(2.0 / math.pi)


def gelu_parts(values):
    square = values * values
    bent = jnp.tanh(SQRT_TWO_OVER_PI * values * (1.0 + 0.044715 * square))
    half = 0.5 * (1.0 + bent)
    slope = half + 0.5 * values * (1.0 - bent * bent) * (
        SQRT_TWO_OVER_PI * (1.0 + 3.0 * 0.044715 * square)
    )
    return values * half, slope


def rope_in_kernel(frame):
    lane = lax.broadcasted_iota(jnp.int32, (256, 128), 1) % 64
    patch = lax.broadcasted_iota(jnp.int32, (256, 128), 0)
    in_time, in_rows = lane < 16, lane < 40
    half = jnp.where(in_time, 8, 12)
    step = jnp.where(in_time, lane, jnp.where(in_rows, lane - 16, lane - 40))
    second = step >= half
    step = jnp.where(second, step - half, step).astype(F32)
    position = jnp.where(in_time, frame, jnp.where(in_rows, patch // GRID_W, patch % GRID_W))
    rate = jnp.exp(-math.log(10000.0) * step / half.astype(F32))
    angle = position.astype(F32) * rate
    sine = jnp.sin(angle)
    return jnp.cos(angle), jnp.where(second, sine, -sine)


BIAS_FIRST = (0, 24, 32, 64, 72)
BIAS_SHARE = (96, 32, 128, 32, 192)


def every_bias(blocks, lines):
    lane = lax.broadcasted_iota(jnp.int32, (8, 128), 1)

    def take(line, first, every):
        return blocks[pl.ds(8 * first + line, 32 // every, stride=8 * every), :]

    def moved(values, lanes):
        return pltpu.roll(values, lanes % 128, 1)

    mixed = [take(2, first, 4) for first in range(4)]
    lines[pl.ds(0, 8, stride=3), :] = jnp.where(lane < 96, mixed[0], moved(mixed[1], 96))
    lines[pl.ds(1, 8, stride=3), :] = jnp.where(lane < 64, moved(mixed[1], 96), moved(mixed[2], 64))
    lines[pl.ds(2, 8, stride=3), :] = jnp.where(lane < 32, moved(mixed[2], 64), moved(mixed[3], 32))

    def quarters(parts, first_lane):
        total = jnp.zeros((8, 128), F32)
        for index, part in enumerate(parts):
            here = (lane >= 32 * index) & (lane < 32 * (index + 1))
            total = jnp.where(here, moved(part, 32 * index - first_lane), total)
        return total

    lines[24:32, :] = quarters(mixed, 96)
    lines[32:64, :] = take(1, 0, 1)
    lines[64:72, :] = quarters([take(4, first, 4) for first in range(4)], 64)
    left = lax.broadcasted_iota(jnp.int32, (16, 128), 1) < 64
    even, odd = take(3, 0, 2), take(3, 1, 2)
    even_rest, odd_rest = take(4, 0, 2), take(4, 1, 2)
    lines[pl.ds(72, 16, stride=3), :] = even
    lines[pl.ds(73, 16, stride=3), :] = jnp.where(left, even_rest, moved(odd, 64))
    lines[pl.ds(74, 16, stride=3), :] = jnp.where(left, moved(odd, 64), moved(odd_rest, 64))


def pack_lanes(rows):
    packed = rows[:, 0]
    for part in range(1, 4):
        packed = packed + pltpu.roll(rows[:, part], 32 * part, 2)
    return packed


def unpack_lanes(packed):
    lane = lax.broadcasted_iota(jnp.int32, packed.shape, packed.ndim - 1)
    parts = [packed] + [pltpu.roll(packed, 128 - 32 * part, 1) for part in range(1, 4)]
    return jnp.concatenate([jnp.where(lane < 32, part, 0.0) for part in parts], axis=0)


def forward_kernel(
    x_ref,
    level_ref,
    table_ref,
    b_qkv_ref,
    b_out_ref,
    b_up_ref,
    b_down_ref,
    b_ada_ref,
    w_qkv_ref,
    w_out_in,
    w_up_in,
    w_down_in,
    w_ada_in,
    cotangent_in,
    layer_out_ref,
    log_total_ref,
    modulation_ref,
    embedded_ref,
    one_hot_ref,
    gate_two_grad_ref,
    wide_out,
    down_out,
    query_out,
    keys_out,
    values_out,
    attended_out,
    tokens_out,
    normed_one_out,
    normed_two_out,
    middle_out,
    branch_one_out,
    act_out,
    slope_out,
    cosine_out,
    sine_out,
    query_ref,
    keys_ref,
    values_ref,
    attended_ref,
    attended_tokens,
    normed_one_ref,
    normed_two_ref,
    middle_ref,
    branch_one_ref,
    act_ref,
    slope_ref,
    cosine_ref,
    sine_ref,
    w_out_ref,
    w_up_ref,
    w_down_ref,
    w_ada_ref,
    cotangent_ref,
    wide,
    down,
    levels,
    found,
    found_dp,
    found_sum,
    found_seq,
    partial_mod,
    mod_dp,
    mod_sum,
    mod_blocks,
    mod_seq,
    bias_lines,
    blocks,
    own_block,
    flat,
    scores,
    send_sems,
    recv_sems,
    back_send,
    back_recv,
    local_sems,
):
    place = Place()
    wire = Wire(place, send_sems, recv_sems)
    dp, seq, z, core = place.dp, place.seq, place.z, place.core
    device = dp * 8 + seq
    local = Local(local_sems)
    loads = [
        local.start(source, target)
        for source, target in (
            (w_ada_in, w_ada_ref),
            (w_out_in, w_out_ref),
            (w_up_in, w_up_ref),
            (w_down_in, w_down_ref),
            (cotangent_in, cotangent_ref),
        )
    ]
    own_block[...] = jnp.full((8, 128), level_ref[0, 0].astype(F32), F32)

    def place_bias(line, lane, ref, first, share):
        values = low(ref[first : first + share]).astype(F32)
        own_block[line : line + 1, lane : lane + share] = values.reshape(1, share)

    place_bias(1, 0, b_up_ref, 0, 128)
    place_bias(2, 0, b_qkv_ref, 0, 96)
    place_bias(2, 96, b_out_ref, 0, 32)
    place_bias(3, 0, b_ada_ref, 0, 128)
    place_bias(4, 0, b_ada_ref, 128, 64)
    place_bias(4, 64, b_down_ref, 0, 32)
    levels[dp, seq] = own_block[...]
    wide[0, dp, z, core] = low(w_qkv_ref[:, :1024])
    place.greet()
    level_gather = SmallGather(wire, place, levels)
    level_gather.along_seq()
    pieces = [Gather(wire, place, wide.at[index]) for index in range(8)]
    pieces += [Gather(wire, place, down.at[index]) for index in range(4)]
    pieces[0].along_z()
    pieces[0].own_xy()
    for block in (1, 2):
        wide[block, dp, z, core] = low(w_qkv_ref[:, 1024 * block : 1024 * (block + 1)])
        pieces[block].own_xy()
    saved = []

    def save(index):
        pieces[index].finish()
        source, target = (
            (wide.at[index], wide_out.at[index])
            if index < 8
            else (down.at[index - 8], down_out.at[index - 8])
        )
        saved.append(local.start(source, target))

    def keep(source, target):
        saved.append(local.start(source, target))

    started = [2]
    passed = [4]

    def start_z(last):
        while started[0] <= min(last, 11):
            pieces[started[0]].along_z()
            started[0] += 1

    def pass_z(last):
        while passed[0] <= min(last, 11):
            pieces[passed[0]].pass_z()
            passed[0] += 1

    def links(step):
        pass_z((0, 0, 0, 5, 7, 8, 9, 9)[step] if step < 8 else step)
        start_z((0, 0, 0, 9, 9, 9, 9, 9, 10, 11)[min(step, 9)])
        if step < 12:
            pieces[step].along_xy()
        if step - 1 < 12:
            pieces[step - 1].across()
        if step > 8:
            pass_z(step + 1)

    def tick(step):
        links(step)
        pieces[step - 2].to_sibling()
        save(step - 3)

    x = x_ref[...].astype(F32)
    normed, unused = norm_parts(x)
    flat[0] = normed
    level_gather.along_dp()
    pieces[1].along_z()
    start_z(2)
    level_gather.finish()
    level_rows = jnp.concatenate(
        [levels[group, frame, 0:1, :] for group in range(4) for frame in range(8)]
        + [jnp.full((96, 128), -1.0, F32)],
        axis=0,
    )
    lane = lax.broadcasted_iota(jnp.int32, (128, 128), 1)
    own_level = (lane + device * 32).astype(F32)
    one_hot = jnp.where((level_rows == own_level) & (lane < 32), 1.0, 0.0)
    one_hot_ref[...] = one_hot
    one_hot_turned = low(one_hot.T)[:32, :]
    rows = contract(low(table_ref[...]), one_hot_turned, 0, 0).reshape(32, 4, 8, 128)
    found[...] = pack_lanes(rows).reshape(found.shape)
    found_copies = spread_dp(wire, place, lambda dp: found.at[dp], found_dp)
    for copy in loads:
        copy.wait()
    wide[3, dp, z, core] = low(w_out_ref[...])
    for block in range(4):
        wide[4 + block, dp, z, core] = low(w_up_ref[:, 1024 * block : 1024 * (block + 1)])
    for block in range(4):
        down[block, dp, z, core] = low(w_down_ref[:, 256 * block : 256 * (block + 1)])
    start_z(3)
    for block in (3, 4, 5):
        pieces[block].own_xy()
    pieces[0].pass_z()
    pieces[0].along_xy()
    collect(found_copies)
    found_sum[...] = total_of(found[dp], found_dp, 3)
    found_copies = spread_seq(wire, place, lambda seq: found_sum.at[seq], found_seq)
    pieces[1].pass_z()
    start_z(5)
    pieces[1].along_xy()
    cosine, sine = rope_in_kernel(seq)
    cosine_ref[...] = cosine
    sine_ref[...] = sine
    keep(cosine_ref, cosine_out)
    keep(sine_ref, sine_out)
    pieces[0].across()
    collect(found_copies)
    embedded = unpack_lanes(total_of(found_sum[seq], found_seq, 7))
    embedded_ref[...] = embedded
    silu_in = low(embedded / (1.0 + jnp.exp(-embedded)))
    for block in range(6):
        part = contract(silu_in, low(w_ada_ref[:, 1024 * block : 1024 * (block + 1)]), 0, 0)
        lines = [part[:32, 128 * line : 128 * (line + 1)].reshape(4, 8, 128) for line in range(8)]
        for pair in range(4):
            both = jnp.concatenate(lines[2 * pair : 2 * pair + 2], axis=1)
            partial_mod[4 * block + pair] = low(both)
    mod_copies = spread_dp(wire, place, lambda dp: partial_mod.at[:, dp], mod_dp)
    blocks[...] = levels[...].reshape(256, 128)
    every_bias(blocks, bias_lines)
    pieces[2].pass_z()
    pieces[3].pass_z()
    start_z(7)
    pieces[2].along_xy()
    pieces[1].across()
    pieces[0].to_sibling()
    collect(mod_copies)
    mod_sum[...] = total_of(partial_mod[:, dp].astype(F32), mod_dp, 3).reshape(384, 128)
    for frame in range(8):
        mod_blocks[frame] = mod_sum[pl.ds(frame, 48, stride=8), :]
    mod_copies = spread_seq(wire, place, lambda seq: mod_blocks.at[seq], mod_seq)
    tick(3)
    biases = bias_lines[...]
    collect(mod_copies)
    modulation = total_of(mod_blocks[seq], mod_seq, 7) + biases[72:120]
    for block in range(6):
        modulation_ref[block : block + 1, :] = row_of(modulation, 8 * block)
    shift_one = modulation_ref[0:1, :]
    scale_one = modulation_ref[1:2, :]
    gate_one = modulation_ref[2:3, :]
    shift_two = modulation_ref[3:4, :]
    scale_two = modulation_ref[4:5, :]
    gate_two = modulation_ref[5:6, :]
    normed_one_ref[...] = low(flat[0] * (1.0 + scale_one) + shift_one)
    keep(normed_one_ref, normed_one_out)
    cosine = cosine_ref[...]
    sine = sine_ref[...]
    head_copies = []

    def project(block, target):
        r = contract(normed_one_ref[...], whole_piece(wide.at[block]), 1, 0)
        r = r + row_of(biases, 8 * block)
        for group in range(8):
            part = r[:, 128 * group : 128 * (group + 1)]
            if block < 2:
                part = part * cosine + half_turn(part) * sine
            if block == 0:
                part = part * 0.125
            act_ref[:, 1024 * block + 128 * group : 1024 * block + 128 * (group + 1)] = low(part)
        parts = []
        for other in place.seq_peers:
            columns = pl.ds(pl.multiple_of(1024 * block + other * 128, 128), 128)
            parts.append((act_ref.at[:, columns], target.at[seq], place.at_seq(other)))
        head_copies.append(wire.send_all(target.at[pl.ds(0, 7)], parts))
        columns = pl.ds(pl.multiple_of(1024 * block + seq * 128, 128), 128)
        target[seq] = act_ref[:, columns]

    project(0, query_ref)
    tick(4)
    project(1, keys_ref)
    tick(5)
    project(2, values_ref)
    tick(6)
    tick(7)
    tick(8)
    arrive(head_copies)
    keep(query_ref, query_out)
    keep(keys_ref, keys_out)
    keep(values_ref, values_out)

    def back_copy(frame, source):
        columns = pl.ds(pl.multiple_of(source * 128, 128), 128)
        return pltpu.make_async_remote_copy(
            src_ref=attended_ref.at[frame],
            dst_ref=attended_tokens.at[:, columns],
            send_sem=back_send.at[frame],
            recv_sem=back_recv.at[source],
            device_id=place.at_seq(frame),
            device_id_type=MESH_ID,
        )

    def send_back(frame):
        @pl.when(seq != frame)
        def _():
            back_copy(frame, seq).start()

        @pl.when(seq == frame)
        def _():
            columns = pl.ds(pl.multiple_of(seq * 128, 128), 128)
            attended_tokens[:, columns] = attended_ref[frame]

    for frame in (7, 0, 6, 1, 5, 2, 4, 3):
        attend_frame(
            frame, query_ref, keys_ref, values_ref, attended_ref, log_total_ref, scores
        )
        send_back(frame)
        if frame == 1:
            links(9)
    keep(attended_ref, attended_out)
    links(10)
    pieces[7].to_sibling()
    save(6)
    for other in place.seq_peers:
        back_copy(other, other).wait_recv()
    for other in place.seq_peers:
        back_copy(other, other).wait_send()
    keep(attended_tokens, tokens_out)
    for batch in head_copies:
        wire.drain(batch.copies)
    branch_one = contract(attended_tokens[...], whole_piece(wide.at[3]), 1, 0)
    branch_one = branch_one + row_of(biases, 24)
    branch_one_ref[...] = branch_one
    keep(branch_one_ref, branch_one_out)
    middle = x_ref[...].astype(F32) + gate_one * branch_one
    middle_ref[...] = middle
    keep(middle_ref, middle_out)
    normed, unused = norm_parts(middle)
    normed_two_ref[...] = low(normed * (1.0 + scale_two) + shift_two)
    keep(normed_two_ref, normed_two_out)
    links(11)
    pieces[8].to_sibling()
    save(7)
    for block in range(4):
        if block == 3:
            links(12)
            pieces[9].to_sibling()
            save(8)
        pre = contract(normed_two_ref[...], whole_piece(wide.at[4 + block]), 1, 0)
        act, slope = gelu_parts(pre + row_of(biases, 32 + 8 * block))
        act_ref[:, 1024 * block : 1024 * (block + 1)] = low(act)
        slope_ref[:, 1024 * block : 1024 * (block + 1)] = low(slope)
    keep(act_ref, act_out)
    keep(slope_ref, slope_out)
    for block in range(4):
        if block == 0:
            pieces[10].to_sibling()
        elif block == 1:
            pieces[11].to_sibling()
            save(9)
        else:
            save(8 + block)
        flat[0, :, 256 * block : 256 * (block + 1)] = contract(
            act_ref[...], whole_piece(down.at[block]), 1, 0
        )
    branch_two = flat[0] + row_of(biases, 64)
    layer_out_ref[...] = low(middle_ref[...] + gate_two * branch_two)
    gate_two_grad_ref[...] = jnp.sum(
        cotangent_ref[...].astype(F32) * branch_two, axis=0, keepdims=True
    )
    wire.drain()
    for copy in saved:
        copy.wait()


def vmem(shape, dtype=F32):
    return pltpu.VMEM(shape, dtype)


def run_forward(x, level, table, biases, w_qkv, w_out, w_up, w_down, w_ada, cotangent):
    shape = jax.ShapeDtypeStruct
    small = [
        ((256, 1024), BF16),
        ((8, 1, 512), F32),
        ((8, 1024), F32),
        ((32, 128), F32),
        ((128, 128), F32),
        ((1, 1024), F32),
    ]
    gathered = [((8, 4, 4, 2, 32, 1024), BF16), ((4, 4, 4, 2, 128, 256), BF16)]
    kept = (
        [((8, 256, 128), BF16)] * 4
        + [((256, 1024), BF16)] * 3
        + [((256, 1024), F32)] * 2
        + [((256, 4096), BF16)] * 2
        + [((256, 128), F32)] * 2
    )
    fetched = [
        ((32, 1024), F32),
        ((32, 4096), F32),
        ((128, 1024), F32),
        ((32, 6144), F32),
        ((256, 1024), BF16),
    ]
    in_vmem = pl.BlockSpec(memory_space=pltpu.VMEM)
    anywhere = pl.BlockSpec(memory_space=pl.ANY)
    scratch = [vmem(*array) for array in kept + fetched + gathered]
    scratch += [
        vmem((4, 8, 8, 128)),
        vmem((4, 8, 8, 128)),
        vmem((3, 8, 8, 128)),
        vmem((8, 8, 128)),
        vmem((7, 8, 128)),
        vmem((24, 4, 16, 128), BF16),
        vmem((3, 24, 16, 128), BF16),
        vmem((384, 128)),
        vmem((8, 48, 128)),
        vmem((7, 48, 128)),
        vmem((120, 128)),
        vmem((256, 128)),
        vmem((8, 128)),
        vmem((1, 256, 1024)),
        vmem((8, 256, 512)),
        pltpu.SemaphoreType.DMA((78,)),
        pltpu.SemaphoreType.DMA((82,)),
        pltpu.SemaphoreType.DMA((8,)),
        pltpu.SemaphoreType.DMA((8,)),
        pltpu.SemaphoreType.DMA((32,)),
    ]
    return pl.pallas_call(
        forward_kernel,
        out_shape=[shape(*out) for out in small + gathered + kept],
        in_specs=[in_vmem, pl.BlockSpec(memory_space=pltpu.SMEM)] + [in_vmem] * 7 + [anywhere] * 5,
        out_specs=[in_vmem] * len(small) + [anywhere] * len(gathered + kept),
        scratch_shapes=scratch,
        compiler_params=pltpu.CompilerParams(
            collective_id=0, has_side_effects=True, vmem_limit_bytes=VMEM_LIMIT
        ),
        name="block_forward",
    )(x, level, table, *biases, w_qkv, w_out, w_up, w_down, w_ada, cotangent)


SLOTS = 5


class Scatter:
    def __init__(self, wire, place, index, terms, buffers, credit, finish):
        self.wire, self.place, self.index, self.terms = wire, place, index, terms
        from_core, from_far, from_xy, from_z = buffers
        self.from_core = from_core.at[index % SLOTS]
        self.from_far = from_far.at[index]
        self.from_xy = from_xy.at[index]
        self.from_z = from_z.at[index]
        self.credit, self.finish = credit, finish
        self.mine = []
        self.rest = []

    def send(self, source, target, device, only=None, landing=None):
        copy = self.wire.send(source, target, device, only, landing)
        self.mine.append(copy)
        return copy

    def batch(self, whole, parts, landing=None):
        batch = self.wire.send_all(whole, parts, landing)
        self.mine += batch.copies
        return batch

    def to_sibling(self):
        place = self.place
        if self.index >= SLOTS:
            pl.semaphore_wait(self.credit, 1)
        self.coming = [
            self.send(self.terms.at[:, :, place.other], self.from_core, place.sibling)
        ]

    def far_to_sibling(self):
        place = self.place
        far = self.terms.at[place.far_dp, :, place.other]
        self.coming = [self.send(far, self.from_core.at[place.far_dp], place.sibling)]

    def rest_to_sibling(self):
        place = self.place
        parts = [
            (self.terms.at[dp, :, place.other], self.from_core.at[dp], place.sibling)
            for dp in (place.x_dp, place.y_dp, place.dp)
        ]
        self.rest = [self.batch(self.from_core.at[pl.ds(0, 3)], parts)]

    def across(self, last):
        place, terms, core = self.place, self.terms, self.place.core
        arrive(self.coming)
        far = place.far_dp
        terms[far, :, core] = terms[far, :, core] + self.from_core[far]
        to_x, to_y = place.at_dp(place.x_dp), place.at_dp(place.y_dp)
        parts = [
            (terms.at[far, pl.ds(0, 2), core], self.from_far.at[0], to_x),
            (terms.at[far, pl.ds(2, 2), core], self.from_far.at[1], to_y),
        ]
        self.coming = [self.batch(self.from_far, parts)]
        arrive(self.rest)
        for group in (place.x_dp, place.y_dp, place.dp):
            terms[group, :, core] = terms[group, :, core] + self.from_core[group]
        if not last:
            pl.semaphore_signal(
                self.credit, inc=1, device_id=place.sibling, device_id_type=MESH_ID
            )

    def along_xy(self):
        place, terms, core = self.place, self.terms, self.place.core
        arrive(self.coming)
        first, second = pl.ds(0, 2), pl.ds(2, 2)
        terms[place.y_dp, first, core] = terms[place.y_dp, first, core] + self.from_far[0]
        terms[place.x_dp, second, core] = terms[place.x_dp, second, core] + self.from_far[1]
        parts = [
            (terms.at[dp, :, core], self.from_xy.at[slot], place.at_dp(dp))
            for slot, dp in enumerate((place.x_dp, place.y_dp))
        ]
        self.coming = [self.batch(self.from_xy, parts)]

    def gather_shares(self):
        place, terms, core = self.place, self.terms, self.place.core
        arrive(self.coming)
        own = terms[place.dp, :, core].astype(F32)
        self.shares = self.from_xy.at[0]
        self.shares[...] = low(total_of(own, self.from_xy, 2))
        self.wire.drain(self.mine)
        self.mine = []

    def along_z(self):
        place, shares = self.place, self.shares
        pair = place.at_z_chip(place.z_pair)
        beyond = shares.at[pl.ds(place.z_beyond, 2)]
        self.first = self.send(shares.at[place.z_pair], self.from_z.at[0], pair)
        self.carried = self.send(beyond, self.from_z.at[pl.ds(2, 2)], pair, place.z_end)

    def pass_z(self):
        place, shares = self.place, self.shares

        @pl.when(place.z_middle)
        def _():
            self.carried.wait_recv()
            beyond = shares.at[pl.ds(place.z_beyond, 2)]
            beyond[...] = beyond[...] + self.from_z[2:4]

        self.second = None
        for z in ((place.z + 2) % 4, 3 - place.z):
            self.second = self.send(
                shares.at[z],
                self.from_z.at[1],
                place.at_z_chip(z),
                place.z_middle,
                landing=self.second,
            )

    def end(self):
        arrive([self.first, self.second])
        own = self.shares[self.place.z].astype(F32)
        self.finish(total_of(own, self.from_z, 2))
        self.wire.drain(self.mine)


class CoreGather:
    def __init__(self, wire, place, ref):
        self.wire, self.place, self.ref = wire, place, ref

    def along_seq(self):
        place = self.place
        own = self.ref.at[place.dp, place.z, place.core]
        parts = [(own, own, place.at_z_chip((place.z + step) % 4)) for step in (1, 2, 3)]
        self.first = self.wire.send_all(self.ref.at[0, pl.ds(0, 3), 0], parts)

    def along_dp_by_core(self):
        place = self.place
        collect(self.first)
        own = self.ref.at[place.dp, :, place.core]
        parts = [(own, own, place.at_dp(dp)) for dp in place.dp_peers]
        self.first = self.wire.send_all(self.ref.at[pl.ds(0, 3), :, 0], parts)

    def to_sibling(self):
        place = self.place
        collect(self.first)
        mine = self.ref.at[:, :, place.core]
        self.last = self.wire.send(mine, mine, place.sibling)

    def finish_by_core(self):
        arrive([self.last])
        self.wire.drain([self.last])


def norm_back(normed, inverse, grad):
    mean = jnp.mean(grad, axis=1, keepdims=True)
    along = jnp.mean(grad * normed, axis=1, keepdims=True)
    return (grad - mean - normed * along) * inverse


def column_sum(values):
    return jnp.sum(values, axis=0, keepdims=True)


def pair_deltas(attended, grad_heads, deltas):
    lane = lax.broadcasted_iota(jnp.int32, (8, 128), 1)
    line = lax.broadcasted_iota(jnp.int32, (8, 128), 0)
    picked = jnp.where(lane // 64 == line, 1.0, 0.0).astype(F32)
    for frame in range(8):
        product = attended[frame].astype(F32) * grad_heads[frame].astype(F32)
        sums = contract(picked, product, 1, 1, precision=lax.Precision.HIGHEST)
        deltas[frame] = jnp.concatenate([sums[0:1], sums[1:2]], axis=1)


def frame_pairs():
    for first in range(4):
        last = 7 - first
        yield [(query, first) for query in range(first, last + 1)], first
        yield [(last, key) for key in range(first + 1, last + 1)], last


def attend_pair_back(query_frame, key_frame, heads, log_total, grad_heads, deltas, sums, fresh):
    query, keys, values = heads
    pair = split_heads(query[query_frame])
    grad_pair = split_heads(grad_heads[query_frame])
    weights = jnp.exp(contract(keys[key_frame], pair, 1, 1) - log_total[query_frame])
    grad_weights = contract(values[key_frame], grad_pair, 1, 1)
    grad_scores = low(weights * (grad_weights - deltas[query_frame]))
    turned = contract(keys[key_frame], grad_scores, 0, 0)
    parts = (
        (query_frame, jnp.concatenate([turned[:64, :256], turned[64:, 256:]], axis=0)),
        (key_frame, contract(grad_scores, pair, 1, 0)),
        (key_frame, contract(low(weights), grad_pair, 1, 0)),
    )
    for total, (frame, part), started in zip(sums, parts, fresh):
        if frame in started:
            total[frame] += part
        else:
            started.add(frame)
            total[frame] = part


def backward_kernel(
    cotangent_ref,
    log_total_ref,
    modulation_ref,
    embedded_ref,
    one_hot_ref,
    gate_two_grad_ref,
    wide,
    down,
    act_in,
    slope_in,
    normed_two_in,
    middle_in,
    branch_one_in,
    query_in,
    keys_in,
    values_in,
    attended_in,
    tokens_in,
    x_in,
    normed_one_in,
    cosine_in,
    sine_in,
    w_ada_in,
    grad_hidden_ref,
    grad_table_ref,
    grad_ada_ref,
    grad_ada_bias_ref,
    grad_qkv_ref,
    grad_out_ref,
    grad_up_ref,
    grad_down_ref,
    grad_bias_ref,
    hidden,
    slope_ref,
    normed_two_ref,
    middle_ref,
    branch_one_ref,
    query_ref,
    keys_ref,
    values_ref,
    attended_ref,
    attended_tokens,
    x_ref,
    normed_one_ref,
    cosine_ref,
    sine_ref,
    w_ada_ref,
    terms,
    from_core,
    from_far,
    from_xy,
    from_z,
    down_block,
    wide_block,
    grad_two,
    grad_one,
    grad_tokens,
    grad_heads,
    deltas,
    query_sum,
    keys_sum,
    values_sum,
    query_back,
    keys_back,
    values_back,
    qkv_back,
    running,
    bias_lines,
    bias_dp,
    bias_sum,
    bias_seq,
    mod_grads,
    mod_lines,
    embedded_grads,
    send_sems,
    recv_sems,
    back_send,
    back_recv,
    local_sems,
    credit,
):
    place = Place()
    wire = Wire(place, send_sems, recv_sems)
    dp, seq, core = place.dp, place.seq, place.core
    loads = {}
    local = Local(local_sems)

    def load(name, source, target):
        loads[name] = local.start(source, target)

    def load_down(block):
        load(("down", block), down.at[:, block], down_block)

    def load_wide(block):
        load(("wide", block), wide.at[block], wide_block.at[block % 2])

    load("act", act_in, hidden)
    load_down(0)
    load("slope", slope_in, slope_ref)
    load_wide(4)
    load_wide(5)
    later = (
        (normed_two_in, normed_two_ref),
        (middle_in, middle_ref),
        (branch_one_in, branch_one_ref),
        (query_in, query_ref),
        (keys_in, keys_ref),
        (values_in, values_ref),
        (attended_in, attended_ref),
        (tokens_in, attended_tokens),
        (x_in, x_ref),
        (normed_one_in, normed_one_ref),
        (cosine_in, cosine_ref),
        (sine_in, sine_ref),
        (w_ada_in, w_ada_ref),
    )
    for index, (source, target) in enumerate(later):
        load(index, source, target)
    place.greet()
    scale_one = modulation_ref[1:2, :]
    gate_one = modulation_ref[2:3, :]
    scale_two = modulation_ref[4:5, :]
    gate_two = modulation_ref[5:6, :]
    cotangent = cotangent_ref[...].astype(F32)
    grad_two[...] = low(cotangent * gate_two)

    def keep_bias(first, grad):
        bias_lines[first : first + 8, :] = lines_of(column_sum(grad.astype(F32)))

    bias_lines[72:80, :] = jnp.zeros((8, 128), F32)
    keep_bias(64, grad_two[...])

    def finish(index):
        def store(total):
            if index < 4:
                grad_down_ref[32 * index : 32 * (index + 1), :] = total
            elif index < 8:
                grad_up_ref[:, 1024 * (index - 4) : 1024 * (index - 3)] = total
            elif index == 8:
                grad_out_ref[...] = total
            else:
                grad_qkv_ref[:, 1024 * (index - 9) : 1024 * (index - 8)] = total

        return store

    buffers = (from_core, from_far, from_xy, from_z)
    pieces = [
        Scatter(
            wire, place, index, terms.at[index % SLOTS], buffers, credit, finish(index)
        )
        for index in range(12)
    ]
    loads["act"].wait()
    for group in (place.far_dp, place.x_dp, place.y_dp, place.dp):
        for z in range(4):
            columns = pl.ds(pl.multiple_of(group * 1024 + 256 * z, 256), 256)
            part = low(contract(hidden[:, columns], grad_two[...], 0, 0)).reshape(2, 4, 32, 1024)
            for index in range(4):
                terms[index, group, z] = part[:, index]
        if group is place.far_dp:
            for index in range(4):
                pieces[index].far_to_sibling()
    for index in range(4):
        pieces[index].rest_to_sibling()

    def make_terms(index):
        for group in range(4):
            rows = slice(256 * group, 256 * (group + 1))
            if index < 8:
                left = normed_two_ref[:, rows]
                right = hidden[:, 1024 * (index - 4) : 1024 * (index - 3)]
            elif index == 8:
                left, right = attended_tokens[:, rows], grad_one[...]
            else:
                left, right = normed_one_ref[:, rows], qkv_back[index - 9]
            part = low(contract(left, right, 0, 0))
            terms[index % SLOTS, group] = part.reshape(4, 2, 32, 1024)

    done = [0, 0, 0]

    reached = [0, 0, 0]

    def advance(across, along, gathered):
        for stage, last in enumerate((across, along, gathered)):
            while reached[stage] <= min(last, 11):
                index = reached[stage]
                if stage == 0:
                    pieces[index].across(index + SLOTS >= 12)
                elif stage == 1:
                    pieces[index].along_xy()
                else:
                    pieces[index].gather_shares()
                reached[stage] += 1

    def begin(index):
        make_terms(index)
        pieces[index].to_sibling()

    def tick(step):
        advance(step - 1, step - 3, step - 5)
        if step >= 4:
            begin(step)

    def settle(sent, passed, ended):
        for stage, last in enumerate((sent, passed, ended)):
            while done[stage] <= min(last, 11):
                piece = pieces[done[stage]]
                (piece.along_z, piece.pass_z, piece.end)[stage]()
                done[stage] += 1

    tick(1)
    tick(2)
    loads["slope"].wait()
    for block in range(4):
        loads[("down", block)].wait()
        grad_act = None
        for index in range(4):
            weight = down_block[index].reshape(1024, 256)
            part = contract(grad_two[:, 256 * index : 256 * (index + 1)], weight, 1, 1)
            grad_act = part if grad_act is None else grad_act + part
        if block < 3:
            load_down(block + 1)
        columns = slice(1024 * block, 1024 * (block + 1))
        grad_pre = low(grad_act * slope_ref[:, columns].astype(F32))
        hidden[:, columns] = grad_pre
        keep_bias(32 + 8 * block, grad_pre)
        loads[("wide", 4 + block)].wait()
        part = contract(grad_pre, whole_piece(wide_block.at[block % 2]), 1, 1)
        running[...] = part if block == 0 else running[...] + part
        load_wide((6, 7, 2, 3)[block])
        if block == 1:
            tick(3)
    for index in range(len(later)):
        loads[index].wait()
    normed, inverse = norm_parts(middle_ref[...])
    grad_normed = running[...]
    grad_shift_two = column_sum(grad_normed)
    grad_scale_two = column_sum(grad_normed * normed)
    grad_middle = cotangent_ref[...].astype(F32) + norm_back(
        normed, inverse, grad_normed * (1.0 + scale_two)
    )
    running[...] = grad_middle
    grad_gate_one = column_sum(grad_middle * branch_one_ref[...])
    grad_one[...] = low(grad_middle * gate_one)
    keep_bias(24, grad_one[...])
    loads[("wide", 3)].wait()
    grad_tokens[...] = low(contract(grad_one[...], whole_piece(wide_block.at[1]), 1, 1))
    load_wide(1)
    parts = []
    for other in place.seq_peers:
        columns = pl.ds(pl.multiple_of(other * 128, 128), 128)
        parts.append((grad_tokens.at[:, columns], grad_heads.at[seq], place.at_seq(other)))
    head_copies = wire.send_all(grad_heads.at[pl.ds(0, 7)], parts)
    own_columns = pl.ds(pl.multiple_of(seq * 128, 128), 128)
    grad_heads[seq] = grad_tokens[:, own_columns]
    tick(4)
    tick(5)
    collect(head_copies)
    backs = (query_back, keys_back, values_back)

    def back_copy(part, frame, source):
        columns = pl.ds(pl.multiple_of(source * 128, 128), 128)
        return pltpu.make_async_remote_copy(
            src_ref=backs[part].at[frame],
            dst_ref=qkv_back.at[part, :, columns],
            send_sem=back_send.at[part, frame],
            recv_sem=back_recv.at[part, source],
            device_id=place.at_seq(frame),
            device_id_type=MESH_ID,
        )

    def send_back(frame):
        @pl.when(seq != frame)
        def _():
            for part in range(3):
                back_copy(part, frame, seq).start()

        @pl.when(seq == frame)
        def _():
            for part in range(3):
                qkv_back[part, :, own_columns] = backs[part][frame]

    pair_deltas(attended_ref, grad_heads, deltas)
    heads = (query_ref, keys_ref, values_ref)
    fresh = (set(), set(), set())
    for pairs, frame in frame_pairs():
        for query_frame, key_frame in pairs:
            attend_pair_back(
                query_frame,
                key_frame,
                heads,
                log_total_ref,
                grad_heads,
                deltas,
                (query_sum, keys_sum, values_sum),
                fresh,
            )
        query_back[frame] = low(query_sum[frame].T * 0.125)
        keys_back[frame] = low(keys_sum[frame])
        values_back[frame] = low(values_sum[frame])
        send_back(frame)
        if frame in (7, 2):
            tick(6 if frame == 7 else 7)
    tick(8)
    advance(8, 7, 4)
    for part in range(3):
        for other in place.seq_peers:
            back_copy(part, other, other).wait_recv()
    cosine, sine = cosine_ref[...], sine_ref[...]
    grad_normed = None
    for part in range(3):
        if part < 2:
            for group in range(8):
                columns = slice(128 * group, 128 * (group + 1))
                grad = qkv_back[part, :, columns].astype(F32)
                qkv_back[part, :, columns] = low(grad * cosine - half_turn(grad) * sine)
        keep_bias(8 * part, qkv_back[part])
        index = (2, 1, 0)[part]
    for block, slot in ((2, 0), (1, 1), (0, 0)):
        loads[("wide", block)].wait()
        part = contract(qkv_back[block], whole_piece(wide_block.at[slot]), 1, 1)
        grad_normed = part if grad_normed is None else grad_normed + part
        if block == 2:
            load_wide(0)
    bias_copies = spread_dp(wire, place, lambda dp: bias_lines, bias_dp)
    normed, inverse = norm_parts(x_ref[...].astype(F32))
    grad_shift_one = column_sum(grad_normed)
    grad_scale_one = column_sum(grad_normed * normed)
    grad_hidden_ref[...] = low(
        running[...] + norm_back(normed, inverse, grad_normed * (1.0 + scale_one))
    )
    rows = (
        grad_shift_one,
        grad_scale_one,
        grad_gate_one,
        grad_shift_two,
        grad_scale_two,
        gate_two_grad_ref[...],
    )
    mod_grads[dp, place.z, core] = low(jnp.concatenate([lines_of(row) for row in rows], axis=0))
    mod_gather = CoreGather(wire, place, mod_grads)
    mod_gather.along_seq()
    begin(9)
    settle(3, -1, -1)
    advance(8, 8, 5)
    begin(10)
    advance(9, 8, 6)
    settle(4, -1, -1)
    begin(11)
    advance(10, 9, 6)
    settle(5, 2, -1)
    mod_gather.along_dp_by_core()
    collect(bias_copies)
    bias_sum[...] = total_of(bias_lines[...], bias_dp, 3)
    bias_copies = spread_seq(wire, place, lambda seq: bias_sum, bias_seq)
    advance(11, 10, 7)
    settle(7, 4, -1)
    advance(11, 11, 8)
    settle(8, 6, -1)
    advance(11, 11, 9)
    settle(9, 7, 2)
    mod_gather.to_sibling()
    mod_gather.finish_by_core()
    lines = mod_grads[...].astype(F32).reshape(1536, 128)
    mod_lines[...] = lines
    grad_ada_bias_ref[...] = jnp.sum(lines.reshape(32, 48, 128), axis=0)
    embedded = embedded_ref[...]
    share = 1.0 / (1.0 + jnp.exp(-embedded))
    silu_in = low(embedded * share)[:, :32]
    empty = jnp.zeros((96, 128), BF16)
    grad_silu = None
    for block in range(6):
        parts = []
        for line in range(8):
            part = mod_lines[pl.ds(8 * block + line, 32, stride=48), :]
            parts.append(jnp.concatenate([low(part), empty], axis=0))
        every = jnp.concatenate(parts, axis=1)
        columns = slice(1024 * block, 1024 * (block + 1))
        grad_ada_ref[:, columns] = contract(silu_in, every[:32], 1, 0)
        part = contract(low(w_ada_ref[:, columns]), every, 1, 1)
        grad_silu = part if grad_silu is None else grad_silu + part
    grad_embedded = grad_silu * share * (1.0 + embedded * (1.0 - share))
    embedded_grads[dp, seq] = pack_lanes(grad_embedded.reshape(1, 4, 8, 128))[0]
    embedded_gather = SmallGather(wire, place, embedded_grads)
    embedded_gather.along_seq()
    advance(11, 11, 10)
    settle(10, 8, 4)
    advance(11, 11, 11)
    settle(11, 10, 4)
    settle(11, 11, 4)
    embedded_gather.along_dp()
    collect(bias_copies)
    grad_bias_ref[...] = total_of(bias_sum[...], bias_seq, 7)
    settle(11, 11, 9)
    embedded_gather.finish()
    every_grad = jnp.concatenate(
        [unpack_lanes(embedded_grads[group, frame]) for group in range(4) for frame in range(8)],
        axis=0,
    )
    grad_table_ref[...] = contract(
        one_hot_ref[...],
        every_grad,
        0,
        1,
        precision=lax.Precision.HIGHEST,
    )[:32]
    settle(11, 11, 11)
    for part in range(3):
        for other in place.seq_peers:
            back_copy(part, other, other).wait_send()
    wire.drain()


def run_backward(cotangent, small, gathered, kept, x, w_ada):
    shape = jax.ShapeDtypeStruct
    outs = [
        ((256, 1024), BF16),
        ((32, 1024), F32),
        ((32, 6144), F32),
        ((48, 128), F32),
        ((32, 3072), F32),
        ((32, 1024), F32),
        ((32, 4096), F32),
        ((128, 1024), F32),
        ((80, 128), F32),
    ]
    query, keys, values, attended, tokens, normed_one, normed_two = kept[:7]
    middle, branch_one, act, slope, cosine, sine = kept[7:]
    fetched = (act, slope, normed_two, middle, branch_one, query, keys, values, attended)
    fetched += (tokens, x, normed_one, cosine, sine, w_ada)
    in_vmem = pl.BlockSpec(memory_space=pltpu.VMEM)
    anywhere = pl.BlockSpec(memory_space=pl.ANY)
    scratch = [vmem(array.shape, array.dtype) for array in fetched]
    scratch += [
        vmem((SLOTS, 4, 4, 2, 32, 1024), BF16),
        vmem((SLOTS, 4, 4, 32, 1024), BF16),
        vmem((12, 2, 2, 32, 1024), BF16),
        vmem((12, 2, 4, 32, 1024), BF16),
        vmem((12, 4, 32, 1024), BF16),
        vmem((4, 4, 2, 128, 256), BF16),
        vmem((2, 4, 4, 2, 32, 1024), BF16),
        vmem((256, 1024), BF16),
        vmem((256, 1024), BF16),
        vmem((256, 1024), BF16),
        vmem((8, 256, 128), BF16),
        vmem((8, 1, 512)),
        vmem((8, 128, 256)),
        vmem((8, 256, 128)),
        vmem((8, 256, 128)),
        vmem((8, 256, 128), BF16),
        vmem((8, 256, 128), BF16),
        vmem((8, 256, 128), BF16),
        vmem((3, 256, 1024), BF16),
        vmem((256, 1024)),
        vmem((80, 128)),
        vmem((3, 80, 128)),
        vmem((80, 128)),
        vmem((7, 80, 128)),
        vmem((4, 4, 2, 48, 128), BF16),
        vmem((1536, 128)),
        vmem((4, 8, 8, 128)),
        pltpu.SemaphoreType.DMA((58,)),
        pltpu.SemaphoreType.DMA((85,)),
        pltpu.SemaphoreType.DMA((3, 8)),
        pltpu.SemaphoreType.DMA((3, 8)),
        pltpu.SemaphoreType.DMA((32,)),
        pltpu.SemaphoreType.REGULAR,
    ]
    return pl.pallas_call(
        backward_kernel,
        out_shape=[shape(*out) for out in outs],
        in_specs=[in_vmem] * 6 + [anywhere] * 17,
        out_specs=[in_vmem] * 9,
        scratch_shapes=scratch,
        compiler_params=pltpu.CompilerParams(
            collective_id=1, has_side_effects=True, vmem_limit_bytes=VMEM_LIMIT
        ),
        name="block_backward",
    )(cotangent, *small, *gathered, *fetched)


def finish_kernel(lines_ref, ada_lines_ref, *refs):
    device = lax.axis_index("dp") * 8 + lax.axis_index("seq")
    for index in range(8):
        refs[8 + index][...] = refs[index][...]
    for index, share in enumerate(BIAS_SHARE):
        lines, first = (lines_ref, BIAS_FIRST[index]) if index < 4 else (ada_lines_ref, 0)
        offset = device * share
        line = first + offset // 128
        pair = jnp.concatenate([lines[pl.ds(line, 1), :], lines[pl.ds(line + 1, 1), :]], axis=1)
        part = pltpu.roll(pair, (256 - offset % 128) % 256, 1)
        refs[16 + index][...] = part[:, :share].reshape(share)


def run_finish(lines, ada_lines, arrays):
    shape = jax.ShapeDtypeStruct
    in_vmem = pl.BlockSpec(memory_space=pltpu.VMEM)
    return pl.pallas_call(
        finish_kernel,
        out_shape=[shape(array.shape, array.dtype) for array in arrays]
        + [shape((share,), F32) for share in BIAS_SHARE],
        in_specs=[in_vmem] * 10,
        out_specs=[in_vmem] * 13,
        name="block_outputs",
    )(lines, ada_lines, *arrays)


def fast_body(
    hidden_in,
    noise_level,
    noise_table,
    w_ada,
    b_ada,
    w_qkv,
    b_qkv,
    w_out,
    b_out,
    w_up,
    b_up,
    w_down,
    b_down,
    grad_out,
):
    biases = (b_qkv, b_out, b_up, b_down, b_ada)
    x, cotangent = hidden_in[0], grad_out[0]
    results = run_forward(
        x, noise_level, noise_table, biases, w_qkv, w_out, w_up, w_down, w_ada, cotangent
    )
    layer_out, small, gathered, kept = results[0], results[1:6], results[6:8], results[8:]
    grads = run_backward(cotangent, small, gathered, kept, x, w_ada)
    grad_hidden, grad_table, grad_ada_w, ada_lines, *weight_grads, lines = grads
    outs = run_finish(
        lines, ada_lines, (layer_out, grad_hidden, grad_table, grad_ada_w, *weight_grads)
    )
    layer_out, grad_hidden, grad_table, grad_ada_w, qkv_w, out_w, up_w, down_w = outs[:8]
    qkv_b, out_b, up_b, down_b, ada_b = outs[8:]
    return (
        layer_out[None],
        grad_hidden[None],
        grad_table,
        grad_ada_w,
        ada_b,
        qkv_w,
        qkv_b,
        out_w,
        out_b,
        up_w,
        up_b,
        down_w,
        down_b,
    )


def solution(mesh):
    tokens = P("dp", "seq", None)
    matrix = P(ALL, None)
    vector = P(ALL)
    parameters = (matrix,) + (matrix, vector) * 5
    chips = dict(mesh.shape) == {"dp": 4, "seq": 8}
    return jax.shard_map(
        fast_body if chips else general_body,
        mesh=mesh,
        in_specs=(tokens, P("dp", "seq")) + parameters + (tokens,),
        out_specs=(tokens, tokens) + parameters,
        check_vma=False,
    )
```

```python
from functools import partial
import math

import jax
import jax.numpy as jnp
from jax import lax
from jax.experimental import pallas as pl
from jax.experimental.pallas import tpu as pltpu
from jax.sharding import PartitionSpec as P

H = 16
GRID_W = 16
PATCHES = 256


norm_eps = 1e-06
masked_score = -1e30
ALL = ("dp", "seq")
F32 = jnp.float32
BF16 = jnp.bfloat16


def layer_norm(values):
    centred = values - jnp.mean(values, axis=-1, keepdims=True)
    spread = jnp.mean(centred * centred, axis=-1, keepdims=True)
    return centred * lax.rsqrt(spread + norm_eps)


def modulate(values, shift_term, scale_term):
    return layer_norm(values) * (1.0 + scale_term) + shift_term


def turn_half(values):
    extent = values.shape[-1]
    side_part = 2 * (3 * extent // 16)
    pieces = []
    offset = 0
    for part_size in (extent - 2 * side_part, side_part, side_part):
        half_size = part_size // 2
        pieces.append(-values[..., offset + half_size : offset + part_size])
        pieces.append(values[..., offset : offset + half_size])
        offset = offset + part_size
    return jnp.concatenate(pieces, axis=-1)


def part_angles(places, part_size):
    half_size = part_size // 2
    rates = jnp.exp(-math.log(10000.0) * jnp.arange(half_size, dtype=F32) / half_size)
    angles = places.astype(F32)[:, None] * rates[None, :]
    return jnp.concatenate([angles, angles], axis=1)


def angle_table(places, extent):
    side_part = 2 * (3 * extent // 16)
    patch_index = places % PATCHES
    angles = jnp.concatenate(
        [
            part_angles(places // PATCHES, extent - 2 * side_part),
            part_angles(patch_index // GRID_W, side_part),
            part_angles(patch_index % GRID_W, side_part),
        ],
        axis=1,
    )
    return (jnp.cos(angles), jnp.sin(angles))


def rotate(values, cosine_table, sine_table):
    return values * cosine_table + turn_half(values) * sine_table


def unrotate(values, cosine_table, sine_table):
    return values * cosine_table - turn_half(values * sine_table)


def low(values):
    return values.astype(BF16)


def dot(left, right):
    return jnp.dot(left, right, preferred_element_type=F32)


def gather_rows(share):
    return lax.all_gather(low(share), ALL, axis=0, tiled=True)


def scatter_rows(whole):
    return lax.psum_scatter(whole, ALL, scatter_dimension=0, tiled=True)


def frame_modulation(noise_level, noise_table, w_ada, b_ada):
    levels = lax.all_gather(noise_level.reshape(-1), ALL, axis=0, tiled=True)
    device = lax.axis_index("dp") * lax.axis_size("seq") + lax.axis_index("seq")
    share = noise_table.shape[0]
    own_levels = device * share + jnp.arange(share, dtype=jnp.int32)
    one_hot = levels[:, None] == own_levels[None, :]
    found = dot(low(one_hot), low(noise_table))
    embedded = lax.psum_scatter(low(found), ALL, scatter_dimension=1, tiled=True).astype(F32)
    silu_in = low(jax.nn.silu(embedded))
    modulation = lax.psum_scatter(
        dot(silu_in, low(w_ada)), ALL, scatter_dimension=0, tiled=True
    ) + gather_rows(b_ada).astype(F32)
    return one_hot, embedded, silu_in, modulation


def frame_gradients(grad_modulation, one_hot, embedded, silu_in, w_ada):
    every = lax.all_gather(grad_modulation, ALL, axis=0, tiled=True)
    grad_ada_w = lax.dot_general(
        silu_in, every, (((0,), (0,)), ((), ())), preferred_element_type=F32
    )
    share = w_ada.shape[1] // lax.axis_size(ALL)
    device = lax.axis_index("dp") * lax.axis_size("seq") + lax.axis_index("seq")
    columns = lax.dynamic_slice_in_dim(every, device * share, share, axis=1)
    grad_ada_b = jnp.sum(columns.astype(F32), axis=0)
    grad_silu = lax.dot_general(
        every, low(w_ada), (((1,), (1,)), ((), ())), preferred_element_type=F32
    )
    unused, silu_back = jax.vjp(jax.nn.silu, embedded)
    grad_embedded = lax.all_gather(silu_back(grad_silu)[0], ALL, axis=1, tiled=True)
    grad_table = jnp.dot(
        one_hot.astype(F32).T, grad_embedded, precision=lax.Precision.HIGHEST
    )
    return grad_table, grad_ada_w, grad_ada_b


def to_heads(values):
    return lax.all_to_all(values, "seq", split_axis=2, concat_axis=1, tiled=True)


def to_tokens(values):
    return lax.all_to_all(values, "seq", split_axis=1, concat_axis=2, tiled=True)


def as_heads(values):
    return values.reshape(*values.shape[:2], -1, 64)


def query_blocks(array, axis):
    blocks = array.shape[axis] // PATCHES
    split = array.shape[:axis] + (blocks, PATCHES) + array.shape[axis + 1 :]
    return jnp.moveaxis(array.reshape(split), axis, 0)


def block_scores(query_block, keys, frame, score_scale):
    scores = (
        jnp.einsum("cqhd,ckhd->chqk", query_block, keys, preferred_element_type=F32) * score_scale
    )
    allowed = jnp.arange(keys.shape[1], dtype=jnp.int32) // PATCHES <= frame
    return jnp.where(allowed, scores, masked_score)


def attend(query, keys, values, score_scale):
    def one_block(block_in):
        query_block, frame = block_in
        scores = block_scores(query_block, keys, frame, score_scale)
        row_max = jnp.max(scores, axis=-1, keepdims=True)
        exponent = jnp.exp(scores - row_max)
        row_total = jnp.sum(exponent, axis=-1, keepdims=True)
        weighted = jnp.einsum(
            "chqk,ckhd->cqhd", low(exponent / row_total), values, preferred_element_type=F32
        )
        return low(weighted), (row_max + jnp.log(row_total))[..., 0]

    frames = jnp.arange(query.shape[1] // PATCHES, dtype=jnp.int32)
    attended, log_total = lax.map(one_block, (query_blocks(query, 1), frames))
    return (
        jnp.moveaxis(attended, 0, 1).reshape(query.shape),
        jnp.moveaxis(log_total, 0, 2).reshape(query.shape[0], query.shape[2], query.shape[1]),
    )


def attend_back(query, keys, values, grad_heads, log_total, row_delta, score_scale):
    def one_block(carried, block_in):
        query_block, grad_block, total_block, delta_block, frame = block_in
        scores = block_scores(query_block, keys, frame, score_scale)
        softmax_weights = jnp.exp(scores - total_block[..., None])
        grad_soft = jnp.einsum("cqhd,ckhd->chqk", grad_block, values, preferred_element_type=F32)
        grad_scores = low(softmax_weights * (grad_soft - delta_block[..., None]))
        query_grad = jnp.einsum("chqk,ckhd->cqhd", grad_scores, keys, preferred_element_type=F32)
        keys_grad = jnp.einsum(
            "chqk,cqhd->ckhd", grad_scores, query_block, preferred_element_type=F32
        )
        values_grad = jnp.einsum(
            "chqk,cqhd->ckhd", low(softmax_weights), grad_block, preferred_element_type=F32
        )
        return (carried[0] + keys_grad, carried[1] + values_grad), query_grad

    frames = jnp.arange(query.shape[1] // PATCHES, dtype=jnp.int32)
    empty = jnp.zeros(keys.shape, F32)
    (grad_keys, grad_values), grad_query = lax.scan(
        one_block,
        (empty, empty),
        (
            query_blocks(query, 1),
            query_blocks(grad_heads, 1),
            query_blocks(log_total, 2),
            query_blocks(row_delta, 2),
            frames,
        ),
    )
    grad_query = jnp.moveaxis(grad_query, 0, 1).reshape(query.shape)
    return grad_query * score_scale, grad_keys * score_scale, grad_values


def general_body(
    hidden_in,
    noise_level,
    noise_table,
    w_ada,
    b_ada,
    w_qkv,
    b_qkv,
    w_out,
    b_out,
    w_up,
    b_up,
    w_down,
    b_down,
    grad_out,
):
    qkv_w, qkv_b, out_w, out_b, up_w, up_b, down_w, down_b = [
        gather_rows(share)
        for share in (w_qkv, b_qkv, w_out, b_out, w_up, b_up, w_down, b_down)
    ]
    clip_count, patches, model_width = hidden_in.shape
    head_dim = model_width // H
    score_scale = 1.0 / math.sqrt(head_dim)
    head_shape = (clip_count, patches, H, head_dim)
    inputs = hidden_in.astype(F32)
    one_hot, embedded, silu_in, modulation = frame_modulation(
        noise_level, noise_table, w_ada, b_ada
    )
    shift_one, scale_one, gate_one, shift_two, scale_two, gate_two = [
        modulation[:, None, column_block * model_width : (column_block + 1) * model_width]
        for column_block in range(6)
    ]
    normed_one = low(modulate(inputs, shift_one, scale_one))
    qkv_all = dot(normed_one, qkv_w) + qkv_b.astype(F32)
    frame_own = lax.axis_index("seq")
    places = frame_own * patches + jnp.arange(patches, dtype=jnp.int32)
    cosine_local, sine_local = angle_table(places, head_dim)
    cosine_wide = cosine_local[None, :, None, :]
    sine_wide = sine_local[None, :, None, :]
    flat_shape = (clip_count, patches, model_width)

    def turned(block):
        part = qkv_all[..., block * model_width : (block + 1) * model_width]
        return low(rotate(part.reshape(head_shape), cosine_wide, sine_wide)).reshape(flat_shape)

    query = as_heads(to_heads(turned(0)))
    keys = as_heads(to_heads(turned(1)))
    values = as_heads(to_heads(low(qkv_all[..., 2 * model_width :])))
    attended, log_total = attend(query, keys, values, score_scale)
    attended_low = to_tokens(attended.reshape(*attended.shape[:2], -1))
    branch_one = dot(attended_low, out_w) + out_b.astype(F32)
    middle = inputs + gate_one * branch_one
    normed_two = low(modulate(middle, shift_two, scale_two))
    hidden_pre = dot(normed_two, up_w) + up_b.astype(F32)
    hidden_act = low(jax.nn.gelu(hidden_pre, approximate=True))
    branch_two = dot(hidden_act, down_w) + down_b.astype(F32)
    outputs = middle + gate_two * branch_two
    cotangent = grad_out.astype(F32)
    grad_gate_two = jnp.sum(cotangent * branch_two, axis=1)
    grad_branch_two = low(cotangent * gate_two)

    def weight_grad(left, right):
        whole = jnp.einsum("cpi,cpo->io", left, right, preferred_element_type=F32)
        return scatter_rows(low(whole)).astype(F32)

    def bias_grad(grad):
        return scatter_rows(jnp.sum(grad.astype(F32), axis=(0, 1)))

    def back_dot(grad, weight):
        return jnp.einsum("cpo,io->cpi", grad, weight, preferred_element_type=F32)

    grad_down_w = weight_grad(hidden_act, grad_branch_two)
    grad_down_b = bias_grad(grad_branch_two)
    grad_act = back_dot(grad_branch_two, down_w)
    unused, gelu_back = jax.vjp(partial(jax.nn.gelu, approximate=True), hidden_pre)
    grad_pre = low(gelu_back(grad_act)[0])
    grad_up_w = weight_grad(normed_two, grad_pre)
    grad_up_b = bias_grad(grad_pre)
    grad_normed_two = back_dot(grad_pre, up_w)
    unused, norm_two_back = jax.vjp(modulate, middle, shift_two, scale_two)
    grad_middle_norm, grad_shift_two, grad_scale_two = norm_two_back(grad_normed_two)
    grad_middle = cotangent + grad_middle_norm
    grad_gate_one = jnp.sum(grad_middle * branch_one, axis=1)
    grad_branch_one = low(grad_middle * gate_one)
    grad_out_w = weight_grad(attended_low, grad_branch_one)
    grad_out_b = bias_grad(grad_branch_one)
    grad_attended = low(back_dot(grad_branch_one, out_w))
    grad_heads = as_heads(to_heads(grad_attended))
    row_delta = jnp.sum(grad_heads.astype(F32) * attended.astype(F32), axis=-1).transpose(0, 2, 1)
    grad_query, grad_keys, grad_values = attend_back(
        query, keys, values, grad_heads, log_total, row_delta, score_scale
    )

    def home(grad):
        return to_tokens(low(grad).reshape(*grad.shape[:2], -1))

    def unturned(grad):
        wide = home(grad).astype(F32).reshape(head_shape)
        return low(unrotate(wide, cosine_wide, sine_wide)).reshape(flat_shape)

    grad_qkv = jnp.concatenate(
        [unturned(grad_query), unturned(grad_keys), home(grad_values)], axis=-1
    )
    grad_qkv_w = weight_grad(normed_one, grad_qkv)
    grad_qkv_b = bias_grad(grad_qkv)
    grad_normed_one = back_dot(grad_qkv, qkv_w)
    unused, norm_one_back = jax.vjp(modulate, inputs, shift_one, scale_one)
    grad_input_norm, grad_shift_one, grad_scale_one = norm_one_back(grad_normed_one)
    grad_input = grad_middle + grad_input_norm
    grad_modulation = low(
        jnp.concatenate(
            [
                grad_shift_one[:, 0],
                grad_scale_one[:, 0],
                grad_gate_one,
                grad_shift_two[:, 0],
                grad_scale_two[:, 0],
                grad_gate_two,
            ],
            axis=-1,
        )
    )
    grad_table, grad_ada_w, grad_ada_b = frame_gradients(
        grad_modulation, one_hot, embedded, silu_in, w_ada
    )
    return (
        low(outputs),
        low(grad_input),
        grad_table,
        grad_ada_w,
        grad_ada_b,
        grad_qkv_w,
        grad_qkv_b,
        grad_out_w,
        grad_out_b,
        grad_up_w,
        grad_up_b,
        grad_down_w,
        grad_down_b,
    )


MESH_ID = pl.DeviceIdType.MESH
VMEM_LIMIT = 63 * 1024 * 1024
HEADS_WIDE = 128


def contract(left, right, left_dim, right_dim, precision=None):
    return lax.dot_general(
        left,
        right,
        (((left_dim,), (right_dim,)), ((), ())),
        preferred_element_type=F32,
        precision=precision,
    )


class Place:
    def __init__(self):
        self.dp = lax.axis_index("dp")
        self.seq = lax.axis_index("seq")
        self.z = self.seq // 2
        self.core = self.seq % 2
        self.other = 1 - self.core
        self.x_dp = self.dp + 1 - 2 * (self.dp % 2)
        self.y_dp = (self.dp + 2) % 4
        self.far_dp = 3 - self.dp
        self.dp_peers = (self.x_dp, self.y_dp, self.far_dp)
        self.seq_peers = [(self.seq + step) % 8 for step in range(1, 8)]
        self.sibling = (self.dp, self.z * 2 + self.other)
        self.z_pair = self.z + 1 - 2 * (self.z % 2)
        self.z_end = (self.z == 0) | (self.z == 3)
        self.z_middle = (self.z == 1) | (self.z == 2)
        self.z_beyond = 2 - 2 * (self.z // 2)

    def at_dp(self, dp):
        return (dp, self.seq)

    def at_seq(self, seq):
        return (self.dp, seq)

    def at_z_chip(self, z):
        return (self.dp, z * 2 + self.core)

    def greet(self):
        barrier = pltpu.get_barrier_semaphore()
        peers = [self.at_dp(dp) for dp in self.dp_peers]
        peers += [self.at_seq(seq) for seq in self.seq_peers]
        for peer in peers:
            pl.semaphore_signal(barrier, inc=1, device_id=peer, device_id_type=MESH_ID)
        pl.semaphore_wait(barrier, len(peers))


def guarded(only, act):
    if only is None:
        act()
    else:
        pl.when(only)(act)


class Copy:
    def __init__(self, wire, source, target, device, only, landing):
        self.wire, self.only = wire, only
        self.sending = wire.take_send()
        self.landing = wire.take_recv() if landing is None else landing.landing
        self.copy = wire.describe(source, target, device, self.sending, self.landing)
        guarded(only, self.copy.start)

    def wait_send(self):
        guarded(self.only, self.copy.wait_send)
        self.wire.free.append(self.sending)

    def wait_recv(self):
        self.copy.wait_recv()


class Batch:
    def __init__(self, wire, copies, whole):
        self.wire, self.copies, self.whole = wire, copies, whole
        self.landing = copies[0].landing

    def wait_recv(self):
        first = self.copies[0]
        place = self.wire.place
        self.wire.describe(
            self.whole, self.whole, place.sibling, first.sending, self.landing
        ).wait_recv()


class Wire:
    def __init__(self, place, send_sems, recv_sems):
        self.place = place
        self.send_sems = send_sems
        self.recv_sems = recv_sems
        self.sends = 0
        self.recvs = 0
        self.free = []
        self.sent = []

    def take_send(self):
        if self.free:
            return self.free.pop(0)
        self.sends += 1
        assert self.sends <= self.send_sems.shape[0]
        return self.sends - 1

    def take_recv(self):
        self.recvs += 1
        assert self.recvs <= self.recv_sems.shape[0]
        return self.recvs - 1

    def describe(self, source, target, device, sending, landing):
        return pltpu.make_async_remote_copy(
            src_ref=source,
            dst_ref=target,
            send_sem=self.send_sems.at[sending],
            recv_sem=self.recv_sems.at[landing],
            device_id=device,
            device_id_type=MESH_ID,
        )

    def send(self, source, target, device, only=None, landing=None):
        copy = Copy(self, source, target, device, only, landing)
        self.sent.append(copy)
        return copy

    def send_all(self, whole, parts, landing=None):
        copies = []
        for source, target, device in parts:
            copies.append(self.send(source, target, device, None, landing))
            landing = copies[0] if landing is None else landing
        return Batch(self, copies, whole)

    def drain(self, copies=None):
        copies = list(self.sent if copies is None else copies)
        for copy in copies:
            copy.wait_send()
        self.sent = [copy for copy in self.sent if not any(copy is done for done in copies)]


class Local:
    def __init__(self, sems):
        self.sems = sems
        self.used = 0

    def start(self, source, target):
        copy = pltpu.make_async_copy(source, target, self.sems.at[self.used])
        self.used += 1
        assert self.used <= self.sems.shape[0]
        copy.start()
        return copy


def arrive(copies):
    for copy in copies:
        copy.wait_recv()


class Gather:
    def __init__(self, wire, place, ref):
        self.wire, self.place, self.ref = wire, place, ref
        self.early = None
        self.mine = []

    def send(self, source, device, only=None, landing=None):
        copy = self.wire.send(source, source, device, only, landing)
        self.mine.append(copy)
        return copy

    def batch(self, whole, parts, landing=None):
        batch = self.wire.send_all(
            whole, [(part, part, device) for part, device in parts], landing
        )
        self.mine += batch.copies
        return batch

    def along_z(self):
        place = self.place
        own = self.ref.at[place.dp, place.z, place.core]
        across = place.at_z_chip(2 - place.z // 2)
        self.paired = self.send(own, place.at_z_chip(place.z_pair))
        self.crossed = self.send(own, across)

    def pass_z(self):
        place = self.place
        two = self.ref.at[place.dp, pl.ds(place.z_beyond, 2), place.core]
        both = Batch(self.wire, [self.crossed], two)
        guarded(place.z_middle, both.wait_recv)
        self.passed = self.send(two, place.at_z_chip(place.z_pair), place.z_middle)

    def all_z(self):
        arrive([self.paired])
        guarded(self.place.z_end, self.passed.wait_recv)

    def xy_devices(self):
        place = self.place
        return [place.at_dp(dp) for dp in (place.x_dp, place.y_dp)]

    def own_xy(self):
        place = self.place
        own = self.ref.at[place.dp, place.z, place.core]
        whole = self.ref.at[pl.ds(0, 2), :, place.core]
        self.early = self.batch(whole, [(own, device) for device in self.xy_devices()])

    def along_xy(self):
        place = self.place
        self.all_z()
        if self.early:
            parts = []
            for step in (1, 2, 3):
                part = self.ref.at[place.dp, (place.z + step) % 4, place.core]
                parts += [(part, device) for device in self.xy_devices()]
            self.batch(None, parts, self.early)
            self.coming = self.early
            return
        own = self.ref.at[place.dp, :, place.core]
        whole = self.ref.at[pl.ds(0, 2), :, place.core]
        self.coming = self.batch(whole, [(own, device) for device in self.xy_devices()])

    def across(self):
        place = self.place
        arrive([self.coming])
        from_x = self.ref.at[place.x_dp, pl.ds(0, 2), place.core]
        from_y = self.ref.at[place.y_dp, pl.ds(2, 2), place.core]
        whole = self.ref.at[0, :, place.core]
        to_x, to_y = self.xy_devices()
        self.coming = self.batch(whole, [(from_x, to_y), (from_y, to_x)])

    def to_sibling(self):
        place = self.place
        arrive([self.coming])
        self.coming = self.send(self.ref.at[:, :, place.core], place.sibling)

    def finish(self):
        arrive([self.coming])
        self.wire.drain(self.mine)


class SmallGather:
    def __init__(self, wire, place, ref):
        self.wire, self.place, self.ref = wire, place, ref

    def along_seq(self):
        place = self.place
        own = self.ref.at[place.dp, place.seq]
        self.seq_coming = self.wire.send_all(
            self.ref.at[0, pl.ds(0, 7)],
            [(own, own, place.at_seq(seq)) for seq in place.seq_peers],
        )

    def along_dp(self):
        place = self.place
        arrive([self.seq_coming])
        own = self.ref.at[place.dp]
        self.dp_coming = self.wire.send_all(
            self.ref.at[pl.ds(0, 3)], [(own, own, place.at_dp(dp)) for dp in place.dp_peers]
        )

    def finish(self):
        arrive([self.dp_coming])
        self.wire.drain(self.seq_coming.copies + self.dp_coming.copies)


def spread_dp(wire, place, part_of, slots):
    parts = [
        (part_of(dp), slots.at[index], place.at_dp(dp)) for index, dp in enumerate(place.dp_peers)
    ]
    return wire.send_all(slots, parts)


def spread_seq(wire, place, part_of, slots):
    parts = [
        (part_of(seq), slots.at[index], place.at_seq(seq))
        for index, seq in enumerate(place.seq_peers)
    ]
    return wire.send_all(slots, parts)


def collect(batch):
    arrive([batch])
    batch.wire.drain(batch.copies)


def total_of(own, slots, count):
    total = own
    for index in range(count):
        total = total + slots[index].astype(F32)
    return total


def row_of(lines, first):
    return jnp.concatenate([lines[first + line : first + line + 1, :] for line in range(8)], axis=1)


def lines_of(row):
    return jnp.concatenate([row[:, 128 * line : 128 * (line + 1)] for line in range(8)], axis=0)


def whole_piece(piece):
    value = piece[...]
    return value.reshape(-1, value.shape[-1])


def norm_parts(values):
    centred = values - jnp.mean(values, axis=1, keepdims=True)
    inverse = lax.rsqrt(jnp.mean(centred * centred, axis=1, keepdims=True) + norm_eps)
    return centred * inverse, inverse


def half_turn(values):
    lane = lax.broadcasted_iota(jnp.int32, values.shape, 1) % 64
    in_time = lane < 16
    first = (lane < 8) | ((lane >= 16) & (lane < 28)) | ((lane >= 40) & (lane < 52))
    up = jnp.where(in_time, pltpu.roll(values, 120, 1), pltpu.roll(values, 116, 1))
    down = jnp.where(in_time, pltpu.roll(values, 8, 1), pltpu.roll(values, 12, 1))
    return jnp.where(first, up, down)


def split_heads(values):
    lane = lax.broadcasted_iota(jnp.int32, values.shape, 1)
    empty = jnp.zeros_like(values)
    return jnp.concatenate(
        [jnp.where(lane < 64, values, empty), jnp.where(lane < 64, empty, values)], axis=0
    )


def join_heads(turned):
    return jnp.concatenate([turned[:64, :256], turned[64:, 256:]], axis=0).T


def attend_frame(frame, query, keys, values, attended, log_total, scores):
    pair = split_heads(query[frame])
    row_max = None
    for block in range(frame + 1):
        block_scores = contract(keys[block], pair, 1, 1)
        scores[block] = block_scores
        block_max = jnp.max(block_scores, axis=0, keepdims=True)
        row_max = block_max if row_max is None else jnp.maximum(row_max, block_max)
    row_total = None
    weighted = None
    for block in range(frame + 1):
        exponent = jnp.exp(scores[block] - row_max)
        block_total = jnp.sum(exponent, axis=0, keepdims=True)
        block_sum = contract(values[block], exponent.astype(BF16), 0, 0)
        row_total = block_total if row_total is None else row_total + block_total
        weighted = block_sum if weighted is None else weighted + block_sum
    attended[frame] = join_heads(weighted / row_total).astype(BF16)
    log_total[frame] = row_max + jnp.log(row_total)


SQRT_TWO_OVER_PI = math.sqrt(2.0 / math.pi)


def gelu_parts(values):
    square = values * values
    bent = jnp.tanh(SQRT_TWO_OVER_PI * values * (1.0 + 0.044715 * square))
    half = 0.5 * (1.0 + bent)
    slope = half + 0.5 * values * (1.0 - bent * bent) * (
        SQRT_TWO_OVER_PI * (1.0 + 3.0 * 0.044715 * square)
    )
    return values * half, slope


def rope_in_kernel(frame):
    lane = lax.broadcasted_iota(jnp.int32, (256, 128), 1) % 64
    patch = lax.broadcasted_iota(jnp.int32, (256, 128), 0)
    in_time, in_rows = lane < 16, lane < 40
    half = jnp.where(in_time, 8, 12)
    step = jnp.where(in_time, lane, jnp.where(in_rows, lane - 16, lane - 40))
    second = step >= half
    step = jnp.where(second, step - half, step).astype(F32)
    position = jnp.where(in_time, frame, jnp.where(in_rows, patch // GRID_W, patch % GRID_W))
    rate = jnp.exp(-math.log(10000.0) * step / half.astype(F32))
    angle = position.astype(F32) * rate
    sine = jnp.sin(angle)
    return jnp.cos(angle), jnp.where(second, sine, -sine)


BIAS_FIRST = (0, 24, 32, 64, 72)
BIAS_SHARE = (96, 32, 128, 32, 192)


def every_bias(blocks, lines):
    lane = lax.broadcasted_iota(jnp.int32, (8, 128), 1)

    def take(line, first, every):
        return blocks[pl.ds(8 * first + line, 32 // every, stride=8 * every), :]

    def moved(values, lanes):
        return pltpu.roll(values, lanes % 128, 1)

    mixed = [take(2, first, 4) for first in range(4)]
    lines[pl.ds(0, 8, stride=3), :] = jnp.where(lane < 96, mixed[0], moved(mixed[1], 96))
    lines[pl.ds(1, 8, stride=3), :] = jnp.where(lane < 64, moved(mixed[1], 96), moved(mixed[2], 64))
    lines[pl.ds(2, 8, stride=3), :] = jnp.where(lane < 32, moved(mixed[2], 64), moved(mixed[3], 32))

    def quarters(parts, first_lane):
        total = jnp.zeros((8, 128), F32)
        for index, part in enumerate(parts):
            here = (lane >= 32 * index) & (lane < 32 * (index + 1))
            total = jnp.where(here, moved(part, 32 * index - first_lane), total)
        return total

    lines[24:32, :] = quarters(mixed, 96)
    lines[32:64, :] = take(1, 0, 1)
    lines[64:72, :] = quarters([take(4, first, 4) for first in range(4)], 64)
    left = lax.broadcasted_iota(jnp.int32, (16, 128), 1) < 64
    even, odd = take(3, 0, 2), take(3, 1, 2)
    even_rest, odd_rest = take(4, 0, 2), take(4, 1, 2)
    lines[pl.ds(72, 16, stride=3), :] = even
    lines[pl.ds(73, 16, stride=3), :] = jnp.where(left, even_rest, moved(odd, 64))
    lines[pl.ds(74, 16, stride=3), :] = jnp.where(left, moved(odd, 64), moved(odd_rest, 64))


def pack_lanes(rows):
    packed = rows[:, 0]
    for part in range(1, 4):
        packed = packed + pltpu.roll(rows[:, part], 32 * part, 2)
    return packed


def unpack_lanes(packed):
    lane = lax.broadcasted_iota(jnp.int32, packed.shape, packed.ndim - 1)
    parts = [packed] + [pltpu.roll(packed, 128 - 32 * part, 1) for part in range(1, 4)]
    return jnp.concatenate([jnp.where(lane < 32, part, 0.0) for part in parts], axis=0)


def forward_kernel(
    x_ref,
    level_ref,
    table_ref,
    b_qkv_ref,
    b_out_ref,
    b_up_ref,
    b_down_ref,
    b_ada_ref,
    w_qkv_ref,
    w_out_in,
    w_up_in,
    w_down_in,
    w_ada_in,
    cotangent_in,
    layer_out_ref,
    log_total_ref,
    modulation_ref,
    embedded_ref,
    one_hot_ref,
    gate_two_grad_ref,
    wide_out,
    down_out,
    query_out,
    keys_out,
    values_out,
    attended_out,
    tokens_out,
    normed_one_out,
    normed_two_out,
    middle_out,
    branch_one_out,
    act_out,
    slope_out,
    cosine_out,
    sine_out,
    query_ref,
    keys_ref,
    values_ref,
    attended_ref,
    attended_tokens,
    normed_one_ref,
    normed_two_ref,
    middle_ref,
    branch_one_ref,
    act_ref,
    slope_ref,
    cosine_ref,
    sine_ref,
    w_out_ref,
    w_up_ref,
    w_down_ref,
    w_ada_ref,
    cotangent_ref,
    wide,
    down,
    levels,
    found,
    found_dp,
    found_sum,
    found_seq,
    partial_mod,
    mod_dp,
    mod_sum,
    mod_blocks,
    mod_seq,
    bias_lines,
    blocks,
    own_block,
    flat,
    scores,
    send_sems,
    recv_sems,
    back_send,
    back_recv,
    local_sems,
):
    place = Place()
    wire = Wire(place, send_sems, recv_sems)
    dp, seq, z, core = place.dp, place.seq, place.z, place.core
    device = dp * 8 + seq
    local = Local(local_sems)
    loads = [
        local.start(source, target)
        for source, target in (
            (w_ada_in, w_ada_ref),
            (w_out_in, w_out_ref),
            (w_up_in, w_up_ref),
            (w_down_in, w_down_ref),
            (cotangent_in, cotangent_ref),
        )
    ]
    own_block[...] = jnp.full((8, 128), level_ref[0, 0].astype(F32), F32)

    def place_bias(line, lane, ref, first, share):
        values = low(ref[first : first + share]).astype(F32)
        own_block[line : line + 1, lane : lane + share] = values.reshape(1, share)

    place_bias(1, 0, b_up_ref, 0, 128)
    place_bias(2, 0, b_qkv_ref, 0, 96)
    place_bias(2, 96, b_out_ref, 0, 32)
    place_bias(3, 0, b_ada_ref, 0, 128)
    place_bias(4, 0, b_ada_ref, 128, 64)
    place_bias(4, 64, b_down_ref, 0, 32)
    levels[dp, seq] = own_block[...]
    wide[0, dp, z, core] = low(w_qkv_ref[:, :1024])
    place.greet()
    level_gather = SmallGather(wire, place, levels)
    level_gather.along_seq()
    pieces = [Gather(wire, place, wide.at[index]) for index in range(8)]
    pieces += [Gather(wire, place, down.at[index]) for index in range(4)]
    pieces[0].along_z()
    pieces[0].own_xy()
    for block in (1, 2):
        wide[block, dp, z, core] = low(w_qkv_ref[:, 1024 * block : 1024 * (block + 1)])
        pieces[block].own_xy()
    saved = []

    def save(index):
        pieces[index].finish()
        source, target = (
            (wide.at[index], wide_out.at[index])
            if index < 8
            else (down.at[index - 8], down_out.at[index - 8])
        )
        saved.append(local.start(source, target))

    def keep(source, target):
        saved.append(local.start(source, target))

    started = [2]
    passed = [4]

    def start_z(last):
        while started[0] <= min(last, 11):
            pieces[started[0]].along_z()
            started[0] += 1

    def pass_z(last):
        while passed[0] <= min(last, 11):
            pieces[passed[0]].pass_z()
            passed[0] += 1

    def links(step):
        pass_z((0, 0, 0, 5, 7, 8, 9, 9)[step] if step < 8 else step)
        start_z((0, 0, 0, 9, 9, 9, 9, 9, 10, 11)[min(step, 9)])
        if step < 12:
            pieces[step].along_xy()
        if step - 1 < 12:
            pieces[step - 1].across()
        if step > 8:
            pass_z(step + 1)

    def tick(step):
        links(step)
        pieces[step - 2].to_sibling()
        save(step - 3)

    x = x_ref[...].astype(F32)
    normed, unused = norm_parts(x)
    flat[0] = normed
    level_gather.along_dp()
    pieces[1].along_z()
    start_z(2)
    level_gather.finish()
    level_rows = jnp.concatenate(
        [levels[group, frame, 0:1, :] for group in range(4) for frame in range(8)]
        + [jnp.full((96, 128), -1.0, F32)],
        axis=0,
    )
    lane = lax.broadcasted_iota(jnp.int32, (128, 128), 1)
    own_level = (lane + device * 32).astype(F32)
    one_hot = jnp.where((level_rows == own_level) & (lane < 32), 1.0, 0.0)
    one_hot_ref[...] = one_hot
    one_hot_turned = low(one_hot.T)[:32, :]
    rows = contract(low(table_ref[...]), one_hot_turned, 0, 0).reshape(32, 4, 8, 128)
    found[...] = pack_lanes(rows).reshape(found.shape)
    found_copies = spread_dp(wire, place, lambda dp: found.at[dp], found_dp)
    for copy in loads:
        copy.wait()
    wide[3, dp, z, core] = low(w_out_ref[...])
    for block in range(4):
        wide[4 + block, dp, z, core] = low(w_up_ref[:, 1024 * block : 1024 * (block + 1)])
    for block in range(4):
        down[block, dp, z, core] = low(w_down_ref[:, 256 * block : 256 * (block + 1)])
    start_z(3)
    for block in (3, 4):
        pieces[block].own_xy()
    pieces[0].pass_z()
    pieces[0].along_xy()
    collect(found_copies)
    found_sum[...] = total_of(found[dp], found_dp, 3)
    found_copies = spread_seq(wire, place, lambda seq: found_sum.at[seq], found_seq)
    pieces[1].pass_z()
    start_z(5)
    pieces[1].along_xy()
    cosine, sine = rope_in_kernel(seq)
    cosine_ref[...] = cosine
    sine_ref[...] = sine
    keep(cosine_ref, cosine_out)
    keep(sine_ref, sine_out)
    pieces[0].across()
    collect(found_copies)
    embedded = unpack_lanes(total_of(found_sum[seq], found_seq, 7))
    embedded_ref[...] = embedded
    silu_in = low(embedded / (1.0 + jnp.exp(-embedded)))
    for block in range(6):
        part = contract(silu_in, low(w_ada_ref[:, 1024 * block : 1024 * (block + 1)]), 0, 0)
        lines = [part[:32, 128 * line : 128 * (line + 1)].reshape(4, 8, 128) for line in range(8)]
        for pair in range(4):
            both = jnp.concatenate(lines[2 * pair : 2 * pair + 2], axis=1)
            partial_mod[4 * block + pair] = low(both)
    mod_copies = spread_dp(wire, place, lambda dp: partial_mod.at[:, dp], mod_dp)
    blocks[...] = levels[...].reshape(256, 128)
    every_bias(blocks, bias_lines)
    pieces[2].pass_z()
    pieces[3].pass_z()
    start_z(7)
    pieces[2].along_xy()
    pieces[1].across()
    pieces[0].to_sibling()
    collect(mod_copies)
    mod_sum[...] = total_of(partial_mod[:, dp].astype(F32), mod_dp, 3).reshape(384, 128)
    for frame in range(8):
        mod_blocks[frame] = mod_sum[pl.ds(frame, 48, stride=8), :]
    mod_copies = spread_seq(wire, place, lambda seq: mod_blocks.at[seq], mod_seq)
    tick(3)
    biases = bias_lines[...]
    collect(mod_copies)
    modulation = total_of(mod_blocks[seq], mod_seq, 7) + biases[72:120]
    for block in range(6):
        modulation_ref[block : block + 1, :] = row_of(modulation, 8 * block)
    shift_one = modulation_ref[0:1, :]
    scale_one = modulation_ref[1:2, :]
    gate_one = modulation_ref[2:3, :]
    shift_two = modulation_ref[3:4, :]
    scale_two = modulation_ref[4:5, :]
    gate_two = modulation_ref[5:6, :]
    normed_one_ref[...] = low(flat[0] * (1.0 + scale_one) + shift_one)
    keep(normed_one_ref, normed_one_out)
    cosine = cosine_ref[...]
    sine = sine_ref[...]
    head_copies = []

    def project(block, target):
        r = contract(normed_one_ref[...], whole_piece(wide.at[block]), 1, 0)
        r = r + row_of(biases, 8 * block)
        for group in range(8):
            part = r[:, 128 * group : 128 * (group + 1)]
            if block < 2:
                part = part * cosine + half_turn(part) * sine
            if block == 0:
                part = part * 0.125
            act_ref[:, 1024 * block + 128 * group : 1024 * block + 128 * (group + 1)] = low(part)
        parts = []
        for other in place.seq_peers:
            columns = pl.ds(pl.multiple_of(1024 * block + other * 128, 128), 128)
            parts.append((act_ref.at[:, columns], target.at[seq], place.at_seq(other)))
        head_copies.append(wire.send_all(target.at[pl.ds(0, 7)], parts))
        columns = pl.ds(pl.multiple_of(1024 * block + seq * 128, 128), 128)
        target[seq] = act_ref[:, columns]

    project(0, query_ref)
    tick(4)
    project(1, keys_ref)
    tick(5)
    project(2, values_ref)
    tick(6)
    tick(7)
    tick(8)
    arrive(head_copies)
    keep(query_ref, query_out)
    keep(keys_ref, keys_out)
    keep(values_ref, values_out)

    def back_copy(frame, source):
        columns = pl.ds(pl.multiple_of(source * 128, 128), 128)
        return pltpu.make_async_remote_copy(
            src_ref=attended_ref.at[frame],
            dst_ref=attended_tokens.at[:, columns],
            send_sem=back_send.at[frame],
            recv_sem=back_recv.at[source],
            device_id=place.at_seq(frame),
            device_id_type=MESH_ID,
        )

    def send_back(frame):
        @pl.when(seq != frame)
        def _():
            back_copy(frame, seq).start()

        @pl.when(seq == frame)
        def _():
            columns = pl.ds(pl.multiple_of(seq * 128, 128), 128)
            attended_tokens[:, columns] = attended_ref[frame]

    for frame in (7, 0, 6, 1, 5, 2, 4, 3):
        attend_frame(
            frame, query_ref, keys_ref, values_ref, attended_ref, log_total_ref, scores
        )
        send_back(frame)
        if frame == 1:
            links(9)
    keep(attended_ref, attended_out)
    links(10)
    pieces[7].to_sibling()
    save(6)
    for other in place.seq_peers:
        back_copy(other, other).wait_recv()
    for other in place.seq_peers:
        back_copy(other, other).wait_send()
    keep(attended_tokens, tokens_out)
    for batch in head_copies:
        wire.drain(batch.copies)
    branch_one = contract(attended_tokens[...], whole_piece(wide.at[3]), 1, 0)
    branch_one = branch_one + row_of(biases, 24)
    branch_one_ref[...] = branch_one
    keep(branch_one_ref, branch_one_out)
    middle = x_ref[...].astype(F32) + gate_one * branch_one
    middle_ref[...] = middle
    keep(middle_ref, middle_out)
    normed, unused = norm_parts(middle)
    normed_two_ref[...] = low(normed * (1.0 + scale_two) + shift_two)
    keep(normed_two_ref, normed_two_out)
    links(11)
    pieces[8].to_sibling()
    save(7)
    for block in range(4):
        if block == 3:
            links(12)
            pieces[9].to_sibling()
            save(8)
        pre = contract(normed_two_ref[...], whole_piece(wide.at[4 + block]), 1, 0)
        act, slope = gelu_parts(pre + row_of(biases, 32 + 8 * block))
        act_ref[:, 1024 * block : 1024 * (block + 1)] = low(act)
        slope_ref[:, 1024 * block : 1024 * (block + 1)] = low(slope)
    keep(act_ref, act_out)
    keep(slope_ref, slope_out)
    for block in range(4):
        if block == 0:
            pieces[10].to_sibling()
        elif block == 1:
            pieces[11].to_sibling()
            save(9)
        else:
            save(8 + block)
        flat[0, :, 256 * block : 256 * (block + 1)] = contract(
            act_ref[...], whole_piece(down.at[block]), 1, 0
        )
    branch_two = flat[0] + row_of(biases, 64)
    layer_out_ref[...] = low(middle_ref[...] + gate_two * branch_two)
    gate_two_grad_ref[...] = jnp.sum(
        cotangent_ref[...].astype(F32) * branch_two, axis=0, keepdims=True
    )
    wire.drain()
    for copy in saved:
        copy.wait()


def vmem(shape, dtype=F32):
    return pltpu.VMEM(shape, dtype)


def run_forward(x, level, table, biases, w_qkv, w_out, w_up, w_down, w_ada, cotangent):
    shape = jax.ShapeDtypeStruct
    small = [
        ((256, 1024), BF16),
        ((8, 1, 512), F32),
        ((8, 1024), F32),
        ((32, 128), F32),
        ((128, 128), F32),
        ((1, 1024), F32),
    ]
    gathered = [((8, 4, 4, 2, 32, 1024), BF16), ((4, 4, 4, 2, 128, 256), BF16)]
    kept = (
        [((8, 256, 128), BF16)] * 4
        + [((256, 1024), BF16)] * 3
        + [((256, 1024), F32)] * 2
        + [((256, 4096), BF16)] * 2
        + [((256, 128), F32)] * 2
    )
    fetched = [
        ((32, 1024), F32),
        ((32, 4096), F32),
        ((128, 1024), F32),
        ((32, 6144), F32),
        ((256, 1024), BF16),
    ]
    in_vmem = pl.BlockSpec(memory_space=pltpu.VMEM)
    anywhere = pl.BlockSpec(memory_space=pl.ANY)
    scratch = [vmem(*array) for array in kept + fetched + gathered]
    scratch += [
        vmem((4, 8, 8, 128)),
        vmem((4, 8, 8, 128)),
        vmem((3, 8, 8, 128)),
        vmem((8, 8, 128)),
        vmem((7, 8, 128)),
        vmem((24, 4, 16, 128), BF16),
        vmem((3, 24, 16, 128), BF16),
        vmem((384, 128)),
        vmem((8, 48, 128)),
        vmem((7, 48, 128)),
        vmem((120, 128)),
        vmem((256, 128)),
        vmem((8, 128)),
        vmem((1, 256, 1024)),
        vmem((8, 256, 512)),
        pltpu.SemaphoreType.DMA((78,)),
        pltpu.SemaphoreType.DMA((82,)),
        pltpu.SemaphoreType.DMA((8,)),
        pltpu.SemaphoreType.DMA((8,)),
        pltpu.SemaphoreType.DMA((32,)),
    ]
    return pl.pallas_call(
        forward_kernel,
        out_shape=[shape(*out) for out in small + gathered + kept],
        in_specs=[in_vmem, pl.BlockSpec(memory_space=pltpu.SMEM)] + [in_vmem] * 7 + [anywhere] * 5,
        out_specs=[in_vmem] * len(small) + [anywhere] * len(gathered + kept),
        scratch_shapes=scratch,
        compiler_params=pltpu.CompilerParams(
            collective_id=0, has_side_effects=True, vmem_limit_bytes=VMEM_LIMIT
        ),
        name="block_forward",
    )(x, level, table, *biases, w_qkv, w_out, w_up, w_down, w_ada, cotangent)


SLOTS = 5


class Scatter:
    def __init__(self, wire, place, index, terms, buffers, credit, finish):
        self.wire, self.place, self.index, self.terms = wire, place, index, terms
        from_core, from_far, from_xy, from_z = buffers
        self.from_core = from_core.at[index % SLOTS]
        self.from_far = from_far.at[index]
        self.from_xy = from_xy.at[index]
        self.from_z = from_z.at[index]
        self.credit, self.finish = credit, finish
        self.mine = []
        self.rest = []

    def send(self, source, target, device, only=None, landing=None):
        copy = self.wire.send(source, target, device, only, landing)
        self.mine.append(copy)
        return copy

    def batch(self, whole, parts, landing=None):
        batch = self.wire.send_all(whole, parts, landing)
        self.mine += batch.copies
        return batch

    def to_sibling(self):
        place = self.place
        if self.index >= SLOTS:
            pl.semaphore_wait(self.credit, 1)
        self.coming = [
            self.send(self.terms.at[:, :, place.other], self.from_core, place.sibling)
        ]

    def far_to_sibling(self):
        place = self.place
        far = self.terms.at[place.far_dp, :, place.other]
        self.coming = [self.send(far, self.from_core.at[place.far_dp], place.sibling)]

    def rest_to_sibling(self):
        place = self.place
        parts = [
            (self.terms.at[dp, :, place.other], self.from_core.at[dp], place.sibling)
            for dp in (place.x_dp, place.y_dp, place.dp)
        ]
        self.rest = [self.batch(self.from_core.at[pl.ds(0, 3)], parts)]

    def across(self, last):
        place, terms, core = self.place, self.terms, self.place.core
        arrive(self.coming)
        far = place.far_dp
        terms[far, :, core] = terms[far, :, core] + self.from_core[far]
        to_x, to_y = place.at_dp(place.x_dp), place.at_dp(place.y_dp)
        parts = [
            (terms.at[far, pl.ds(0, 2), core], self.from_far.at[0], to_x),
            (terms.at[far, pl.ds(2, 2), core], self.from_far.at[1], to_y),
        ]
        self.coming = [self.batch(self.from_far, parts)]
        arrive(self.rest)
        for group in (place.x_dp, place.y_dp, place.dp):
            terms[group, :, core] = terms[group, :, core] + self.from_core[group]
        if not last:
            pl.semaphore_signal(
                self.credit, inc=1, device_id=place.sibling, device_id_type=MESH_ID
            )

    def along_xy(self):
        place, terms, core = self.place, self.terms, self.place.core
        arrive(self.coming)
        first, second = pl.ds(0, 2), pl.ds(2, 2)
        terms[place.y_dp, first, core] = terms[place.y_dp, first, core] + self.from_far[0]
        terms[place.x_dp, second, core] = terms[place.x_dp, second, core] + self.from_far[1]
        parts = [
            (terms.at[dp, :, core], self.from_xy.at[slot], place.at_dp(dp))
            for slot, dp in enumerate((place.x_dp, place.y_dp))
        ]
        self.coming = [self.batch(self.from_xy, parts)]

    def gather_shares(self):
        place, terms, core = self.place, self.terms, self.place.core
        arrive(self.coming)
        own = terms[place.dp, :, core].astype(F32)
        self.shares = self.from_xy.at[0]
        self.shares[...] = low(total_of(own, self.from_xy, 2))
        self.wire.drain(self.mine)
        self.mine = []

    def along_z(self):
        place, shares = self.place, self.shares
        pair = place.at_z_chip(place.z_pair)
        beyond = shares.at[pl.ds(place.z_beyond, 2)]
        self.first = self.send(shares.at[place.z_pair], self.from_z.at[0], pair)
        self.carried = self.send(beyond, self.from_z.at[pl.ds(2, 2)], pair, place.z_end)

    def pass_z(self):
        place, shares = self.place, self.shares

        @pl.when(place.z_middle)
        def _():
            self.carried.wait_recv()
            beyond = shares.at[pl.ds(place.z_beyond, 2)]
            beyond[...] = beyond[...] + self.from_z[2:4]

        self.second = None
        for z in ((place.z + 2) % 4, 3 - place.z):
            self.second = self.send(
                shares.at[z],
                self.from_z.at[1],
                place.at_z_chip(z),
                place.z_middle,
                landing=self.second,
            )

    def end(self):
        arrive([self.first, self.second])
        own = self.shares[self.place.z].astype(F32)
        self.finish(total_of(own, self.from_z, 2))
        self.wire.drain(self.mine)


class CoreGather:
    def __init__(self, wire, place, ref):
        self.wire, self.place, self.ref = wire, place, ref

    def along_seq(self):
        place = self.place
        own = self.ref.at[place.dp, place.z, place.core]
        parts = [(own, own, place.at_z_chip((place.z + step) % 4)) for step in (1, 2, 3)]
        self.first = self.wire.send_all(self.ref.at[0, pl.ds(0, 3), 0], parts)

    def along_dp_by_core(self):
        place = self.place
        collect(self.first)
        own = self.ref.at[place.dp, :, place.core]
        parts = [(own, own, place.at_dp(dp)) for dp in place.dp_peers]
        self.first = self.wire.send_all(self.ref.at[pl.ds(0, 3), :, 0], parts)

    def to_sibling(self):
        place = self.place
        collect(self.first)
        mine = self.ref.at[:, :, place.core]
        self.last = self.wire.send(mine, mine, place.sibling)

    def finish_by_core(self):
        arrive([self.last])
        self.wire.drain([self.last])


def norm_back(normed, inverse, grad):
    mean = jnp.mean(grad, axis=1, keepdims=True)
    along = jnp.mean(grad * normed, axis=1, keepdims=True)
    return (grad - mean - normed * along) * inverse


def column_sum(values):
    return jnp.sum(values, axis=0, keepdims=True)


def pair_deltas(attended, grad_heads, deltas):
    lane = lax.broadcasted_iota(jnp.int32, (8, 128), 1)
    line = lax.broadcasted_iota(jnp.int32, (8, 128), 0)
    picked = jnp.where(lane // 64 == line, 1.0, 0.0).astype(F32)
    for frame in range(8):
        product = attended[frame].astype(F32) * grad_heads[frame].astype(F32)
        sums = contract(picked, product, 1, 1, precision=lax.Precision.HIGHEST)
        deltas[frame] = jnp.concatenate([sums[0:1], sums[1:2]], axis=1)


def frame_pairs():
    for first in range(4):
        last = 7 - first
        yield [(query, first) for query in range(first, last + 1)], first
        yield [(last, key) for key in range(first + 1, last + 1)], last


def attend_pair_back(query_frame, key_frame, heads, log_total, grad_heads, deltas, sums, fresh):
    query, keys, values = heads
    pair = split_heads(query[query_frame])
    grad_pair = split_heads(grad_heads[query_frame])
    weights = jnp.exp(contract(keys[key_frame], pair, 1, 1) - log_total[query_frame])
    grad_weights = contract(values[key_frame], grad_pair, 1, 1)
    grad_scores = low(weights * (grad_weights - deltas[query_frame]))
    turned = contract(keys[key_frame], grad_scores, 0, 0)
    parts = (
        (query_frame, jnp.concatenate([turned[:64, :256], turned[64:, 256:]], axis=0)),
        (key_frame, contract(grad_scores, pair, 1, 0)),
        (key_frame, contract(low(weights), grad_pair, 1, 0)),
    )
    for total, (frame, part), started in zip(sums, parts, fresh):
        if frame in started:
            total[frame] += part
        else:
            started.add(frame)
            total[frame] = part


def backward_kernel(
    cotangent_ref,
    log_total_ref,
    modulation_ref,
    embedded_ref,
    one_hot_ref,
    gate_two_grad_ref,
    wide,
    down,
    act_in,
    slope_in,
    normed_two_in,
    middle_in,
    branch_one_in,
    query_in,
    keys_in,
    values_in,
    attended_in,
    tokens_in,
    x_in,
    normed_one_in,
    cosine_in,
    sine_in,
    w_ada_in,
    grad_hidden_ref,
    grad_table_ref,
    grad_ada_ref,
    grad_ada_bias_ref,
    grad_qkv_ref,
    grad_out_ref,
    grad_up_ref,
    grad_down_ref,
    grad_bias_ref,
    hidden,
    slope_ref,
    normed_two_ref,
    middle_ref,
    branch_one_ref,
    query_ref,
    keys_ref,
    values_ref,
    attended_ref,
    attended_tokens,
    x_ref,
    normed_one_ref,
    cosine_ref,
    sine_ref,
    w_ada_ref,
    terms,
    from_core,
    from_far,
    from_xy,
    from_z,
    down_block,
    wide_block,
    grad_two,
    grad_one,
    grad_tokens,
    grad_heads,
    deltas,
    query_sum,
    keys_sum,
    values_sum,
    query_back,
    keys_back,
    values_back,
    qkv_back,
    running,
    bias_lines,
    bias_dp,
    bias_sum,
    bias_seq,
    mod_grads,
    mod_lines,
    embedded_grads,
    send_sems,
    recv_sems,
    back_send,
    back_recv,
    local_sems,
    credit,
):
    place = Place()
    wire = Wire(place, send_sems, recv_sems)
    dp, seq, core = place.dp, place.seq, place.core
    loads = {}
    local = Local(local_sems)

    def load(name, source, target):
        loads[name] = local.start(source, target)

    def load_down(block):
        load(("down", block), down.at[:, block], down_block)

    def load_wide(block):
        load(("wide", block), wide.at[block], wide_block.at[block % 2])

    load("act", act_in, hidden)
    load_down(0)
    load("slope", slope_in, slope_ref)
    load_wide(4)
    load_wide(5)
    later = (
        (normed_two_in, normed_two_ref),
        (middle_in, middle_ref),
        (branch_one_in, branch_one_ref),
        (query_in, query_ref),
        (keys_in, keys_ref),
        (values_in, values_ref),
        (attended_in, attended_ref),
        (tokens_in, attended_tokens),
        (x_in, x_ref),
        (normed_one_in, normed_one_ref),
        (cosine_in, cosine_ref),
        (sine_in, sine_ref),
        (w_ada_in, w_ada_ref),
    )
    for index, (source, target) in enumerate(later):
        load(index, source, target)
    place.greet()
    scale_one = modulation_ref[1:2, :]
    gate_one = modulation_ref[2:3, :]
    scale_two = modulation_ref[4:5, :]
    gate_two = modulation_ref[5:6, :]
    cotangent = cotangent_ref[...].astype(F32)
    grad_two[...] = low(cotangent * gate_two)

    def keep_bias(first, grad):
        bias_lines[first : first + 8, :] = lines_of(column_sum(grad.astype(F32)))

    bias_lines[72:80, :] = jnp.zeros((8, 128), F32)
    keep_bias(64, grad_two[...])

    def finish(index):
        def store(total):
            if index < 4:
                grad_down_ref[32 * index : 32 * (index + 1), :] = total
            elif index < 8:
                grad_up_ref[:, 1024 * (index - 4) : 1024 * (index - 3)] = total
            elif index == 8:
                grad_out_ref[...] = total
            else:
                grad_qkv_ref[:, 1024 * (index - 9) : 1024 * (index - 8)] = total

        return store

    buffers = (from_core, from_far, from_xy, from_z)
    pieces = [
        Scatter(
            wire, place, index, terms.at[index % SLOTS], buffers, credit, finish(index)
        )
        for index in range(12)
    ]
    loads["act"].wait()
    for group in (place.far_dp, place.x_dp, place.y_dp, place.dp):
        for z in range(4):
            columns = pl.ds(pl.multiple_of(group * 1024 + 256 * z, 256), 256)
            part = low(contract(hidden[:, columns], grad_two[...], 0, 0)).reshape(2, 4, 32, 1024)
            for index in range(4):
                terms[index, group, z] = part[:, index]
        if group is place.far_dp:
            for index in range(4):
                pieces[index].far_to_sibling()
    for index in range(4):
        pieces[index].rest_to_sibling()

    def make_terms(index):
        for group in range(4):
            rows = slice(256 * group, 256 * (group + 1))
            if index < 8:
                left = normed_two_ref[:, rows]
                right = hidden[:, 1024 * (index - 4) : 1024 * (index - 3)]
            elif index == 8:
                left, right = attended_tokens[:, rows], grad_one[...]
            else:
                left, right = normed_one_ref[:, rows], qkv_back[index - 9]
            part = low(contract(left, right, 0, 0))
            terms[index % SLOTS, group] = part.reshape(4, 2, 32, 1024)

    done = [0, 0, 0]

    reached = [0, 0, 0]

    def advance(across, along, gathered):
        for stage, last in enumerate((across, along, gathered)):
            while reached[stage] <= min(last, 11):
                index = reached[stage]
                if stage == 0:
                    pieces[index].across(index + SLOTS >= 12)
                elif stage == 1:
                    pieces[index].along_xy()
                else:
                    pieces[index].gather_shares()
                reached[stage] += 1

    def begin(index):
        make_terms(index)
        pieces[index].to_sibling()

    def tick(step):
        advance(step - 1, step - 3, step - 5)
        if step >= 4:
            begin(step)

    def settle(sent, passed, ended):
        for stage, last in enumerate((sent, passed, ended)):
            while done[stage] <= min(last, 11):
                piece = pieces[done[stage]]
                (piece.along_z, piece.pass_z, piece.end)[stage]()
                done[stage] += 1

    tick(1)
    tick(2)
    loads["slope"].wait()
    for block in range(4):
        loads[("down", block)].wait()
        grad_act = None
        for index in range(4):
            weight = down_block[index].reshape(1024, 256)
            part = contract(grad_two[:, 256 * index : 256 * (index + 1)], weight, 1, 1)
            grad_act = part if grad_act is None else grad_act + part
        if block < 3:
            load_down(block + 1)
        columns = slice(1024 * block, 1024 * (block + 1))
        grad_pre = low(grad_act * slope_ref[:, columns].astype(F32))
        hidden[:, columns] = grad_pre
        keep_bias(32 + 8 * block, grad_pre)
        loads[("wide", 4 + block)].wait()
        part = contract(grad_pre, whole_piece(wide_block.at[block % 2]), 1, 1)
        running[...] = part if block == 0 else running[...] + part
        load_wide((6, 7, 2, 3)[block])
        if block == 1:
            tick(3)
    for index in range(len(later)):
        loads[index].wait()
    normed, inverse = norm_parts(middle_ref[...])
    grad_normed = running[...]
    grad_shift_two = column_sum(grad_normed)
    grad_scale_two = column_sum(grad_normed * normed)
    grad_middle = cotangent_ref[...].astype(F32) + norm_back(
        normed, inverse, grad_normed * (1.0 + scale_two)
    )
    running[...] = grad_middle
    grad_gate_one = column_sum(grad_middle * branch_one_ref[...])
    grad_one[...] = low(grad_middle * gate_one)
    keep_bias(24, grad_one[...])
    loads[("wide", 3)].wait()
    grad_tokens[...] = low(contract(grad_one[...], whole_piece(wide_block.at[1]), 1, 1))
    load_wide(1)
    parts = []
    for other in place.seq_peers:
        columns = pl.ds(pl.multiple_of(other * 128, 128), 128)
        parts.append((grad_tokens.at[:, columns], grad_heads.at[seq], place.at_seq(other)))
    head_copies = wire.send_all(grad_heads.at[pl.ds(0, 7)], parts)
    own_columns = pl.ds(pl.multiple_of(seq * 128, 128), 128)
    grad_heads[seq] = grad_tokens[:, own_columns]
    tick(4)
    tick(5)
    collect(head_copies)
    backs = (query_back, keys_back, values_back)

    def back_copy(part, frame, source):
        columns = pl.ds(pl.multiple_of(source * 128, 128), 128)
        return pltpu.make_async_remote_copy(
            src_ref=backs[part].at[frame],
            dst_ref=qkv_back.at[part, :, columns],
            send_sem=back_send.at[part, frame],
            recv_sem=back_recv.at[part, source],
            device_id=place.at_seq(frame),
            device_id_type=MESH_ID,
        )

    def send_back(frame):
        @pl.when(seq != frame)
        def _():
            for part in range(3):
                back_copy(part, frame, seq).start()

        @pl.when(seq == frame)
        def _():
            for part in range(3):
                qkv_back[part, :, own_columns] = backs[part][frame]

    pair_deltas(attended_ref, grad_heads, deltas)
    heads = (query_ref, keys_ref, values_ref)
    fresh = (set(), set(), set())
    for pairs, frame in frame_pairs():
        for query_frame, key_frame in pairs:
            attend_pair_back(
                query_frame,
                key_frame,
                heads,
                log_total_ref,
                grad_heads,
                deltas,
                (query_sum, keys_sum, values_sum),
                fresh,
            )
        query_back[frame] = low(query_sum[frame].T * 0.125)
        keys_back[frame] = low(keys_sum[frame])
        values_back[frame] = low(values_sum[frame])
        send_back(frame)
        if frame in (7, 2):
            tick(6 if frame == 7 else 7)
    tick(8)
    advance(8, 7, 4)
    for part in range(3):
        for other in place.seq_peers:
            back_copy(part, other, other).wait_recv()
    cosine, sine = cosine_ref[...], sine_ref[...]
    grad_normed = None
    for part in range(3):
        if part < 2:
            for group in range(8):
                columns = slice(128 * group, 128 * (group + 1))
                grad = qkv_back[part, :, columns].astype(F32)
                qkv_back[part, :, columns] = low(grad * cosine - half_turn(grad) * sine)
        keep_bias(8 * part, qkv_back[part])
        index = (2, 1, 0)[part]
    for block, slot in ((2, 0), (1, 1), (0, 0)):
        loads[("wide", block)].wait()
        part = contract(qkv_back[block], whole_piece(wide_block.at[slot]), 1, 1)
        grad_normed = part if grad_normed is None else grad_normed + part
        if block == 2:
            load_wide(0)
    bias_copies = spread_dp(wire, place, lambda dp: bias_lines, bias_dp)
    normed, inverse = norm_parts(x_ref[...].astype(F32))
    grad_shift_one = column_sum(grad_normed)
    grad_scale_one = column_sum(grad_normed * normed)
    grad_hidden_ref[...] = low(
        running[...] + norm_back(normed, inverse, grad_normed * (1.0 + scale_one))
    )
    rows = (
        grad_shift_one,
        grad_scale_one,
        grad_gate_one,
        grad_shift_two,
        grad_scale_two,
        gate_two_grad_ref[...],
    )
    mod_grads[dp, place.z, core] = low(jnp.concatenate([lines_of(row) for row in rows], axis=0))
    mod_gather = CoreGather(wire, place, mod_grads)
    mod_gather.along_seq()
    begin(9)
    settle(3, -1, -1)
    advance(8, 8, 5)
    begin(10)
    advance(9, 8, 6)
    settle(4, -1, -1)
    begin(11)
    advance(10, 9, 6)
    settle(5, 2, -1)
    mod_gather.along_dp_by_core()
    collect(bias_copies)
    bias_sum[...] = total_of(bias_lines[...], bias_dp, 3)
    bias_copies = spread_seq(wire, place, lambda seq: bias_sum, bias_seq)
    advance(11, 10, 7)
    settle(7, 4, -1)
    advance(11, 11, 8)
    settle(8, 6, -1)
    advance(11, 11, 9)
    settle(9, 7, 2)
    mod_gather.to_sibling()
    mod_gather.finish_by_core()
    lines = mod_grads[...].astype(F32).reshape(1536, 128)
    mod_lines[...] = lines
    grad_ada_bias_ref[...] = jnp.sum(lines.reshape(32, 48, 128), axis=0)
    embedded = embedded_ref[...]
    share = 1.0 / (1.0 + jnp.exp(-embedded))
    silu_in = low(embedded * share)[:, :32]
    empty = jnp.zeros((96, 128), BF16)
    grad_silu = None
    for block in range(6):
        parts = []
        for line in range(8):
            part = mod_lines[pl.ds(8 * block + line, 32, stride=48), :]
            parts.append(jnp.concatenate([low(part), empty], axis=0))
        every = jnp.concatenate(parts, axis=1)
        columns = slice(1024 * block, 1024 * (block + 1))
        grad_ada_ref[:, columns] = contract(silu_in, every[:32], 1, 0)
        part = contract(low(w_ada_ref[:, columns]), every, 1, 1)
        grad_silu = part if grad_silu is None else grad_silu + part
    grad_embedded = grad_silu * share * (1.0 + embedded * (1.0 - share))
    embedded_grads[dp, seq] = pack_lanes(grad_embedded.reshape(1, 4, 8, 128))[0]
    embedded_gather = SmallGather(wire, place, embedded_grads)
    embedded_gather.along_seq()
    advance(11, 11, 10)
    settle(10, 8, 4)
    advance(11, 11, 11)
    settle(11, 10, 4)
    settle(11, 11, 4)
    embedded_gather.along_dp()
    collect(bias_copies)
    grad_bias_ref[...] = total_of(bias_sum[...], bias_seq, 7)
    settle(11, 11, 9)
    embedded_gather.finish()
    every_grad = jnp.concatenate(
        [unpack_lanes(embedded_grads[group, frame]) for group in range(4) for frame in range(8)],
        axis=0,
    )
    grad_table_ref[...] = contract(
        one_hot_ref[...],
        every_grad,
        0,
        1,
        precision=lax.Precision.HIGHEST,
    )[:32]
    settle(11, 11, 11)
    for part in range(3):
        for other in place.seq_peers:
            back_copy(part, other, other).wait_send()
    wire.drain()


def run_backward(cotangent, small, gathered, kept, x, w_ada):
    shape = jax.ShapeDtypeStruct
    outs = [
        ((256, 1024), BF16),
        ((32, 1024), F32),
        ((32, 6144), F32),
        ((48, 128), F32),
        ((32, 3072), F32),
        ((32, 1024), F32),
        ((32, 4096), F32),
        ((128, 1024), F32),
        ((80, 128), F32),
    ]
    query, keys, values, attended, tokens, normed_one, normed_two = kept[:7]
    middle, branch_one, act, slope, cosine, sine = kept[7:]
    fetched = (act, slope, normed_two, middle, branch_one, query, keys, values, attended)
    fetched += (tokens, x, normed_one, cosine, sine, w_ada)
    in_vmem = pl.BlockSpec(memory_space=pltpu.VMEM)
    anywhere = pl.BlockSpec(memory_space=pl.ANY)
    scratch = [vmem(array.shape, array.dtype) for array in fetched]
    scratch += [
        vmem((SLOTS, 4, 4, 2, 32, 1024), BF16),
        vmem((SLOTS, 4, 4, 32, 1024), BF16),
        vmem((12, 2, 2, 32, 1024), BF16),
        vmem((12, 2, 4, 32, 1024), BF16),
        vmem((12, 4, 32, 1024), BF16),
        vmem((4, 4, 2, 128, 256), BF16),
        vmem((2, 4, 4, 2, 32, 1024), BF16),
        vmem((256, 1024), BF16),
        vmem((256, 1024), BF16),
        vmem((256, 1024), BF16),
        vmem((8, 256, 128), BF16),
        vmem((8, 1, 512)),
        vmem((8, 128, 256)),
        vmem((8, 256, 128)),
        vmem((8, 256, 128)),
        vmem((8, 256, 128), BF16),
        vmem((8, 256, 128), BF16),
        vmem((8, 256, 128), BF16),
        vmem((3, 256, 1024), BF16),
        vmem((256, 1024)),
        vmem((80, 128)),
        vmem((3, 80, 128)),
        vmem((80, 128)),
        vmem((7, 80, 128)),
        vmem((4, 4, 2, 48, 128), BF16),
        vmem((1536, 128)),
        vmem((4, 8, 8, 128)),
        pltpu.SemaphoreType.DMA((58,)),
        pltpu.SemaphoreType.DMA((85,)),
        pltpu.SemaphoreType.DMA((3, 8)),
        pltpu.SemaphoreType.DMA((3, 8)),
        pltpu.SemaphoreType.DMA((32,)),
        pltpu.SemaphoreType.REGULAR,
    ]
    return pl.pallas_call(
        backward_kernel,
        out_shape=[shape(*out) for out in outs],
        in_specs=[in_vmem] * 6 + [anywhere] * 17,
        out_specs=[in_vmem] * 9,
        scratch_shapes=scratch,
        compiler_params=pltpu.CompilerParams(
            collective_id=1, has_side_effects=True, vmem_limit_bytes=VMEM_LIMIT
        ),
        name="block_backward",
    )(cotangent, *small, *gathered, *fetched)


def finish_kernel(lines_ref, ada_lines_ref, *refs):
    device = lax.axis_index("dp") * 8 + lax.axis_index("seq")
    for index in range(8):
        refs[8 + index][...] = refs[index][...]
    for index, share in enumerate(BIAS_SHARE):
        lines, first = (lines_ref, BIAS_FIRST[index]) if index < 4 else (ada_lines_ref, 0)
        offset = device * share
        line = first + offset // 128
        pair = jnp.concatenate([lines[pl.ds(line, 1), :], lines[pl.ds(line + 1, 1), :]], axis=1)
        part = pltpu.roll(pair, (256 - offset % 128) % 256, 1)
        refs[16 + index][...] = part[:, :share].reshape(share)


def run_finish(lines, ada_lines, arrays):
    shape = jax.ShapeDtypeStruct
    in_vmem = pl.BlockSpec(memory_space=pltpu.VMEM)
    return pl.pallas_call(
        finish_kernel,
        out_shape=[shape(array.shape, array.dtype) for array in arrays]
        + [shape((share,), F32) for share in BIAS_SHARE],
        in_specs=[in_vmem] * 10,
        out_specs=[in_vmem] * 13,
        name="block_outputs",
    )(lines, ada_lines, *arrays)


def fast_body(
    hidden_in,
    noise_level,
    noise_table,
    w_ada,
    b_ada,
    w_qkv,
    b_qkv,
    w_out,
    b_out,
    w_up,
    b_up,
    w_down,
    b_down,
    grad_out,
):
    biases = (b_qkv, b_out, b_up, b_down, b_ada)
    x, cotangent = hidden_in[0], grad_out[0]
    results = run_forward(
        x, noise_level, noise_table, biases, w_qkv, w_out, w_up, w_down, w_ada, cotangent
    )
    layer_out, small, gathered, kept = results[0], results[1:6], results[6:8], results[8:]
    grads = run_backward(cotangent, small, gathered, kept, x, w_ada)
    grad_hidden, grad_table, grad_ada_w, ada_lines, *weight_grads, lines = grads
    outs = run_finish(
        lines, ada_lines, (layer_out, grad_hidden, grad_table, grad_ada_w, *weight_grads)
    )
    layer_out, grad_hidden, grad_table, grad_ada_w, qkv_w, out_w, up_w, down_w = outs[:8]
    qkv_b, out_b, up_b, down_b, ada_b = outs[8:]
    return (
        layer_out[None],
        grad_hidden[None],
        grad_table,
        grad_ada_w,
        ada_b,
        qkv_w,
        qkv_b,
        out_w,
        out_b,
        up_w,
        up_b,
        down_w,
        down_b,
    )


def solution(mesh):
    tokens = P("dp", "seq", None)
    matrix = P(ALL, None)
    vector = P(ALL)
    parameters = (matrix,) + (matrix, vector) * 5
    chips = dict(mesh.shape) == {"dp": 4, "seq": 8}
    return jax.shard_map(
        fast_body if chips else general_body,
        mesh=mesh,
        in_specs=(tokens, P("dp", "seq")) + parameters + (tokens,),
        out_specs=(tokens, tokens) + parameters,
        check_vma=False,
    )
```
